512 devices in a mesh: ctx: 16 (over y, x_hi), exp: 32 (over z, x_lo, core).
Axes of the slice: x: 4 (x_hi: 2, x_lo: 2; x = x_hi * 2 + x_lo), y: 8, z: 8, core: 2. Of those that a mesh axis runs over, the one named last changes fastest.
Arguments:
- queries: bfloat16 [1920, 64, 576], P('ctx', 'exp'), may hold values from -40 to 40
- latents: bfloat16 [1920, 576], P('ctx'), may hold values from -6 to 6
- block_mask: int32 [16, 16], replicated, may hold values from 0 to 1, as said below
- value_up: bfloat16 [64, 512, 128], P('exp'), may hold values from -0.25 to 0.25
- out_proj: bfloat16 [8192, 2560], P('exp'), may hold values from -0.125 to 0.125
- residual: bfloat16 [1920, 2560], P('ctx', 'exp'), may hold values from -9 to 9
- norm_gain: bfloat16 [2560], P('exp'), may hold values from 0.099609375 to 1.8984375
- group_ids: int32 [1920, 3], P('ctx'), may hold values from 0 to 15, all different within a row; in each aligned block of 120 rows (0 to 119, 120 to 239, ...) at most 30 rows name the same one
- expert_ids: int32 [1920, 3, 2], P('ctx'), may hold values from 0 to 5, all different within a row
- route_weights: bfloat16 [1920, 3, 2], P('ctx'), may hold values from 0.049804688 to 0.59765625
- w_gate: bfloat16 [96, 2560, 768], P('ctx', 'exp'), may hold values from -0.125 to 0.125
- w_up: bfloat16 [96, 2560, 768], P('ctx', 'exp'), may hold values from -0.125 to 0.125
- w_down: bfloat16 [96, 768, 2560], P('ctx', None, 'exp'), may hold values from -0.21875 to 0.21875
Outputs:
- layer_out: bfloat16 [1920, 2560], P('ctx', 'exp')
The draws below stay inside these ranges and needn't reach their ends.
Inputs may be any that keep to these rules, and one draw needn't show every extreme that they name: block_mask[a, a] = 1, block_mask[a, b] = 0 for b > a, and block_mask[a, a - 8] = 1 for a >= 8. `group_ids`: the 3 groups of a token differ. Among the 120 tokens of one context block (aligned blocks of 120 rows) no group is named more than 30 times, a bound that some block reaches. `expert_ids`: the 2 experts of a token within one group differ.
All inputs are finite; a program needn't handle non-finite values.
Results may differ from the reference program's by a relative error of at most 0.024.
Values may be sent and summed in bfloat16 or wider, within the bound.
No kernel may reach another device: no remote copies, remote signals or barrier semaphores. Data moves between devices by JAX's collectives and lax.ppermute only.
A program may use at most 64 MiB of HBM per device.

```python
import math
import jax
import jax.numpy as jnp
import numpy as np
from jax import lax

KB = 120
LAT = 512
VH = 128
D = 2560
FF = 768
EXP_GRP = 6
TOPG = 3
TOPE = 2
QK = 576
HEADS = 64
EXPERTS = 96
SEQ = 1920
CAP = 30
N_CTX = 16
N_EXP = 32


def latent_base(key):
    return jax.random.normal(key, (SEQ, QK), jnp.float32)


def draw_latents(key, part):
    base = latent_base(key)
    return jnp.clip(base, -6.0, 6.0).astype(jnp.bfloat16)


def draw_queries(key, part):
    key = jax.random.fold_in(key, 11)
    noise = jax.random.normal(key, (SEQ, HEADS, QK), jnp.float32)
    return jnp.clip(noise, -6.0, 6.0).astype(jnp.bfloat16)


def draw_residual(key, part):
    key = jax.random.fold_in(key, 5)
    ramp = jnp.arange(D, dtype=jnp.float32) / D
    noise = jnp.clip(jax.random.normal(key, (SEQ, D), jnp.float32), -6.0, 6.0)
    return (0.7 * jnp.power(3.0, 0.5 * ramp)[None, :] * noise).astype(jnp.bfloat16)


def draw_block_mask(key, part):
    key = jax.random.fold_in(key, 3)
    coin = jax.random.randint(key, (N_CTX, N_CTX), 0, 8)
    rows = jnp.arange(N_CTX)[:, None]
    columns = jnp.arange(N_CTX)[None, :]
    below = jnp.where(coin == 0, 1, 0)
    opening = jnp.where(columns == rows - N_CTX // 2, 1, 0)
    earlier = jnp.maximum(below, opening)
    return jnp.where(columns == rows, 1, jnp.where(columns < rows, earlier, 0)).astype(jnp.int32)


def with_spikes(entries, key, source, target, shards_of, factor):
    owner, partner = [(jnp.arange(entries.shape[axis_at]) // (entries.shape[axis_at] // shards_of)).reshape([-1 if axis == axis_at else 1 for axis in range(entries.ndim)]) for axis_at in (source, target)]
    chosen = jax.random.permutation(key, shards_of)[partner]
    strong = (owner == chosen) | (owner == (partner + shards_of // 2) % shards_of)
    return jnp.where(strong, factor * entries, entries)


def shard_levels(own_key, shape, pieces, smallest, top_value):
    loudness = 1.0
    for axis_at, shards_of in pieces:
        draws = jax.random.uniform(jax.random.fold_in(jax.random.fold_in(own_key, 6), axis_at), (shards_of,), jnp.float32, smallest / len(pieces), top_value / len(pieces))
        loudness = loudness * jnp.repeat(jnp.exp(draws), shape[axis_at] // shards_of).reshape((-1,) + (1,) * (len(shape) - 1 - axis_at))
    return loudness


def picks_of(own_key, rows, count, top, lift):
    sequence = jax.random.permutation(jax.random.fold_in(own_key, 1), count)
    pull = sequence
    for power in range(3):
        pull = pull * pull // count
    pull = pull * lift // count
    lots = jax.random.randint(jax.random.fold_in(own_key, 2), (rows, count), 0, 4096) + pull
    holders = jax.random.permutation(jax.random.fold_in(own_key, 3), rows)[jnp.arange(count) % rows]
    lots = jnp.where(jnp.arange(rows)[:, None] == holders[None, :], 1 << 14, lots)
    score = lots * count + jnp.arange(count)
    return lax.top_k(score.astype(jnp.int32), top)[1].astype(jnp.int32)


def shared_out(stream_key, own, number, rows, count, top, reach, lean):
    order = jax.random.permutation(stream_key, count)
    heavy_load, ordinary = load_shares(count, rows * top, reach, lean, True), load_shares(count, rows * top, reach, lean, False)
    places = jnp.arange(count)

    def named(tallies, offset_by):
        used = int((tallies > 0).sum())
        fixed = max(1, used // 4)
        passed = fixed + (places - fixed + offset_by * (used - fixed)) % max(1, count - fixed)
        return jnp.zeros((count,), jnp.int32).at[order[jnp.where(places < fixed, places, passed)]].set(jnp.asarray(tallies, jnp.int32))

    tallies = jnp.where(number % 4 == 0, named(heavy_load, number // 4), named(ordinary, number - number // 4 - 1))
    mixed = jax.random.permutation(jax.random.fold_in(own, 3), count)
    donor, taker = mixed[0:count // 2 * 2:2], mixed[1:count // 2 * 2:2]
    margin = jnp.minimum(tallies[donor] - 1, reach - tallies[taker]) // 2
    margin = jnp.where((donor == order[0]) | (taker == order[0]) | (tallies[taker] == 0), 0, jnp.maximum(margin, 0))
    passed = jax.random.randint(jax.random.fold_in(own, 4), (count // 2,), 0, 1 << 20) % (margin + 1)
    tallies = tallies.at[donor].add(-passed).at[taker].add(passed)
    members = jnp.searchsorted(jnp.cumsum(tallies), jnp.arange(rows * top), side="right").astype(jnp.int32)
    listing = members.reshape(top, rows).T
    listing = listing[jax.random.permutation(jax.random.fold_in(own, 1), rows)]
    offset_by = jax.random.randint(jax.random.fold_in(own, 2), (rows, 1), 0, top)
    return jnp.take_along_axis(listing, (jnp.arange(top)[None, :] + offset_by) % top, axis=1)


def load_shares(number_of, total, reach, skew, full):
    portions = [(1 << 20) // math.isqrt(rank ** skew) + 1 for rank in range(1, number_of + 1)]
    largest = reach if full else min(reach, max(-(-total // number_of), total * portions[0] // sum(portions)))
    least = 1 if total - largest >= number_of - 1 else 0
    holding, surplus = [largest] + [least] * (number_of - 1), total - largest - least * (number_of - 1)
    while surplus > 0:
        candidates = [i for i in range(1, number_of) if holding[i] < largest] or [i for i in range(1, number_of) if holding[i] < reach]
        pool, remaining = sum([portions[i] for i in candidates]), surplus
        for i in candidates:
            extra = min(reach - holding[i], max(1, remaining * portions[i] // pool), surplus)
            holding[i] = holding[i] + extra
            surplus = surplus - extra
    return np.array(holding)


def normal_values(own_key, extent, scale, bound, split=(), kind=jnp.bfloat16):
    level = shard_levels(own_key, extent, split, -0.22, 0.18) if split else 1.0
    entries = jax.random.normal(own_key, extent, jnp.float32) * scale * level
    return jnp.minimum(jnp.maximum(entries, -bound), bound).astype(kind)


def heavy_noise(own_key, extent, scale, bound, split, heavy, held_as=jnp.bfloat16):
    entries = scale * jax.random.normal(own_key, extent, jnp.float32)
    if split:
        entries = entries * shard_levels(own_key, extent, split, -0.22, 0.18)
    return jnp.clip(with_spikes(entries, jax.random.fold_in(own_key, 3), *heavy), -bound, bound).astype(held_as)


def setup_inputs(seed: int = 0) -> dict:
    arg_keys = jax.random.split(jax.random.key(seed), 14)
    queries = draw_queries(jax.random.fold_in(arg_keys[13], 71), 0)
    latents = draw_latents(jax.random.fold_in(arg_keys[13], 71), 0)
    block_mask = draw_block_mask(jax.random.fold_in(arg_keys[13], 71), 0)
    value_up = normal_values(arg_keys[3], (HEADS, LAT, VH), LAT ** -0.5, 0.25, ((0, 32),))
    out_proj = heavy_noise(arg_keys[4], (HEADS * VH, D), (HEADS * VH) ** -0.5, 0.125, ((0, 32),), (0, 1, 32, 2.75))
    residual = draw_residual(jax.random.fold_in(arg_keys[13], 71), 0)
    norm_gain = jnp.clip(1.0 + 0.18 * jax.random.normal(arg_keys[6], (D,), jnp.float32), 0.099609375, 1.8984375).astype(jnp.bfloat16)
    group_ids_keys = jax.random.split(jax.random.fold_in(arg_keys[7], 1), SEQ // KB)
    group_ids_turns = jax.random.permutation(jax.random.fold_in(arg_keys[7], 3), SEQ // KB)
    group_ids = jax.vmap(lambda own, number: shared_out(jax.random.fold_in(arg_keys[7], 2), own, number, KB, N_CTX, TOPG, CAP, 1))(group_ids_keys, group_ids_turns).reshape((SEQ, TOPG))
    expert_ids = picks_of(arg_keys[8], SEQ * TOPG, EXP_GRP, TOPE, 2730).reshape((SEQ, TOPG, TOPE))
    route_weights = jnp.clip(jnp.exp(math.log(0.59765625) - 2.4849066 * jax.random.uniform(arg_keys[9], (SEQ, TOPG, TOPE), jnp.float32) ** shard_levels(arg_keys[9], (SEQ, TOPG, TOPE), ((0, 16),), -0.2, 0.2)), 0.049804688, 0.59765625).astype(jnp.bfloat16)
    w_gate = normal_values(arg_keys[10], (EXPERTS, D, FF), D ** -0.5, 0.125, ((0, 16), (1, 32)))
    w_up = normal_values(arg_keys[11], (EXPERTS, D, FF), D ** -0.5, 0.125, ((0, 16), (1, 32)))
    w_down = normal_values(arg_keys[12], (EXPERTS, FF, D), FF ** -0.5, 0.21875, ((0, 16), (2, 32)))
    return {"queries": queries, "latents": latents, "block_mask": block_mask, "value_up": value_up, "out_proj": out_proj, "residual": residual, "norm_gain": norm_gain, "group_ids": group_ids, "expert_ids": expert_ids, "route_weights": route_weights, "w_gate": w_gate, "w_up": w_up, "w_down": w_down}


MASKED_SCORE = -1e+30
EPSILON = 1e-06

def rounded(values):
    return lax.optimization_barrier(values.astype(jnp.bfloat16)).astype(jnp.float32)

def reference(queries, latents, block_mask, value_up, out_proj, residual, norm_gain, group_ids, expert_ids, route_weights, w_gate, w_up, w_down):
    positions = jnp.arange(SEQ, dtype=jnp.int32)
    blocks = positions // KB
    block_view = jnp.repeat(jnp.repeat(block_mask, KB, axis=0), KB, axis=1)
    allowed = (block_view == 1) & ((blocks[:, None] != blocks[None, :]) | (positions[None, :] <= positions[:, None]))
    values = latents[:, :LAT]

    def one_head(head_index):
        query_rows = lax.dynamic_index_in_dim(queries, head_index, 1, keepdims=False)
        scores = jnp.dot(query_rows, latents.T, preferred_element_type=jnp.float32) * QK ** (-0.5)
        masked = jnp.where(allowed, scores, MASKED_SCORE)
        row_top = lax.optimization_barrier(jnp.max(masked, axis=1, keepdims=True))
        exp_terms = jnp.where(allowed, jnp.exp(masked - row_top), 0.0)
        weighted = jnp.dot(exp_terms.astype(jnp.bfloat16), values, preferred_element_type=jnp.float32)
        return weighted / lax.optimization_barrier(jnp.sum(exp_terms, axis=1, keepdims=True))
    attn_latent = lax.map(one_head, jnp.arange(HEADS, dtype=jnp.int32))
    attn_value = jnp.einsum('hrl,hlv->rhv', attn_latent, value_up.astype(jnp.float32), precision=lax.Precision.HIGHEST).astype(jnp.bfloat16)
    attn_out = jnp.dot(attn_value.reshape(SEQ, HEADS * VH), out_proj, preferred_element_type=jnp.float32)
    hidden = (residual.astype(jnp.float32) + attn_out).astype(jnp.bfloat16)
    hidden_wide = hidden.astype(jnp.float32)
    mean_square = lax.optimization_barrier(jnp.mean(hidden_wide * hidden_wide, axis=1))
    normed = (hidden_wide * lax.rsqrt(mean_square + EPSILON)[:, None] * norm_gain.astype(jnp.float32)[None, :]).astype(jnp.bfloat16)
    group_range = jnp.arange(N_CTX, dtype=jnp.int32)
    expert_range = jnp.arange(EXP_GRP, dtype=jnp.int32)
    member = jnp.zeros((SEQ, N_CTX), jnp.int32)
    shares = jnp.zeros((SEQ, N_CTX, EXP_GRP), jnp.float32)
    for group_slot in range(TOPG):
        group_hit = group_ids[:, group_slot, None] == group_range[None, :]
        member = member + group_hit.astype(jnp.int32)
        for expert_slot in range(TOPE):
            expert_hit = (expert_ids[:, group_slot, expert_slot, None] == expert_range[None, :]).astype(jnp.float32)
            shares = shares + group_hit.astype(jnp.float32)[:, :, None] * expert_hit[:, None, :] * route_weights[:, group_slot, expert_slot, None, None].astype(jnp.float32)
    member = member.reshape(N_CTX, KB, N_CTX)
    ranking = jnp.cumsum(member, axis=1) - 1
    placement = ((member[..., None] == 1) & (ranking[..., None] == jnp.arange(CAP, dtype=jnp.int32))).astype(jnp.float32)
    shares = shares.reshape(N_CTX, KB, N_CTX, EXP_GRP)
    normed_blocks = normed.astype(jnp.float32).reshape(N_CTX, KB, D)
    feature_run = D // N_EXP

    def one_group(state, group):
        spots = lax.dynamic_index_in_dim(placement, group, 2, keepdims=False)
        group_share = lax.dynamic_index_in_dim(shares, group, 2, keepdims=False)
        inputs = jnp.einsum('btc,btd->bcd', spots, normed_blocks).reshape(N_CTX * CAP, D)
        weights = jnp.einsum('btc,bte->bce', spots, group_share).reshape(N_CTX * CAP, EXP_GRP)
        split_inputs = inputs.reshape(N_CTX * CAP, N_EXP, feature_run)
        outputs = jnp.zeros((N_CTX * CAP, D), jnp.float32)
        for expert in range(EXP_GRP):
            expert_index = group * EXP_GRP + expert
            gate_matrix = lax.dynamic_index_in_dim(w_gate, expert_index, 0, keepdims=False).astype(jnp.float32).reshape(N_EXP, feature_run, FF)
            up_matrix = lax.dynamic_index_in_dim(w_up, expert_index, 0, keepdims=False).astype(jnp.float32).reshape(N_EXP, feature_run, FF)
            down_matrix = lax.dynamic_index_in_dim(w_down, expert_index, 0, keepdims=False)
            gate = lax.optimization_barrier(jnp.sum(rounded(jnp.einsum('snd,ndf->snf', split_inputs, gate_matrix)), axis=1))
            lifted = lax.optimization_barrier(jnp.sum(rounded(jnp.einsum('snd,ndf->snf', split_inputs, up_matrix)), axis=1))
            activated = (jax.nn.silu(gate) * lifted).astype(jnp.bfloat16)
            down_part = jnp.dot(activated, down_matrix, preferred_element_type=jnp.float32)
            outputs = outputs + weights[:, expert, None] * down_part
        branch = rounded(outputs).reshape(N_CTX, CAP, D)
        return (state + jnp.einsum('btc,bcd->btd', spots, branch), None)
    expert_sum, unused = lax.scan(one_group, jnp.zeros((N_CTX, KB, D), jnp.float32), jnp.arange(N_CTX, dtype=jnp.int32))
    return (hidden_wide + expert_sum.reshape(SEQ, D)).astype(jnp.bfloat16)
```

```python
import functools

import jax
import jax.numpy as jnp
from jax import lax
from jax.experimental import pallas as pl
from jax.experimental.pallas import tpu as pltpu
from jax.sharding import Mesh
from jax.sharding import PartitionSpec as P

D = 2560
EPSILON = 1e-06
MASKED_SCORE = -1e30
CTX = ("y", "xh")
EXP = ("z", "xl", "core")
ZX = ("z", "xl")
XC = ("xl", "core")
TOK = 128
SLOT = 32
F32 = jnp.float32
BF16 = jnp.bfloat16
VMEM = pl.BlockSpec(memory_space=pltpu.VMEM)
SMEM = pl.BlockSpec(memory_space=pltpu.SMEM)


def call(body, out_shape, in_specs, scratch=(), flops=0, limit=40):
    many = isinstance(out_shape, (tuple, list))
    return pl.pallas_call(
        body,
        out_shape=out_shape,
        in_specs=in_specs,
        out_specs=[VMEM] * len(out_shape) if many else VMEM,
        scratch_shapes=scratch,
        compiler_params=pltpu.CompilerParams(vmem_limit_bytes=limit << 20),
    )


def shape(dims, dtype=BF16):
    return jax.ShapeDtypeStruct(dims, dtype)


def dot(a, b):
    return jnp.dot(a, b, preferred_element_type=F32)


def dot_nt(a, b):
    return lax.dot_general(a, b, (((1,), (1,)), ((), ())), preferred_element_type=F32)


def attend(
    rows, width, place, mask, qa, qb, ka, kb, va, vb, wo, mine, theirs, top, total, acc_a, acc_b
):
    block, core = place[0], place[1]
    inverse_root = width**-0.5
    q_a, q_b = qa[...], qb[...]
    query = lax.broadcasted_iota(jnp.int32, (2 * TOK, TOK), 0) % TOK
    key = lax.broadcasted_iota(jnp.int32, (2 * TOK, TOK), 1)

    def scores_of(b):
        return (dot(q_a, ka[b]) + dot(q_b, kb[b])) * inverse_root

    own = (key <= query) & (key < rows)
    masked = jnp.where(own, scores_of(block), MASKED_SCORE)
    best = jnp.max(masked, axis=1, keepdims=True)
    terms = jnp.where(own, jnp.exp(masked - best), 0.0)
    top[...] = best
    total[...] = jnp.sum(terms, axis=1, keepdims=True)
    acc_a[...] = dot_nt(terms.astype(BF16), ka[block])
    acc_b[...] = dot_nt(terms.astype(BF16), kb[block])

    def step(b, carry):
        @pl.when((mask[block, b] == 1) & (b != block))
        def _():
            inside = key < rows
            masked = jnp.where(inside, scores_of(b), MASKED_SCORE)
            old = top[...]
            best = jnp.maximum(old, jnp.max(masked, axis=1, keepdims=True))
            terms = jnp.where(inside, jnp.exp(masked - best), 0.0)
            shrink = jnp.exp(old - best)
            top[...] = best
            total[...] = total[...] * shrink + jnp.sum(terms, axis=1, keepdims=True)
            rounded = terms.astype(BF16)
            acc_a[...] = acc_a[...] * shrink + dot_nt(rounded, ka[b])
            acc_b[...] = acc_b[...] * shrink + dot_nt(rounded, kb[b])

        return carry

    lax.fori_loop(0, mask.shape[1], step, 0)
    inverse = 1.0 / total[...]
    values = []
    for head in range(2):
        span = slice(head * TOK, (head + 1) * TOK)
        value = jnp.zeros((TOK, TOK), F32)
        for acc, up in ((acc_a, va), (acc_b, vb)):
            latent = acc[span, :] * inverse[span, :]
            high = latent.astype(BF16)
            low = (latent - high.astype(F32)).astype(BF16)
            value = value + dot(high, up[head]) + dot(low, up[head])
        values.append(value.T.astype(BF16))
    stacked = jnp.concatenate(values, axis=0)
    runs, _, run, depth = wo.shape
    mine[...] = dot(wo[:, core].reshape(runs * run, depth), stacked).reshape(runs, run, TOK)
    theirs[...] = (
        dot(wo[:, 1 - core].reshape(runs * run, depth), stacked).reshape(runs, run, TOK).astype(BF16)
    )


def split_pair(value):
    high = value.astype(BF16).astype(F32)
    return high, (value - high).astype(BF16).astype(F32)


def tail_rows(value, count):
    high, low = split_pair(value)
    row = lax.broadcasted_iota(jnp.int32, (count, value.shape[1]), 0)
    return jnp.where(row == 0, high, jnp.where(row == 1, low, 0.0))


def make_rows(parts, residual, gain, places, hidden, sent):
    mixed = jnp.sum(parts[...].astype(F32), axis=0)
    held = (residual[...].astype(F32) + mixed).astype(BF16)
    hidden[...] = held
    wide = held.astype(F32)
    square = jnp.sum(wide * wide, axis=0, keepdims=True)
    run = wide.shape[0]
    rows = jnp.concatenate([wide * gain[...], tail_rows(square, TOK - run)], axis=0).astype(BF16)
    sent[...] = dot_nt(places[...], rows).astype(BF16)


def spread_rows(keep_rows, got, out):
    turned = got[...].T[:keep_rows]
    for i in range(out.shape[0]):
        out[i] = turned


def project_up(run, sub, inputs, weights, keep, out):
    count, _, slots = inputs.shape
    features = inputs[:, :run, :].reshape(count * run, slots)
    ends = inputs[:, run : run + 16, :].astype(F32)
    ends = jnp.sum(ends, axis=0)
    square = ends[0:1] + ends[1:2]
    unit = 2 * sub * out.shape[0]
    sums = [jnp.zeros((unit, slots), F32) for _ in range(2)]
    for expert in range(weights.shape[0] // unit):
        part = dot(weights[expert * unit : (expert + 1) * unit, :], features)
        for pick in range(2):
            sums[pick] = sums[pick] + keep[2 * expert + pick : 2 * expert + pick + 1, :] * part
    tail = tail_rows(square, 16)
    for dest in range(out.shape[0]):
        pieces = []
        for pick in range(2):
            for kind in range(2):
                start = kind * unit // 2 + dest * sub
                pieces.append(sums[pick][start : start + sub])
        out[dest] = jnp.concatenate(pieces + [tail], axis=0).astype(BF16)


def activate(sub, got, weight, out):
    total = jnp.sum(got[...].astype(F32), axis=0)
    square = total[4 * sub : 4 * sub + 1] + total[4 * sub + 1 : 4 * sub + 2]
    scale = lax.rsqrt(square / D + EPSILON)
    pieces = []
    for pick in range(2):
        gate = total[2 * pick * sub : (2 * pick + 1) * sub] * scale
        up = total[(2 * pick + 1) * sub : (2 * pick + 2) * sub] * scale
        act = gate / (1.0 + jnp.exp(-gate)) * up
        pieces.append(act * weight[pick : pick + 1, :])
    rounded = jnp.concatenate(pieces, axis=0).astype(BF16)
    for i in range(out.shape[0]):
        out[i] = rounded


def project_down(sub, acts, weights, keep, out):
    count, _, slots = acts.shape
    wide = acts[...].astype(F32)
    first = wide[:, :sub].reshape(count * sub, slots)
    second = wide[:, sub:].reshape(count * sub, slots)
    picked = []
    for expert in range(keep.shape[0] // 2):
        picked.append(
            (
                keep[2 * expert : 2 * expert + 1, :] * first
                + keep[2 * expert + 1 : 2 * expert + 2, :] * second
            ).astype(BF16)
        )
    stacked = jnp.concatenate(picked, axis=0)
    for dest in range(out.shape[0]):
        out[dest] = dot(weights[dest], stacked).astype(BF16)


def finish_rows(got, out):
    total = jnp.sum(got[...].astype(F32), axis=0).astype(BF16)
    run, slots = total.shape
    padded = jnp.concatenate([total, jnp.zeros((TOK - run, slots), BF16)], axis=0)
    out[...] = padded.T


def combine(got, places, hidden, out):
    run, rows = out.shape
    turned = got[...].T[:run]
    added = dot(turned, places[...])
    out[...] = (hidden[...].astype(F32) + added)[:, :rows].astype(BF16)


def exchange(x, axes):
    return lax.all_to_all(x, axes, split_axis=0, concat_axis=0, tiled=True)


def on_device(
    queries,
    latents,
    block_mask,
    value_up,
    out_proj,
    residual,
    norm_gain,
    group_ids,
    expert_ids,
    route_weights,
    w_gate,
    w_up,
    w_down,
):
    ctx_count = lax.axis_size(CTX)
    z_count = lax.axis_size("z")
    xc_count = lax.axis_size(XC)
    my_block = lax.axis_index(CTX)
    core = lax.axis_index("core")
    block_rows, key_width = latents.shape
    heads = queries.shape[1]
    latent_width, value_width = value_up.shape[1:]
    run = residual.shape[1]
    local_experts, _, hidden_units = w_gate.shape
    half = key_width // 2
    pad_rows = TOK - block_rows
    slots = ctx_count * SLOT
    part = hidden_units // z_count
    sub = part // xc_count

    keys = jnp.pad(latents.T, ((0, 0), (0, pad_rows)))
    own_half = lax.dynamic_slice_in_dim(keys, core * half, half, 0)
    keys_a = exchange(jnp.broadcast_to(own_half[None], (ctx_count, half, TOK)), CTX)
    keys_b = lax.ppermute(keys_a, "core", [(0, 1), (1, 0)])

    pairs = local_experts // 2
    both = jnp.stack([w_gate, w_up], axis=1).reshape(pairs, 2, 2, run, z_count, part)
    both = both.transpose(4, 0, 3, 1, 2, 5).reshape(z_count, pairs, run, 4 * part)
    both = exchange(both, "z")
    weights_in = both.transpose(1, 3, 0, 2).reshape(pairs * 4 * part, z_count * run)
    down = w_down.transpose(0, 2, 1).reshape(local_experts, run, z_count, xc_count, sub)
    down = down.transpose(3, 1, 0, 2, 4).reshape(xc_count, run, local_experts * z_count * sub)
    down = exchange(down, XC)

    group_range = jnp.arange(ctx_count)
    expert_range = jnp.arange(local_experts)
    member = jnp.zeros((block_rows, ctx_count), jnp.int32)
    shares = jnp.zeros((block_rows, ctx_count, local_experts), F32)
    for group_slot in range(group_ids.shape[1]):
        group_hit = group_ids[:, group_slot, None] == group_range[None, :]
        member = member + group_hit.astype(jnp.int32)
        for expert_slot in range(expert_ids.shape[2]):
            expert_hit = (
                expert_ids[:, group_slot, expert_slot, None] == expert_range[None, :]
            ).astype(F32)
            shares = shares + group_hit.astype(F32)[:, :, None] * expert_hit[
                :, None, :
            ] * route_weights[:, group_slot, expert_slot, None, None].astype(F32)
    ranking = jnp.cumsum(member, axis=0) - 1
    placement = (
        (member[:, :, None] == 1) & (ranking[:, :, None] == jnp.arange(SLOT)[None, None, :])
    ).astype(BF16)
    sent_weights = jnp.einsum(
        "tge,tgc->gec", shares.astype(BF16), placement, preferred_element_type=F32
    ).astype(BF16)
    got_weights = exchange(sent_weights, CTX)
    weights = got_weights.transpose(1, 0, 2).reshape(local_experts, slots).astype(F32)
    chosen = (weights > 0.0).astype(jnp.int32)
    ordinal = jnp.cumsum(chosen, axis=0) - 1
    keep = jnp.stack(
        [((chosen == 1) & (ordinal == pick)).astype(F32) for pick in range(2)], axis=1
    )
    pick_weight = jnp.sum(keep * weights[:, None, :], axis=0)
    keep = keep.reshape(2 * local_experts, slots)
    places = jnp.pad(placement.reshape(block_rows, slots).T, ((0, 0), (0, pad_rows)))

    wide_q = jnp.pad(queries.transpose(1, 0, 2), ((0, 0), (0, pad_rows), (0, 0)))
    wide_q = wide_q.reshape(heads * TOK, key_width)
    q_low, q_high = wide_q[:, :half], wide_q[:, half:]
    v_low = value_up[:, :half]
    v_high = jnp.pad(value_up[:, half:], ((0, 0), (0, key_width - latent_width), (0, 0)))
    flip = core == 1
    place = jnp.stack([my_block, core]).astype(jnp.int32)
    runs = D // run
    out_weights = out_proj.T.reshape(runs // 2, 2, run, heads * value_width)
    mine, theirs = call(
        functools.partial(attend, block_rows, key_width),
        [shape((runs // 2, run, TOK), F32), shape((runs // 2, run, TOK))],
        [SMEM, SMEM] + [VMEM] * 7,
        [
            pltpu.VMEM((2 * TOK, 1), F32),
            pltpu.VMEM((2 * TOK, 1), F32),
            pltpu.VMEM((2 * TOK, half), F32),
            pltpu.VMEM((2 * TOK, half), F32),
        ],
    )(
        place,
        block_mask,
        jnp.where(flip, q_high, q_low),
        jnp.where(flip, q_low, q_high),
        keys_a,
        keys_b,
        jnp.where(flip, v_high, v_low),
        jnp.where(flip, v_low, v_high),
        out_weights,
    )
    summed = (mine + lax.ppermute(theirs, "core", [(0, 1), (1, 0)]).astype(F32)).astype(BF16)
    parts = exchange(summed, ZX)

    hidden, sent = call(make_rows, [shape((run, TOK)), shape((slots, TOK))], [VMEM] * 4)(
        parts,
        jnp.pad(residual.T, ((0, 0), (0, pad_rows))),
        norm_gain.astype(F32)[:, None],
        places,
    )
    got = exchange(sent.reshape(ctx_count, SLOT, TOK), CTX).reshape(slots, TOK)
    spread = call(
        functools.partial(spread_rows, run + 16), shape((z_count, run + 16, slots)), [VMEM]
    )(got)
    inputs = exchange(spread, "z")
    partial_sums = call(
        functools.partial(project_up, run, sub),
        shape((xc_count, 4 * sub + 16, slots)),
        [VMEM] * 3,
    )(inputs, weights_in, keep)
    acts = call(functools.partial(activate, sub), shape((z_count, 2 * sub, slots)), [VMEM] * 2)(
        exchange(partial_sums, XC), pick_weight
    )
    outputs = call(
        functools.partial(project_down, sub), shape((xc_count, run, slots)), [VMEM] * 3
    )(exchange(acts, "z"), down, keep)
    returned = call(finish_rows, shape((slots, TOK)), [VMEM])(exchange(outputs, XC))
    returned = exchange(returned.reshape(ctx_count, SLOT, TOK), CTX).reshape(slots, TOK)
    out = call(combine, shape((run, block_rows)), [VMEM] * 3)(returned, places, hidden)
    return out.T


def solution(mesh):
    names = ("y", "xh", "z", "xl", "core")
    fine = Mesh(mesh.devices.reshape(8, 2, 8, 2, 2), names)
    return jax.shard_map(
        on_device,
        mesh=fine,
        in_specs=(
            P(CTX, EXP, None),
            P(CTX, None),
            P(),
            P(EXP, None, None),
            P(EXP, None),
            P(CTX, EXP),
            P(EXP),
            P(CTX, None),
            P(CTX, None, None),
            P(CTX, None, None),
            P(CTX, EXP, None),
            P(CTX, EXP, None),
            P(CTX, None, EXP),
        ),
        out_specs=P(CTX, EXP),
        check_vma=False,
    )
```

```python
import functools

import jax
import jax.numpy as jnp
from jax import lax
from jax.experimental import pallas as pl
from jax.experimental.pallas import tpu as pltpu
from jax.sharding import Mesh
from jax.sharding import PartitionSpec as P

D = 2560
EPSILON = 1e-06
MASKED_SCORE = -1e30
CTX = ("y", "xh")
EXP = ("z", "xl", "core")
ZX = ("z", "xl")
XC = ("xl", "core")
TOK = 128
SLOT = 32
F32 = jnp.float32
BF16 = jnp.bfloat16
VMEM = pl.BlockSpec(memory_space=pltpu.VMEM)
SMEM = pl.BlockSpec(memory_space=pltpu.SMEM)


def call(body, out_shape, in_specs, scratch=(), flops=0, limit=40):
    many = isinstance(out_shape, (tuple, list))
    return pl.pallas_call(
        body,
        out_shape=out_shape,
        in_specs=in_specs,
        out_specs=[VMEM] * len(out_shape) if many else VMEM,
        scratch_shapes=scratch,
        compiler_params=pltpu.CompilerParams(vmem_limit_bytes=limit << 20),
    )


def shape(dims, dtype=BF16):
    return jax.ShapeDtypeStruct(dims, dtype)


def dot(a, b):
    return jnp.dot(a, b, preferred_element_type=F32)


def dot_nt(a, b):
    return lax.dot_general(a, b, (((1,), (1,)), ((), ())), preferred_element_type=F32)


def attend(
    rows, width, place, mask, qa, qb, ka, kb, va, vb, wo, mine, theirs, top, total, acc_a, acc_b
):
    block, core = place[0], place[1]
    inverse_root = width**-0.5
    q_a, q_b = qa[...], qb[...]
    query = lax.broadcasted_iota(jnp.int32, (2 * TOK, TOK), 0) % TOK
    key = lax.broadcasted_iota(jnp.int32, (2 * TOK, TOK), 1)

    def scores_of(b):
        return (dot(q_a, ka[b]) + dot(q_b, kb[b])) * inverse_root

    own = (key <= query) & (key < rows)
    masked = jnp.where(own, scores_of(block), MASKED_SCORE)
    best = jnp.max(masked, axis=1, keepdims=True)
    terms = jnp.where(own, jnp.exp(masked - best), 0.0)
    top[...] = best
    total[...] = jnp.sum(terms, axis=1, keepdims=True)
    acc_a[...] = dot_nt(terms.astype(BF16), ka[block])
    acc_b[...] = dot_nt(terms.astype(BF16), kb[block])

    def step(b, carry):
        @pl.when((mask[block, b] == 1) & (b != block))
        def _():
            inside = key < rows
            masked = jnp.where(inside, scores_of(b), MASKED_SCORE)
            old = top[...]
            best = jnp.maximum(old, jnp.max(masked, axis=1, keepdims=True))
            terms = jnp.where(inside, jnp.exp(masked - best), 0.0)
            shrink = jnp.exp(old - best)
            top[...] = best
            total[...] = total[...] * shrink + jnp.sum(terms, axis=1, keepdims=True)
            rounded = terms.astype(BF16)
            acc_a[...] = acc_a[...] * shrink + dot_nt(rounded, ka[b])
            acc_b[...] = acc_b[...] * shrink + dot_nt(rounded, kb[b])

        return carry

    lax.fori_loop(0, mask.shape[1], step, 0)
    inverse = 1.0 / total[...]
    values = []
    for head in range(2):
        span = slice(head * TOK, (head + 1) * TOK)
        value = jnp.zeros((TOK, TOK), F32)
        for acc, up in ((acc_a, va), (acc_b, vb)):
            latent = acc[span, :] * inverse[span, :]
            high = latent.astype(BF16)
            low = (latent - high.astype(F32)).astype(BF16)
            value = value + dot(high, up[head]) + dot(low, up[head])
        values.append(value.T.astype(BF16))
    stacked = jnp.concatenate(values, axis=0)
    runs, _, run, depth = wo.shape
    mine[...] = dot(wo[:, core].reshape(runs * run, depth), stacked).reshape(runs, run, TOK)
    theirs[...] = (
        dot(wo[:, 1 - core].reshape(runs * run, depth), stacked).reshape(runs, run, TOK).astype(BF16)
    )


def split_pair(value):
    high = value.astype(BF16).astype(F32)
    return high, (value - high).astype(BF16).astype(F32)


def tail_rows(value, count):
    high, low = split_pair(value)
    row = lax.broadcasted_iota(jnp.int32, (count, value.shape[1]), 0)
    return jnp.where(row == 0, high, jnp.where(row == 1, low, 0.0))


def make_rows(parts, residual, gain, places, shares, hidden, sent):
    mixed = jnp.sum(parts[...].astype(F32), axis=0)
    held = (residual[...].astype(F32) + mixed).astype(BF16)
    hidden[...] = held
    wide = held.astype(F32)
    square = jnp.sum(wide * wide, axis=0, keepdims=True)
    run = wide.shape[0]
    rows = jnp.concatenate([wide * gain[...], tail_rows(square, TOK - run)], axis=0).astype(BF16)
    sent[...] = (dot_nt(places[...], rows) + shares[...].astype(F32)).astype(BF16)


def spread_rows(keep_rows, first, got, out, keep, weight):
    turned = got[...].T
    kept = turned[:keep_rows]
    for i in range(out.shape[0]):
        out[i] = kept
    count = keep.shape[0] // 2
    weights = turned[first : first + 16].astype(F32)
    seen = jnp.zeros((1, weights.shape[1]), F32)
    picked = [jnp.zeros((1, weights.shape[1]), F32) for _ in range(2)]
    for expert in range(count):
        row = weights[expert : expert + 1]
        chosen = jnp.where(row > 0.0, 1.0, 0.0)
        for pick in range(2):
            flag = jnp.where(seen == pick, chosen, 0.0)
            keep[2 * expert + pick : 2 * expert + pick + 1, :] = flag
            picked[pick] = picked[pick] + flag * row
        seen = seen + chosen
    weight[...] = jnp.concatenate(picked, axis=0)


def pack_in(place, gate, up, *refs):
    outs, held = refs[:-1], refs[-1]
    count = held.shape[0]
    part = gate.shape[2] // count
    for pair in range(held.shape[1]):
        for z in range(count):
            span = slice(z * part, (z + 1) * part)
            pieces = []
            for expert in (2 * pair, 2 * pair + 1):
                pieces += [gate[expert, :, span], up[expert, :, span]]
            held[z, pair] = jnp.concatenate(pieces, axis=1)
    for shift in range(count):
        outs[shift][...] = held[lax.rem(place[2] + shift, count)]


def turn_in(*refs):
    got, out = refs[:-1], refs[-1]
    for pair in range(got[0].shape[0]):
        wide = jnp.concatenate([g[pair] for g in got], axis=0)
        out[pair * wide.shape[1] : (pair + 1) * wide.shape[1], :] = wide.T


def pack_down(sub, place, weights, *refs):
    outs, held = refs[:-1], refs[-1]
    experts, run, hidden = weights.shape
    count = held.shape[0]
    per = hidden // count
    source = lax.broadcasted_iota(jnp.int32, (hidden, 1), 0)
    dest = (source % (count * sub)) // sub
    spot = (source // (count * sub)) * sub + source % sub
    column = lax.broadcasted_iota(jnp.int32, (hidden, count * 2 * TOK), 1)
    for odd in range(2):
        goal = dest * 2 * TOK + spot + jnp.where(spot >= TOK, odd * (2 * TOK - per), 0)
        order = jnp.where(column == goal, 1.0, 0.0).astype(BF16)
        stacked = jnp.concatenate([weights[i] for i in range(odd, experts, 2)], axis=0)
        moved = dot(stacked, order).astype(BF16).reshape(experts // 2, run, count * 2 * TOK)
        for pair in range(experts // 2):
            for i in range(count):
                a = moved[pair, :, i * 2 * TOK : i * 2 * TOK + TOK]
                b = moved[pair, :, i * 2 * TOK + TOK : (i + 1) * 2 * TOK]
                first, last = (2 * pair + odd) * TOK, (experts + pair) * TOK
                held[i, :, first : first + TOK] = a
                if odd == 0:
                    held[i, :, last : last + TOK] = b
                else:
                    held[i, :, last : last + TOK] += b
    for flip in range(count):
        outs[flip][...] = held[place[3] ^ flip]


def project_up(run, sub, place, inputs, weights, keep, out):
    count, _, slots = inputs.shape
    features = jnp.concatenate(
        [inputs[lax.rem(place[2] + count - i, count), :run, :] for i in range(count)], axis=0
    )
    ends = inputs[:, run : run + 16, :].astype(F32)
    ends = jnp.sum(ends, axis=0)
    square = ends[0:1] + ends[1:2]
    unit = 2 * sub * out.shape[0]
    sums = [jnp.zeros((unit, slots), F32) for _ in range(2)]
    for expert in range(weights.shape[0] // unit):
        part = dot(weights[expert * unit : (expert + 1) * unit, :], features)
        for pick in range(2):
            sums[pick] = sums[pick] + keep[2 * expert + pick : 2 * expert + pick + 1, :] * part
    tail = tail_rows(square, 16)
    for dest in range(out.shape[0]):
        pieces = []
        for pick in range(2):
            for kind in range(2):
                start = kind * unit // 2 + dest * sub
                pieces.append(sums[pick][start : start + sub])
        out[dest] = jnp.concatenate(pieces + [tail], axis=0).astype(BF16)


def activate(sub, got, weight, out):
    total = jnp.sum(got[...].astype(F32), axis=0)
    square = total[4 * sub : 4 * sub + 1] + total[4 * sub + 1 : 4 * sub + 2]
    scale = lax.rsqrt(square / D + EPSILON)
    pieces = []
    for pick in range(2):
        gate = total[2 * pick * sub : (2 * pick + 1) * sub] * scale
        up = total[(2 * pick + 1) * sub : (2 * pick + 2) * sub] * scale
        act = gate / (1.0 + jnp.exp(-gate)) * up
        pieces.append(act * weight[pick : pick + 1, :])
    rounded = jnp.concatenate(pieces, axis=0).astype(BF16)
    for i in range(out.shape[0]):
        out[i] = rounded


def project_down(sub, place, acts, keep, *refs):
    weights, out = refs[:-1], refs[-1]
    count, _, slots = acts.shape
    wide = acts[...].astype(F32)
    first = wide[:, :sub].reshape(count * sub, slots)
    second = wide[:, sub:].reshape(count * sub, slots)
    heads, tails = [], []
    for expert in range(keep.shape[0] // 2):
        picked = (
            keep[2 * expert : 2 * expert + 1, :] * first
            + keep[2 * expert + 1 : 2 * expert + 2, :] * second
        ).astype(BF16)
        heads.append(picked[:TOK])
        tails.append(picked[TOK:])
    stacked = jnp.concatenate(heads + tails, axis=0)
    for flip in range(len(weights)):
        out[place[3] ^ flip] = dot(weights[flip][...], stacked).astype(BF16)


def finish_rows(got, out):
    total = jnp.sum(got[...].astype(F32), axis=0).astype(BF16)
    run, slots = total.shape
    padded = jnp.concatenate([total, jnp.zeros((TOK - run, slots), BF16)], axis=0)
    out[...] = padded.T


def combine(got, places, hidden, out):
    run, rows = out.shape
    turned = got[...].T[:run]
    added = dot(turned, places[...])
    out[...] = (hidden[...].astype(F32) + added)[:, :rows].astype(BF16)


def exchange(x, axes):
    return lax.all_to_all(x, axes, split_axis=0, concat_axis=0, tiled=True)


def on_device(
    queries,
    latents,
    block_mask,
    value_up,
    out_proj,
    residual,
    norm_gain,
    group_ids,
    expert_ids,
    route_weights,
    w_gate,
    w_up,
    w_down,
):
    ctx_count = lax.axis_size(CTX)
    z_count = lax.axis_size("z")
    xc_count = lax.axis_size(XC)
    my_block = lax.axis_index(CTX)
    core = lax.axis_index("core")
    block_rows, key_width = latents.shape
    heads = queries.shape[1]
    latent_width, value_width = value_up.shape[1:]
    run = residual.shape[1]
    local_experts, _, hidden_units = w_gate.shape
    half = key_width // 2
    pad_rows = TOK - block_rows
    slots = ctx_count * SLOT
    part = hidden_units // z_count
    sub = part // xc_count

    keys = jnp.pad(latents.T, ((0, 0), (0, pad_rows)))
    own_half = lax.dynamic_slice_in_dim(keys, core * half, half, 0)
    keys_a = exchange(jnp.broadcast_to(own_half[None], (ctx_count, half, TOK)), CTX)
    keys_b = lax.ppermute(keys_a, "core", [(0, 1), (1, 0)])

    place = jnp.stack([my_block, core, lax.axis_index("z"), lax.axis_index(XC)]).astype(jnp.int32)
    pairs = local_experts // 2
    block = (pairs, run, 4 * part)
    packed = call(
        pack_in,
        [shape(block)] * z_count,
        [SMEM] + [VMEM] * 2,
        [pltpu.VMEM((z_count,) + block, BF16)],
    )(place, w_gate, w_up)
    moved_in = [packed[0]] + [
        lax.ppermute(packed[i], "z", [(a, (a + i) % z_count) for a in range(z_count)])
        for i in range(1, z_count)
    ]
    block = (run, local_experts * z_count * sub)
    packed = call(
        functools.partial(pack_down, sub),
        [shape(block)] * xc_count,
        [SMEM, VMEM],
        [pltpu.VMEM((xc_count,) + block, BF16)],
    )(place, w_down.transpose(0, 2, 1))
    moved_down = [packed[0]] + [
        lax.ppermute(packed[i], XC, [(a, a ^ i) for a in range(xc_count)])
        for i in range(1, xc_count)
    ]

    group_range = jnp.arange(ctx_count)
    expert_range = jnp.arange(local_experts)
    member = jnp.zeros((block_rows, ctx_count), jnp.int32)
    shares = jnp.zeros((block_rows, ctx_count, local_experts), F32)
    for group_slot in range(group_ids.shape[1]):
        group_hit = group_ids[:, group_slot, None] == group_range[None, :]
        member = member + group_hit.astype(jnp.int32)
        for expert_slot in range(expert_ids.shape[2]):
            expert_hit = (
                expert_ids[:, group_slot, expert_slot, None] == expert_range[None, :]
            ).astype(F32)
            shares = shares + group_hit.astype(F32)[:, :, None] * expert_hit[
                :, None, :
            ] * route_weights[:, group_slot, expert_slot, None, None].astype(F32)
    ranking = jnp.cumsum(member, axis=0) - 1
    placement = (
        (member[:, :, None] == 1) & (ranking[:, :, None] == jnp.arange(SLOT)[None, None, :])
    ).astype(BF16)
    first_share = run + 16
    slot_shares = jnp.einsum(
        "tge,tgc->gce", shares.astype(BF16), placement, preferred_element_type=F32
    ).astype(BF16)
    slot_shares = jnp.pad(
        slot_shares.reshape(slots, local_experts),
        ((0, 0), (first_share, TOK - first_share - local_experts)),
    )
    places = jnp.pad(placement.reshape(block_rows, slots).T, ((0, 0), (0, pad_rows)))

    wide_q = jnp.pad(queries.transpose(1, 0, 2), ((0, 0), (0, pad_rows), (0, 0)))
    wide_q = wide_q.reshape(heads * TOK, key_width)
    q_low, q_high = wide_q[:, :half], wide_q[:, half:]
    v_low = value_up[:, :half]
    v_high = jnp.pad(value_up[:, half:], ((0, 0), (0, key_width - latent_width), (0, 0)))
    flip = core == 1
    runs = D // run
    out_weights = out_proj.T.reshape(runs // 2, 2, run, heads * value_width)
    mine, theirs = call(
        functools.partial(attend, block_rows, key_width),
        [shape((runs // 2, run, TOK), F32), shape((runs // 2, run, TOK))],
        [SMEM, SMEM] + [VMEM] * 7,
        [
            pltpu.VMEM((2 * TOK, 1), F32),
            pltpu.VMEM((2 * TOK, 1), F32),
            pltpu.VMEM((2 * TOK, half), F32),
            pltpu.VMEM((2 * TOK, half), F32),
        ],
    )(
        place,
        block_mask,
        jnp.where(flip, q_high, q_low),
        jnp.where(flip, q_low, q_high),
        keys_a,
        keys_b,
        jnp.where(flip, v_high, v_low),
        jnp.where(flip, v_low, v_high),
        out_weights,
    )
    summed = (mine + lax.ppermute(theirs, "core", [(0, 1), (1, 0)]).astype(F32)).astype(BF16)
    parts = exchange(summed, ZX)
    hidden, sent = call(make_rows, [shape((run, TOK)), shape((slots, TOK))], [VMEM] * 5)(
        parts,
        jnp.pad(residual.T, ((0, 0), (0, pad_rows))),
        norm_gain.astype(F32)[:, None],
        places,
        slot_shares,
    )
    sent, *moved_in = lax.optimization_barrier((sent, *moved_in))
    weights_in = call(
        turn_in, shape((pairs * 4 * part, z_count * run)), [VMEM] * z_count
    )(*moved_in)
    got = exchange(sent.reshape(ctx_count, SLOT, TOK), CTX).reshape(slots, TOK)
    spread, keep, pick_weight = call(
        functools.partial(spread_rows, run + 16, first_share),
        [
            shape((z_count, run + 16, slots)),
            shape((2 * local_experts, slots), F32),
            shape((2, slots), F32),
        ],
        [VMEM],
    )(got)
    spread, *moved_down = lax.optimization_barrier((spread, *moved_down))
    inputs = exchange(spread, "z")
    partial_sums = call(
        functools.partial(project_up, run, sub),
        shape((xc_count, 4 * sub + 16, slots)),
        [SMEM] + [VMEM] * 3,
    )(place, inputs, weights_in, keep)
    acts = call(functools.partial(activate, sub), shape((z_count, 2 * sub, slots)), [VMEM] * 2)(
        exchange(partial_sums, XC), pick_weight
    )
    outputs = call(
        functools.partial(project_down, sub),
        shape((xc_count, run, slots)),
        [SMEM] + [VMEM] * (2 + xc_count),
    )(place, exchange(acts, "z"), keep, *moved_down)
    returned = call(finish_rows, shape((slots, TOK)), [VMEM])(exchange(outputs, XC))
    returned = exchange(returned.reshape(ctx_count, SLOT, TOK), CTX).reshape(slots, TOK)
    out = call(combine, shape((run, block_rows)), [VMEM] * 3)(returned, places, hidden)
    return out.T


def solution(mesh):
    names = ("y", "xh", "z", "xl", "core")
    fine = Mesh(mesh.devices.reshape(8, 2, 8, 2, 2), names)
    return jax.shard_map(
        on_device,
        mesh=fine,
        in_specs=(
            P(CTX, EXP, None),
            P(CTX, None),
            P(),
            P(EXP, None, None),
            P(EXP, None),
            P(CTX, EXP),
            P(EXP),
            P(CTX, None),
            P(CTX, None, None),
            P(CTX, None, None),
            P(CTX, EXP, None),
            P(CTX, EXP, None),
            P(CTX, None, EXP),
        ),
        out_specs=P(CTX, EXP),
        check_vma=False,
    )
```

```python
import functools

import jax
import jax.numpy as jnp
from jax import lax
from jax.experimental import pallas as pl
from jax.experimental.pallas import tpu as pltpu
from jax.sharding import Mesh
from jax.sharding import PartitionSpec as P

D = 2560
EPSILON = 1e-06
MASKED_SCORE = -1e30
CTX = ("y", "xh")
EXP = ("za", "zb", "xl", "core")
ZX = ("za", "zb", "xl")
NEAR = ("zb", "xl", "core")
FAR = "za"
TOK = 128
SLOT = 32
F32 = jnp.float32
BF16 = jnp.bfloat16
VMEM = pl.BlockSpec(memory_space=pltpu.VMEM)
SMEM = pl.BlockSpec(memory_space=pltpu.SMEM)


def call(body, out_shape, in_specs, scratch=(), flops=0, limit=40):
    many = isinstance(out_shape, (tuple, list))
    return pl.pallas_call(
        body,
        out_shape=out_shape,
        in_specs=in_specs,
        out_specs=[VMEM] * len(out_shape) if many else VMEM,
        scratch_shapes=scratch,
        compiler_params=pltpu.CompilerParams(vmem_limit_bytes=limit << 20),
    )


def shape(dims, dtype=BF16):
    return jax.ShapeDtypeStruct(dims, dtype)


def dot(a, b):
    return jnp.dot(a, b, preferred_element_type=F32)


def dot_nt(a, b):
    return lax.dot_general(a, b, (((1,), (1,)), ((), ())), preferred_element_type=F32)


def attend(
    rows, width, place, mask, qa, qb, ka, kb, va, vb, wo, mine, theirs, top, total, acc_a, acc_b
):
    block, core = place[0], place[1]
    inverse_root = width**-0.5
    q_a, q_b = qa[...], qb[...]
    query = lax.broadcasted_iota(jnp.int32, (2 * TOK, TOK), 0) % TOK
    key = lax.broadcasted_iota(jnp.int32, (2 * TOK, TOK), 1)

    def scores_of(b):
        return (dot(q_a, ka[b]) + dot(q_b, kb[b])) * inverse_root

    own = (key <= query) & (key < rows)
    masked = jnp.where(own, scores_of(block), MASKED_SCORE)
    best = jnp.max(masked, axis=1, keepdims=True)
    terms = jnp.where(own, jnp.exp(masked - best), 0.0)
    top[...] = best
    total[...] = jnp.sum(terms, axis=1, keepdims=True)
    acc_a[...] = dot_nt(terms.astype(BF16), ka[block])
    acc_b[...] = dot_nt(terms.astype(BF16), kb[block])

    def step(b, carry):
        @pl.when((mask[block, b] == 1) & (b != block))
        def _():
            inside = key < rows
            masked = jnp.where(inside, scores_of(b), MASKED_SCORE)
            old = top[...]
            best = jnp.maximum(old, jnp.max(masked, axis=1, keepdims=True))
            terms = jnp.where(inside, jnp.exp(masked - best), 0.0)
            shrink = jnp.exp(old - best)
            top[...] = best
            total[...] = total[...] * shrink + jnp.sum(terms, axis=1, keepdims=True)
            rounded = terms.astype(BF16)
            acc_a[...] = acc_a[...] * shrink + dot_nt(rounded, ka[b])
            acc_b[...] = acc_b[...] * shrink + dot_nt(rounded, kb[b])

        return carry

    lax.fori_loop(0, mask.shape[1], step, 0)
    inverse = 1.0 / total[...]
    values = []
    for head in range(2):
        span = slice(head * TOK, (head + 1) * TOK)
        value = jnp.zeros((TOK, TOK), F32)
        for acc, up in ((acc_a, va), (acc_b, vb)):
            latent = acc[span, :] * inverse[span, :]
            high = latent.astype(BF16)
            low = (latent - high.astype(F32)).astype(BF16)
            value = value + dot(high, up[head]) + dot(low, up[head])
        values.append(value.T.astype(BF16))
    stacked = jnp.concatenate(values, axis=0)
    runs, _, run, depth = wo.shape
    mine[...] = dot(wo[:, core].reshape(runs * run, depth), stacked).reshape(runs, run, TOK)
    theirs[...] = (
        dot(wo[:, 1 - core].reshape(runs * run, depth), stacked).reshape(runs, run, TOK).astype(BF16)
    )


def split_pair(value):
    high = value.astype(BF16).astype(F32)
    return high, (value - high).astype(BF16).astype(F32)


def tail_rows(value, count):
    high, low = split_pair(value)
    row = lax.broadcasted_iota(jnp.int32, (count, value.shape[1]), 0)
    return jnp.where(row == 0, high, jnp.where(row == 1, low, 0.0))


def make_rows(parts, residual, gain, places, shares, hidden, sent):
    mixed = jnp.sum(parts[...].astype(F32), axis=0)
    held = (residual[...].astype(F32) + mixed).astype(BF16)
    hidden[...] = held
    wide = held.astype(F32)
    square = jnp.sum(wide * wide, axis=0, keepdims=True)
    run = wide.shape[0]
    rows = jnp.concatenate([wide * gain[...], tail_rows(square, TOK - run)], axis=0).astype(BF16)
    sent[...] = (dot_nt(places[...], rows) + shares[...].astype(F32)).astype(BF16)


def spread_rows(keep_rows, first, got, out, keep, weight):
    turned = got[...].T
    kept = turned[:keep_rows]
    for i in range(out.shape[0]):
        out[i] = kept
    count = keep.shape[0] // 2
    weights = turned[first : first + 16].astype(F32)
    seen = jnp.zeros((1, weights.shape[1]), F32)
    picked = [jnp.zeros((1, weights.shape[1]), F32) for _ in range(2)]
    for expert in range(count):
        row = weights[expert : expert + 1]
        chosen = jnp.where(row > 0.0, 1.0, 0.0)
        for pick in range(2):
            flag = jnp.where(seen == pick, chosen, 0.0)
            keep[2 * expert + pick : 2 * expert + pick + 1, :] = flag
            picked[pick] = picked[pick] + flag * row
        seen = seen + chosen
    weight[...] = jnp.concatenate(picked, axis=0)


def pack(place, gate, up, down, *refs):
    outs, held = refs[:-1], refs[-1]
    count = held.shape[0]
    part = gate.shape[2] // count
    for pair in range(held.shape[1]):
        for near in range(count):
            span = slice(near * part, (near + 1) * part)
            pieces = []
            for expert in (2 * pair, 2 * pair + 1):
                pieces += [gate[expert, :, span], up[expert, :, span]]
            pieces += [down[2 * pair, :, span], down[2 * pair + 1, :, span]]
            held[near, pair] = jnp.concatenate(pieces, axis=1)
    for flip in range(count):
        outs[flip][...] = held[place[2] ^ flip]


def unpack(part, *refs):
    got, into, back = refs[:-2], refs[-2], refs[-1]
    pairs = got[0].shape[0]
    for pair in range(pairs):
        wide = jnp.concatenate([g[pair, :, : 4 * part] for g in got], axis=0)
        into[pair * 4 * part : (pair + 1) * 4 * part, :] = wide.T
    for flip, g in enumerate(got):
        back[flip] = jnp.concatenate([g[pair, :, 4 * part :] for pair in range(pairs)], axis=1)


def project_up(run, sub, place, inputs, weights, keep, out):
    count, _, slots = inputs.shape
    features = jnp.concatenate(
        [inputs[place[2] ^ flip, :run, :] for flip in range(count)], axis=0
    )
    ends = inputs[:, run : run + 16, :].astype(F32)
    ends = jnp.sum(ends, axis=0)
    square = ends[0:1] + ends[1:2]
    unit = 2 * sub * out.shape[0]
    sums = [jnp.zeros((unit, slots), F32) for _ in range(2)]
    for expert in range(weights.shape[0] // unit):
        part = dot(weights[expert * unit : (expert + 1) * unit, :], features)
        for pick in range(2):
            sums[pick] = sums[pick] + keep[2 * expert + pick : 2 * expert + pick + 1, :] * part
    tail = tail_rows(square, 16)
    for dest in range(out.shape[0]):
        pieces = []
        for pick in range(2):
            for kind in range(2):
                start = kind * unit // 2 + dest * sub
                pieces.append(sums[pick][start : start + sub])
        out[dest] = jnp.concatenate(pieces + [tail], axis=0).astype(BF16)


def activate(sub, got, weight, out):
    total = jnp.sum(got[...].astype(F32), axis=0)
    square = total[4 * sub : 4 * sub + 1] + total[4 * sub + 1 : 4 * sub + 2]
    scale = lax.rsqrt(square / D + EPSILON)
    pieces = []
    for pick in range(2):
        gate = total[2 * pick * sub : (2 * pick + 1) * sub] * scale
        up = total[(2 * pick + 1) * sub : (2 * pick + 2) * sub] * scale
        act = gate / (1.0 + jnp.exp(-gate)) * up
        pieces.append(act * weight[pick : pick + 1, :])
    rounded = jnp.concatenate(pieces, axis=0).astype(BF16)
    for i in range(out.shape[0]):
        out[i] = rounded


def project_down(sub, place, acts, keep, weights, out):
    count, _, slots = acts.shape
    wide = acts[...].astype(F32)
    first = wide[:, :sub].reshape(count * sub, slots)
    second = wide[:, sub:].reshape(count * sub, slots)
    picked = []
    for expert in range(keep.shape[0] // 2):
        picked.append(
            (
                keep[2 * expert : 2 * expert + 1, :] * first
                + keep[2 * expert + 1 : 2 * expert + 2, :] * second
            ).astype(BF16)
        )
    stacked = jnp.concatenate(picked, axis=0)
    for flip in range(weights.shape[0]):
        out[place[2] ^ flip] = dot(weights[flip], stacked).astype(BF16)


def finish_rows(got, out):
    total = jnp.sum(got[...].astype(F32), axis=0).astype(BF16)
    run, slots = total.shape
    padded = jnp.concatenate([total, jnp.zeros((TOK - run, slots), BF16)], axis=0)
    out[...] = padded.T


def combine(got, places, hidden, out):
    run, rows = out.shape
    turned = got[...].T[:run]
    added = dot(turned, places[...])
    out[...] = (hidden[...].astype(F32) + added)[:, :rows].astype(BF16)


def exchange(x, axes):
    return lax.all_to_all(x, axes, split_axis=0, concat_axis=0, tiled=True)


def on_device(
    queries,
    latents,
    block_mask,
    value_up,
    out_proj,
    residual,
    norm_gain,
    group_ids,
    expert_ids,
    route_weights,
    w_gate,
    w_up,
    w_down,
):
    ctx_count = lax.axis_size(CTX)
    near_count = lax.axis_size(NEAR)
    far_count = lax.axis_size(FAR)
    my_block = lax.axis_index(CTX)
    core = lax.axis_index("core")
    block_rows, key_width = latents.shape
    heads = queries.shape[1]
    latent_width, value_width = value_up.shape[1:]
    run = residual.shape[1]
    local_experts, _, hidden_units = w_gate.shape
    half = key_width // 2
    pad_rows = TOK - block_rows
    slots = ctx_count * SLOT
    part = hidden_units // near_count
    sub = part // far_count

    keys = jnp.pad(latents.T, ((0, 0), (0, pad_rows)))
    own_half = lax.dynamic_slice_in_dim(keys, core * half, half, 0)
    keys_a = exchange(jnp.broadcast_to(own_half[None], (ctx_count, half, TOK)), CTX)

    place = jnp.stack([my_block, core, lax.axis_index(NEAR)]).astype(jnp.int32)
    pairs = local_experts // 2
    block = (pairs, run, 6 * part)
    packed = call(
        pack,
        [shape(block)] * near_count,
        [SMEM] + [VMEM] * 3,
        [pltpu.VMEM((near_count,) + block, BF16)],
    )(place, w_gate, w_up, w_down.transpose(0, 2, 1))

    def flipped(x, flip):
        return lax.ppermute(x, NEAR, [(a, a ^ flip) for a in range(near_count)])

    moved = [packed[0]] + [flipped(packed[i], i) for i in range(1, near_count)]

    group_range = jnp.arange(ctx_count)
    expert_range = jnp.arange(local_experts)
    member = jnp.zeros((block_rows, ctx_count), jnp.int32)
    shares = jnp.zeros((block_rows, ctx_count, local_experts), F32)
    for group_slot in range(group_ids.shape[1]):
        group_hit = group_ids[:, group_slot, None] == group_range[None, :]
        member = member + group_hit.astype(jnp.int32)
        for expert_slot in range(expert_ids.shape[2]):
            expert_hit = (
                expert_ids[:, group_slot, expert_slot, None] == expert_range[None, :]
            ).astype(F32)
            shares = shares + group_hit.astype(F32)[:, :, None] * expert_hit[
                :, None, :
            ] * route_weights[:, group_slot, expert_slot, None, None].astype(F32)
    ranking = jnp.cumsum(member, axis=0) - 1
    placement = (
        (member[:, :, None] == 1) & (ranking[:, :, None] == jnp.arange(SLOT)[None, None, :])
    ).astype(BF16)
    first_share = run + 16
    slot_shares = jnp.einsum(
        "tge,tgc->gce", shares.astype(BF16), placement, preferred_element_type=F32
    ).astype(BF16)
    slot_shares = jnp.pad(
        slot_shares.reshape(slots, local_experts),
        ((0, 0), (first_share, TOK - first_share - local_experts)),
    )
    places = jnp.pad(placement.reshape(block_rows, slots).T, ((0, 0), (0, pad_rows)))

    wide_q = jnp.pad(queries.transpose(1, 0, 2), ((0, 0), (0, pad_rows), (0, 0)))
    wide_q = wide_q.reshape(heads * TOK, key_width)
    q_low, q_high = wide_q[:, :half], wide_q[:, half:]
    v_low = value_up[:, :half]
    v_high = jnp.pad(value_up[:, half:], ((0, 0), (0, key_width - latent_width), (0, 0)))
    flip = core == 1
    runs = D // run
    out_weights = out_proj.T.reshape(runs // 2, 2, run, heads * value_width)
    operands = (
        jnp.where(flip, q_high, q_low),
        jnp.where(flip, q_low, q_high),
        jnp.where(flip, v_high, v_low),
        jnp.where(flip, v_low, v_high),
        out_weights,
    )
    resid = jnp.pad(residual.T, ((0, 0), (0, pad_rows)))
    gain = norm_gain.astype(F32)[:, None]
    keys_a, operands, moved, places, slot_shares, resid, gain = lax.optimization_barrier(
        (keys_a, operands, moved, places, slot_shares, resid, gain)
    )
    keys_b = lax.ppermute(keys_a, "core", [(0, 1), (1, 0)])
    q_a, q_b, v_a, v_b, out_weights = operands
    mine, theirs = call(
        functools.partial(attend, block_rows, key_width),
        [shape((runs // 2, run, TOK), F32), shape((runs // 2, run, TOK))],
        [SMEM, SMEM] + [VMEM] * 7,
        [
            pltpu.VMEM((2 * TOK, 1), F32),
            pltpu.VMEM((2 * TOK, 1), F32),
            pltpu.VMEM((2 * TOK, half), F32),
            pltpu.VMEM((2 * TOK, half), F32),
        ],
    )(place, block_mask, q_a, q_b, keys_a, keys_b, v_a, v_b, out_weights)
    summed = (mine + lax.ppermute(theirs, "core", [(0, 1), (1, 0)]).astype(F32)).astype(BF16)
    parts = exchange(summed, ZX)

    hidden, sent = call(make_rows, [shape((run, TOK)), shape((slots, TOK))], [VMEM] * 5)(
        parts,
        resid,
        gain,
        places,
        slot_shares,
    )
    weights_in, weights_back = call(
        functools.partial(unpack, part),
        [
            shape((pairs * 4 * part, near_count * run)),
            shape((near_count, run, local_experts * part)),
        ],
        [VMEM] * near_count,
    )(*moved)
    got = exchange(sent.reshape(ctx_count, SLOT, TOK), CTX).reshape(slots, TOK)
    spread, keep, pick_weight = call(
        functools.partial(spread_rows, run + 16, first_share),
        [
            shape((near_count, run + 16, slots)),
            shape((2 * local_experts, slots), F32),
            shape((2, slots), F32),
        ],
        [VMEM],
    )(got)
    inputs = exchange(spread, NEAR)
    partial_sums = call(
        functools.partial(project_up, run, sub),
        shape((far_count, 4 * sub + 16, slots)),
        [SMEM] + [VMEM] * 3,
    )(place, inputs, weights_in, keep)
    acts = call(functools.partial(activate, sub), shape((far_count, 2 * sub, slots)), [VMEM] * 2)(
        exchange(partial_sums, FAR), pick_weight
    )
    outputs = call(
        functools.partial(project_down, sub),
        shape((near_count, run, slots)),
        [SMEM] + [VMEM] * 3,
    )(place, exchange(acts, FAR), keep, weights_back)
    returned = call(finish_rows, shape((slots, TOK)), [VMEM])(exchange(outputs, NEAR))
    returned = exchange(returned.reshape(ctx_count, SLOT, TOK), CTX).reshape(slots, TOK)
    out = call(combine, shape((run, block_rows)), [VMEM] * 3)(returned, places, hidden)
    return out.T


def solution(mesh):
    names = ("y", "xh", "za", "zb", "xl", "core")
    fine = Mesh(mesh.devices.reshape(8, 2, 4, 2, 2, 2), names)
    return jax.shard_map(
        on_device,
        mesh=fine,
        in_specs=(
            P(CTX, EXP, None),
            P(CTX, None),
            P(),
            P(EXP, None, None),
            P(EXP, None),
            P(CTX, EXP),
            P(EXP),
            P(CTX, None),
            P(CTX, None, None),
            P(CTX, None, None),
            P(CTX, EXP, None),
            P(CTX, EXP, None),
            P(CTX, None, EXP),
        ),
        out_specs=P(CTX, EXP),
        check_vma=False,
    )
```

```python
import functools

import jax
import jax.numpy as jnp
from jax import lax
from jax.experimental import pallas as pl
from jax.experimental.pallas import tpu as pltpu
from jax.sharding import Mesh
from jax.sharding import PartitionSpec as P

D = 2560
EPSILON = 1e-06
MASKED_SCORE = -1e30
CTX = ("y", "xh")
EXP = ("za", "zb", "xl", "core")
ZX = ("za", "zb", "xl")
NEAR = ("zb", "xl", "core")
FAR = "za"
TOK = 128
SLOT = 32
F32 = jnp.float32
BF16 = jnp.bfloat16
VMEM = pl.BlockSpec(memory_space=pltpu.VMEM)
SMEM = pl.BlockSpec(memory_space=pltpu.SMEM)


def call(body, out_shape, in_specs, scratch=(), flops=0, limit=40):
    many = isinstance(out_shape, (tuple, list))
    return pl.pallas_call(
        body,
        out_shape=out_shape,
        in_specs=in_specs,
        out_specs=[VMEM] * len(out_shape) if many else VMEM,
        scratch_shapes=scratch,
        compiler_params=pltpu.CompilerParams(vmem_limit_bytes=limit << 20),
    )


def shape(dims, dtype=BF16):
    return jax.ShapeDtypeStruct(dims, dtype)


def dot(a, b):
    return jnp.dot(a, b, preferred_element_type=F32)


def dot_nt(a, b):
    return lax.dot_general(a, b, (((1,), (1,)), ((), ())), preferred_element_type=F32)


def attend(
    rows, width, place, mask, qa, qb, ka, kb, va, vb, wo, mine, theirs, top, total, acc_a, acc_b
):
    block, core = place[0], place[1]
    inverse_root = width**-0.5
    q_a, q_b = qa[...], qb[...]
    query = lax.broadcasted_iota(jnp.int32, (2 * TOK, TOK), 0) % TOK
    key = lax.broadcasted_iota(jnp.int32, (2 * TOK, TOK), 1)

    def scores_of(b):
        return (dot(q_a, ka[b]) + dot(q_b, kb[b])) * inverse_root

    own = (key <= query) & (key < rows)
    masked = jnp.where(own, scores_of(block), MASKED_SCORE)
    best = jnp.max(masked, axis=1, keepdims=True)
    terms = jnp.where(own, jnp.exp(masked - best), 0.0)
    top[...] = best
    total[...] = jnp.sum(terms, axis=1, keepdims=True)
    acc_a[...] = dot_nt(terms.astype(BF16), ka[block])
    acc_b[...] = dot_nt(terms.astype(BF16), kb[block])

    def step(b, carry):
        @pl.when((mask[block, b] == 1) & (b != block))
        def _():
            inside = key < rows
            masked = jnp.where(inside, scores_of(b), MASKED_SCORE)
            old = top[...]
            best = jnp.maximum(old, jnp.max(masked, axis=1, keepdims=True))
            terms = jnp.where(inside, jnp.exp(masked - best), 0.0)
            shrink = jnp.exp(old - best)
            top[...] = best
            total[...] = total[...] * shrink + jnp.sum(terms, axis=1, keepdims=True)
            rounded = terms.astype(BF16)
            acc_a[...] = acc_a[...] * shrink + dot_nt(rounded, ka[b])
            acc_b[...] = acc_b[...] * shrink + dot_nt(rounded, kb[b])

        return carry

    lax.fori_loop(0, mask.shape[1], step, 0)
    inverse = 1.0 / total[...]
    values = []
    for head in range(2):
        span = slice(head * TOK, (head + 1) * TOK)
        value = jnp.zeros((TOK, TOK), F32)
        for acc, up in ((acc_a, va), (acc_b, vb)):
            latent = acc[span, :] * inverse[span, :]
            high = latent.astype(BF16)
            low = (latent - high.astype(F32)).astype(BF16)
            value = value + dot(high, up[head]) + dot(low, up[head])
        values.append(value.T.astype(BF16))
    stacked = jnp.concatenate(values, axis=0)
    runs, _, run, depth = wo.shape
    mine[...] = dot(wo[:, core].reshape(runs * run, depth), stacked).reshape(runs, run, TOK)
    theirs[...] = (
        dot(wo[:, 1 - core].reshape(runs * run, depth), stacked).reshape(runs, run, TOK).astype(BF16)
    )


def split_pair(value):
    high = value.astype(BF16).astype(F32)
    return high, (value - high).astype(BF16).astype(F32)


def tail_rows(value, count):
    high, low = split_pair(value)
    row = lax.broadcasted_iota(jnp.int32, (count, value.shape[1]), 0)
    return jnp.where(row == 0, high, jnp.where(row == 1, low, 0.0))


def make_rows(parts, residual, gain, places, shares, hidden, sent):
    mixed = jnp.sum(parts[...].astype(F32), axis=0)
    held = (residual[...].astype(F32) + mixed).astype(BF16)
    hidden[...] = held
    wide = held.astype(F32)
    square = jnp.sum(wide * wide, axis=0, keepdims=True)
    run = wide.shape[0]
    rows = jnp.concatenate([wide * gain[...], tail_rows(square, TOK - run)], axis=0).astype(BF16)
    sent[...] = (dot_nt(places[...], rows) + shares[...].astype(F32)).astype(BF16)


def spread_rows(keep_rows, first, got, out, keep, weight):
    turned = got[...].T
    kept = turned[:keep_rows]
    for i in range(out.shape[0]):
        out[i] = kept
    count = keep.shape[0] // 2
    weights = turned[first : first + 16].astype(F32)
    seen = jnp.zeros((1, weights.shape[1]), F32)
    picked = [jnp.zeros((1, weights.shape[1]), F32) for _ in range(2)]
    for expert in range(count):
        row = weights[expert : expert + 1]
        chosen = jnp.where(row > 0.0, 1.0, 0.0)
        for pick in range(2):
            flag = jnp.where(seen == pick, chosen, 0.0)
            keep[2 * expert + pick : 2 * expert + pick + 1, :] = flag
            picked[pick] = picked[pick] + flag * row
        seen = seen + chosen
    weight[...] = jnp.concatenate(picked, axis=0)


def pack(place, gate, up, down, *refs):
    outs, held = refs[:-1], refs[-1]
    count = held.shape[0]
    part = gate.shape[2] // count
    for pair in range(held.shape[1]):
        for near in range(count):
            span = slice(near * part, (near + 1) * part)
            pieces = []
            for expert in (2 * pair, 2 * pair + 1):
                pieces += [gate[expert, :, span], up[expert, :, span]]
            pieces += [down[2 * pair, :, span], down[2 * pair + 1, :, span]]
            held[near, pair] = jnp.concatenate(pieces, axis=1)
    for flip in range(count):
        outs[flip][...] = held[place[2] ^ flip]


def unpack(part, *refs):
    got, into, back = refs[:-2], refs[-2], refs[-1]
    pairs = got[0].shape[0]
    for pair in range(pairs):
        wide = jnp.concatenate([g[pair, :, : 4 * part] for g in got], axis=0)
        into[pair * 4 * part : (pair + 1) * 4 * part, :] = wide.T
    for flip, g in enumerate(got):
        back[flip] = jnp.concatenate([g[pair, :, 4 * part :] for pair in range(pairs)], axis=1)


def project_up(run, sub, place, inputs, weights, keep, out):
    count, _, slots = inputs.shape
    features = jnp.concatenate(
        [inputs[place[2] ^ flip, :run, :] for flip in range(count)], axis=0
    )
    ends = inputs[:, run : run + 16, :].astype(F32)
    ends = jnp.sum(ends, axis=0)
    square = ends[0:1] + ends[1:2]
    unit = 2 * sub * out.shape[0]
    sums = [jnp.zeros((unit, slots), F32) for _ in range(2)]
    for expert in range(weights.shape[0] // unit):
        part = dot(weights[expert * unit : (expert + 1) * unit, :], features)
        for pick in range(2):
            sums[pick] = sums[pick] + keep[2 * expert + pick : 2 * expert + pick + 1, :] * part
    tail = tail_rows(square, 16)
    for dest in range(out.shape[0]):
        pieces = []
        for pick in range(2):
            for kind in range(2):
                start = kind * unit // 2 + dest * sub
                pieces.append(sums[pick][start : start + sub])
        out[dest] = jnp.concatenate(pieces + [tail], axis=0).astype(BF16)


def activate(sub, got, weight, out):
    total = jnp.sum(got[...].astype(F32), axis=0)
    square = total[4 * sub : 4 * sub + 1] + total[4 * sub + 1 : 4 * sub + 2]
    scale = lax.rsqrt(square / D + EPSILON)
    pieces = []
    for pick in range(2):
        gate = total[2 * pick * sub : (2 * pick + 1) * sub] * scale
        up = total[(2 * pick + 1) * sub : (2 * pick + 2) * sub] * scale
        act = gate / (1.0 + jnp.exp(-gate)) * up
        pieces.append(act * weight[pick : pick + 1, :])
    rounded = jnp.concatenate(pieces, axis=0).astype(BF16)
    for i in range(out.shape[0]):
        out[i] = rounded


def project_down(sub, place, acts, keep, weights, out):
    count, _, slots = acts.shape
    wide = acts[...].astype(F32)
    first = wide[:, :sub].reshape(count * sub, slots)
    second = wide[:, sub:].reshape(count * sub, slots)
    picked = []
    for expert in range(keep.shape[0] // 2):
        picked.append(
            (
                keep[2 * expert : 2 * expert + 1, :] * first
                + keep[2 * expert + 1 : 2 * expert + 2, :] * second
            ).astype(BF16)
        )
    stacked = jnp.concatenate(picked, axis=0)
    for flip in range(weights.shape[0]):
        out[place[2] ^ flip] = dot(weights[flip], stacked).astype(BF16)


def finish_rows(got, out):
    total = jnp.sum(got[...].astype(F32), axis=0).astype(BF16)
    run, slots = total.shape
    padded = jnp.concatenate([total, jnp.zeros((TOK - run, slots), BF16)], axis=0)
    out[...] = padded.T


def combine(got, places, hidden, out):
    run, rows = out.shape
    turned = got[...].T[:run]
    added = dot(turned, places[...])
    out[...] = (hidden[...].astype(F32) + added)[:, :rows].astype(BF16)


def exchange(x, axes):
    return lax.all_to_all(x, axes, split_axis=0, concat_axis=0, tiled=True)


def on_device(
    queries,
    latents,
    block_mask,
    value_up,
    out_proj,
    residual,
    norm_gain,
    group_ids,
    expert_ids,
    route_weights,
    w_gate,
    w_up,
    w_down,
):
    ctx_count = lax.axis_size(CTX)
    near_count = lax.axis_size(NEAR)
    far_count = lax.axis_size(FAR)
    my_block = lax.axis_index(CTX)
    core = lax.axis_index("core")
    block_rows, key_width = latents.shape
    heads = queries.shape[1]
    latent_width, value_width = value_up.shape[1:]
    run = residual.shape[1]
    local_experts, _, hidden_units = w_gate.shape
    half = key_width // 2
    pad_rows = TOK - block_rows
    slots = ctx_count * SLOT
    part = hidden_units // near_count
    sub = part // far_count

    keys = jnp.pad(latents.T, ((0, 0), (0, pad_rows)))
    own_half = lax.dynamic_slice_in_dim(keys, core * half, half, 0)
    keys_a = exchange(jnp.broadcast_to(own_half[None], (ctx_count, half, TOK)), CTX)

    group_range = jnp.arange(ctx_count)
    expert_range = jnp.arange(local_experts)
    member = jnp.zeros((block_rows, ctx_count), jnp.int32)
    shares = jnp.zeros((block_rows, ctx_count, local_experts), F32)
    for group_slot in range(group_ids.shape[1]):
        group_hit = group_ids[:, group_slot, None] == group_range[None, :]
        member = member + group_hit.astype(jnp.int32)
        for expert_slot in range(expert_ids.shape[2]):
            expert_hit = (
                expert_ids[:, group_slot, expert_slot, None] == expert_range[None, :]
            ).astype(F32)
            shares = shares + group_hit.astype(F32)[:, :, None] * expert_hit[
                :, None, :
            ] * route_weights[:, group_slot, expert_slot, None, None].astype(F32)
    ranking = jnp.cumsum(member, axis=0) - 1
    placement = (
        (member[:, :, None] == 1) & (ranking[:, :, None] == jnp.arange(SLOT)[None, None, :])
    ).astype(BF16)
    first_share = run + 16
    slot_shares = jnp.einsum(
        "tge,tgc->gce", shares.astype(BF16), placement, preferred_element_type=F32
    ).astype(BF16)
    slot_shares = jnp.pad(
        slot_shares.reshape(slots, local_experts),
        ((0, 0), (first_share, TOK - first_share - local_experts)),
    )
    places = jnp.pad(placement.reshape(block_rows, slots).T, ((0, 0), (0, pad_rows)))

    place = jnp.stack([my_block, core, lax.axis_index(NEAR)]).astype(jnp.int32)
    pairs = local_experts // 2
    block = (pairs, run, 6 * part)
    w_gate, places, slot_shares = lax.optimization_barrier((w_gate, places, slot_shares))
    packed = call(
        pack,
        [shape(block)] * near_count,
        [SMEM] + [VMEM] * 3,
        [pltpu.VMEM((near_count,) + block, BF16)],
    )(place, w_gate, w_up, w_down.transpose(0, 2, 1))

    def flipped(x, flip):
        return lax.ppermute(x, NEAR, [(a, a ^ flip) for a in range(near_count)])

    moved = [packed[0]] + [flipped(packed[i], i) for i in range(1, 6)]

    wide_q = jnp.pad(queries.transpose(1, 0, 2), ((0, 0), (0, pad_rows), (0, 0)))
    wide_q = wide_q.reshape(heads * TOK, key_width)
    q_low, q_high = wide_q[:, :half], wide_q[:, half:]
    v_low = value_up[:, :half]
    v_high = jnp.pad(value_up[:, half:], ((0, 0), (0, key_width - latent_width), (0, 0)))
    flip = core == 1
    runs = D // run
    out_weights = out_proj.T.reshape(runs // 2, 2, run, heads * value_width)
    operands = (
        jnp.where(flip, q_high, q_low),
        jnp.where(flip, q_low, q_high),
        jnp.where(flip, v_high, v_low),
        jnp.where(flip, v_low, v_high),
        out_weights,
    )
    resid = jnp.pad(residual.T, ((0, 0), (0, pad_rows)))
    gain = norm_gain.astype(F32)[:, None]
    keys_a, operands, moved, places, slot_shares, resid, gain = lax.optimization_barrier(
        (keys_a, operands, moved, places, slot_shares, resid, gain)
    )
    keys_b = lax.ppermute(keys_a, "core", [(0, 1), (1, 0)])
    q_a, q_b, v_a, v_b, out_weights = operands
    mine, theirs = call(
        functools.partial(attend, block_rows, key_width),
        [shape((runs // 2, run, TOK), F32), shape((runs // 2, run, TOK))],
        [SMEM, SMEM] + [VMEM] * 7,
        [
            pltpu.VMEM((2 * TOK, 1), F32),
            pltpu.VMEM((2 * TOK, 1), F32),
            pltpu.VMEM((2 * TOK, half), F32),
            pltpu.VMEM((2 * TOK, half), F32),
        ],
    )(place, block_mask, q_a, q_b, keys_a, keys_b, v_a, v_b, out_weights)
    summed = (mine + lax.ppermute(theirs, "core", [(0, 1), (1, 0)]).astype(F32)).astype(BF16)
    summed, late = lax.optimization_barrier((summed, packed[6:]))
    parts = exchange(summed, ZX)
    moved += [flipped(x, i + 6) for i, x in enumerate(late)]

    hidden, sent = call(make_rows, [shape((run, TOK)), shape((slots, TOK))], [VMEM] * 5)(
        parts,
        resid,
        gain,
        places,
        slot_shares,
    )
    got = exchange(sent.reshape(ctx_count, SLOT, TOK), CTX).reshape(slots, TOK)
    spread, keep, pick_weight = call(
        functools.partial(spread_rows, run + 16, first_share),
        [
            shape((near_count, run + 16, slots)),
            shape((2 * local_experts, slots), F32),
            shape((2, slots), F32),
        ],
        [VMEM],
    )(got)
    spread, moved = lax.optimization_barrier((spread, moved))
    inputs = exchange(spread, NEAR)
    weights_in, weights_back = call(
        functools.partial(unpack, part),
        [
            shape((pairs * 4 * part, near_count * run)),
            shape((near_count, run, local_experts * part)),
        ],
        [VMEM] * near_count,
    )(*moved)
    partial_sums = call(
        functools.partial(project_up, run, sub),
        shape((far_count, 4 * sub + 16, slots)),
        [SMEM] + [VMEM] * 3,
    )(place, inputs, weights_in, keep)
    acts = call(functools.partial(activate, sub), shape((far_count, 2 * sub, slots)), [VMEM] * 2)(
        exchange(partial_sums, FAR), pick_weight
    )
    outputs = call(
        functools.partial(project_down, sub),
        shape((near_count, run, slots)),
        [SMEM] + [VMEM] * 3,
    )(place, exchange(acts, FAR), keep, weights_back)
    returned = call(finish_rows, shape((slots, TOK)), [VMEM])(exchange(outputs, NEAR))
    returned = exchange(returned.reshape(ctx_count, SLOT, TOK), CTX).reshape(slots, TOK)
    out = call(combine, shape((run, block_rows)), [VMEM] * 3)(returned, places, hidden)
    return out.T


def solution(mesh):
    names = ("y", "xh", "za", "zb", "xl", "core")
    fine = Mesh(mesh.devices.reshape(8, 2, 4, 2, 2, 2), names)
    return jax.shard_map(
        on_device,
        mesh=fine,
        in_specs=(
            P(CTX, EXP, None),
            P(CTX, None),
            P(),
            P(EXP, None, None),
            P(EXP, None),
            P(CTX, EXP),
            P(EXP),
            P(CTX, None),
            P(CTX, None, None),
            P(CTX, None, None),
            P(CTX, EXP, None),
            P(CTX, EXP, None),
            P(CTX, None, EXP),
        ),
        out_specs=P(CTX, EXP),
        check_vma=False,
    )
```

```python
import functools

import jax
import jax.numpy as jnp
from jax import lax
from jax.experimental import pallas as pl
from jax.experimental.pallas import tpu as pltpu
from jax.sharding import Mesh
from jax.sharding import PartitionSpec as P

D = 2560
EPSILON = 1e-06
MASKED_SCORE = -1e30
CTX = ("y", "xh")
EXP = ("za", "zb", "xl", "core")
ZX = ("za", "zb", "xl")
NEAR = ("zb", "xl", "core")
FAR = "za"
TOK = 128
SLOT = 32
F32 = jnp.float32
BF16 = jnp.bfloat16
VMEM = pl.BlockSpec(memory_space=pltpu.VMEM)
SMEM = pl.BlockSpec(memory_space=pltpu.SMEM)


def call(body, out_shape, in_specs, scratch=(), flops=0, limit=40):
    many = isinstance(out_shape, (tuple, list))
    return pl.pallas_call(
        body,
        out_shape=out_shape,
        in_specs=in_specs,
        out_specs=[VMEM] * len(out_shape) if many else VMEM,
        scratch_shapes=scratch,
        compiler_params=pltpu.CompilerParams(vmem_limit_bytes=limit << 20),
    )


def shape(dims, dtype=BF16):
    return jax.ShapeDtypeStruct(dims, dtype)


def dot(a, b):
    return jnp.dot(a, b, preferred_element_type=F32)


def dot_nt(a, b):
    return lax.dot_general(a, b, (((1,), (1,)), ((), ())), preferred_element_type=F32)


def spread_keys(keys, out):
    count, half, _ = out.shape
    width, rows = keys.shape
    own = keys[pl.ds(pl.multiple_of(lax.axis_index("core") * half, half), half), :]
    own = jnp.concatenate([own, jnp.zeros((half, TOK - rows), BF16)], axis=1)
    for i in range(count):
        out[i] = own


def route(first, groups, experts, weights, places, shares):
    picks, rows = groups.shape
    slots = places.shape[0]
    count = slots // SLOT
    group = lax.broadcasted_iota(jnp.int32, (count, rows), 0)
    hits = [jnp.where(groups[k : k + 1, :] == group, 1.0, 0.0) for k in range(picks)]
    upto = lax.broadcasted_iota(jnp.int32, (rows, rows), 0)
    upto = jnp.where(upto <= lax.broadcasted_iota(jnp.int32, (rows, rows), 1), 1.0, 0.0)
    rank = dot(sum(hits).astype(BF16), upto.astype(BF16)) - 1.0
    spot = lax.broadcasted_iota(jnp.int32, (count, SLOT, rows), 1).astype(F32)
    here = jnp.where(rank[:, None, :] == spot, 1.0, 0.0)
    lane = lax.broadcasted_iota(jnp.int32, (TOK, rows), 0)
    every = jnp.zeros((slots, rows), F32)
    share = jnp.zeros((slots, TOK), F32)
    for k in range(picks):
        placed = (hits[k][:, None, :] * here).reshape(slots, rows)
        every = every + placed
        table = jnp.zeros((TOK, rows), F32)
        for m in range(experts.shape[1]):
            weight = weights[k, m : m + 1, :].astype(F32)
            table = table + jnp.where(lane == first + experts[k, m : m + 1, :], weight, 0.0)
        share = share + dot_nt(placed.astype(BF16), table.astype(BF16))
    every = jnp.concatenate([every, jnp.zeros((slots, TOK - rows), F32)], axis=1)
    places[...] = every.astype(BF16)
    shares[...] = share.astype(BF16)


def attend(rows, width, mask, qa, qb, ka, kb, va, vb, out, top, total, acc_a, acc_b):
    block = lax.axis_index(CTX)
    inverse_root = width**-0.5
    q_a, q_b = qa[...], qb[...]
    query = lax.broadcasted_iota(jnp.int32, (2 * TOK, TOK), 0) % TOK
    key = lax.broadcasted_iota(jnp.int32, (2 * TOK, TOK), 1)

    def scores_of(b):
        return (dot(q_a, ka[b]) + dot(q_b, kb[b])) * inverse_root

    own = (key <= query) & (key < rows)
    masked = jnp.where(own, scores_of(block), MASKED_SCORE)
    best = jnp.max(masked, axis=1, keepdims=True)
    terms = jnp.where(own, jnp.exp(masked - best), 0.0)
    top[...] = best
    total[...] = jnp.sum(terms, axis=1, keepdims=True)
    acc_a[...] = dot_nt(terms.astype(BF16), ka[block])
    acc_b[...] = dot_nt(terms.astype(BF16), kb[block])

    def step(b, carry):
        @pl.when((mask[block, b] == 1) & (b != block))
        def _():
            inside = key < rows
            masked = jnp.where(inside, scores_of(b), MASKED_SCORE)
            old = top[...]
            best = jnp.maximum(old, jnp.max(masked, axis=1, keepdims=True))
            terms = jnp.where(inside, jnp.exp(masked - best), 0.0)
            shrink = jnp.exp(old - best)
            top[...] = best
            total[...] = total[...] * shrink + jnp.sum(terms, axis=1, keepdims=True)
            rounded = terms.astype(BF16)
            acc_a[...] = acc_a[...] * shrink + dot_nt(rounded, ka[b])
            acc_b[...] = acc_b[...] * shrink + dot_nt(rounded, kb[b])

        return carry

    lax.fori_loop(0, mask.shape[1], step, 0)
    inverse = 1.0 / total[...]
    values = []
    for head in range(2):
        span = slice(head * TOK, (head + 1) * TOK)
        value = jnp.zeros((TOK, TOK), F32)
        for acc, up in ((acc_a, va), (acc_b, vb)):
            latent = acc[span, :] * inverse[span, :]
            high = latent.astype(BF16)
            low = (latent - high.astype(F32)).astype(BF16)
            value = value + dot(high, up[head]) + dot(low, up[head])
        values.append(value.T.astype(BF16))
    out[...] = jnp.concatenate(values, axis=0)


def project_out(mine, theirs, weights_mine, weights_theirs, out):
    runs, run, depth = weights_mine.shape
    total = dot(weights_mine[...].reshape(runs * run, depth), mine[...])
    total = total + dot(weights_theirs[...].reshape(runs * run, depth), theirs[...])
    out[...] = total.reshape(runs, run, TOK).astype(BF16)


def split_pair(value):
    high = value.astype(BF16).astype(F32)
    return high, (value - high).astype(BF16).astype(F32)


def tail_rows(value, count):
    high, low = split_pair(value)
    row = lax.broadcasted_iota(jnp.int32, (count, value.shape[1]), 0)
    return jnp.where(row == 0, high, jnp.where(row == 1, low, 0.0))


def make_rows(parts, residual, gain, places, shares, hidden, sent):
    mixed = jnp.sum(parts[...].astype(F32), axis=0)
    held = (residual[...].astype(F32) + mixed).astype(BF16)
    hidden[...] = held
    wide = held.astype(F32)
    square = jnp.sum(wide * wide, axis=0, keepdims=True)
    run = wide.shape[0]
    rows = jnp.concatenate([wide * gain[...], tail_rows(square, TOK - run)], axis=0).astype(BF16)
    sent[...] = (dot_nt(places[...], rows) + shares[...].astype(F32)).astype(BF16)


def spread_rows(keep_rows, first, got, out, keep, weight):
    turned = got[...].T
    kept = turned[:keep_rows]
    for i in range(out.shape[0]):
        out[i] = kept
    count = keep.shape[0] // 2
    weights = turned[first : first + 16].astype(F32)
    seen = jnp.zeros((1, weights.shape[1]), F32)
    picked = [jnp.zeros((1, weights.shape[1]), F32) for _ in range(2)]
    for expert in range(count):
        row = weights[expert : expert + 1]
        chosen = jnp.where(row > 0.0, 1.0, 0.0)
        for pick in range(2):
            flag = jnp.where(seen == pick, chosen, 0.0)
            keep[2 * expert + pick : 2 * expert + pick + 1, :] = flag
            picked[pick] = picked[pick] + flag * row
        seen = seen + chosen
    weight[...] = jnp.concatenate(picked, axis=0)


def pack(gate, up, down, *refs):
    outs, held = refs[:-1], refs[-1]
    count = held.shape[0]
    part = gate.shape[2] // count
    for pair in range(held.shape[1]):
        for near in range(count):
            span = slice(near * part, (near + 1) * part)
            pieces = []
            for expert in (2 * pair, 2 * pair + 1):
                pieces += [gate[expert, :, span], up[expert, :, span]]
            pieces += [down[2 * pair, :, span], down[2 * pair + 1, :, span]]
            held[near, pair] = jnp.concatenate(pieces, axis=1)
    for flip in range(count):
        outs[flip][...] = held[lax.axis_index(NEAR) ^ flip]


def unpack(part, *refs):
    got, into, back = refs[:-2], refs[-2], refs[-1]
    pairs = got[0].shape[0]
    for pair in range(pairs):
        wide = jnp.concatenate([g[pair, :, : 4 * part] for g in got], axis=0)
        into[pair * 4 * part : (pair + 1) * 4 * part, :] = wide.T
    for flip, g in enumerate(got):
        back[flip] = jnp.concatenate([g[pair, :, 4 * part :] for pair in range(pairs)], axis=1)


def project_up(run, sub, inputs, weights, keep, out):
    count, _, slots = inputs.shape
    features = jnp.concatenate(
        [inputs[lax.axis_index(NEAR) ^ flip, :run, :] for flip in range(count)], axis=0
    )
    ends = inputs[:, run : run + 16, :].astype(F32)
    ends = jnp.sum(ends, axis=0)
    square = ends[0:1] + ends[1:2]
    unit = 2 * sub * out.shape[0]
    sums = [jnp.zeros((unit, slots), F32) for _ in range(2)]
    for expert in range(weights.shape[0] // unit):
        part = dot(weights[expert * unit : (expert + 1) * unit, :], features)
        for pick in range(2):
            sums[pick] = sums[pick] + keep[2 * expert + pick : 2 * expert + pick + 1, :] * part
    tail = tail_rows(square, 16)
    for dest in range(out.shape[0]):
        pieces = []
        for pick in range(2):
            for kind in range(2):
                start = kind * unit // 2 + dest * sub
                pieces.append(sums[pick][start : start + sub])
        out[dest] = jnp.concatenate(pieces + [tail], axis=0).astype(BF16)


def activate(sub, got, weight, out):
    total = jnp.sum(got[...].astype(F32), axis=0)
    square = total[4 * sub : 4 * sub + 1] + total[4 * sub + 1 : 4 * sub + 2]
    scale = lax.rsqrt(square / D + EPSILON)
    pieces = []
    for pick in range(2):
        gate = total[2 * pick * sub : (2 * pick + 1) * sub] * scale
        up = total[(2 * pick + 1) * sub : (2 * pick + 2) * sub] * scale
        act = gate / (1.0 + jnp.exp(-gate)) * up
        pieces.append(act * weight[pick : pick + 1, :])
    rounded = jnp.concatenate(pieces, axis=0).astype(BF16)
    for i in range(out.shape[0]):
        out[i] = rounded


def project_down(sub, acts, keep, weights, out):
    count, _, slots = acts.shape
    wide = acts[...].astype(F32)
    first = wide[:, :sub].reshape(count * sub, slots)
    second = wide[:, sub:].reshape(count * sub, slots)
    picked = []
    for expert in range(keep.shape[0] // 2):
        picked.append(
            (
                keep[2 * expert : 2 * expert + 1, :] * first
                + keep[2 * expert + 1 : 2 * expert + 2, :] * second
            ).astype(BF16)
        )
    stacked = jnp.concatenate(picked, axis=0)
    for flip in range(weights.shape[0]):
        out[lax.axis_index(NEAR) ^ flip] = dot(weights[flip], stacked).astype(BF16)


def finish_rows(got, out):
    total = jnp.sum(got[...].astype(F32), axis=0).astype(BF16)
    run, slots = total.shape
    padded = jnp.concatenate([total, jnp.zeros((TOK - run, slots), BF16)], axis=0)
    out[...] = padded.T


def combine(got, places, hidden, out):
    run, rows = out.shape
    turned = got[...].T[:run]
    added = dot(turned, places[...])
    out[...] = (hidden[...].astype(F32) + added)[:, :rows].astype(BF16)


def exchange(x, axes):
    return lax.all_to_all(x, axes, split_axis=0, concat_axis=0, tiled=True)


def on_device(
    queries,
    latents,
    block_mask,
    value_up,
    out_proj,
    residual,
    norm_gain,
    group_ids,
    expert_ids,
    route_weights,
    w_gate,
    w_up,
    w_down,
):
    ctx_count = lax.axis_size(CTX)
    near_count = lax.axis_size(NEAR)
    far_count = lax.axis_size(FAR)
    core = lax.axis_index("core")
    block_rows, key_width = latents.shape
    heads = queries.shape[1]
    latent_width, value_width = value_up.shape[1:]
    run = residual.shape[1]
    local_experts, _, hidden_units = w_gate.shape
    half = key_width // 2
    pad_rows = TOK - block_rows
    slots = ctx_count * SLOT
    part = hidden_units // near_count
    sub = part // far_count

    spread = call(spread_keys, shape((ctx_count, half, TOK)), [VMEM])(latents.T)
    keys_a = exchange(spread, CTX)

    first_share = run + 16
    places, slot_shares = call(
        functools.partial(route, first_share), [shape((slots, TOK))] * 2, [VMEM] * 3
    )(group_ids.T, expert_ids.transpose(1, 2, 0), route_weights.transpose(1, 2, 0))

    pairs = local_experts // 2
    block = (pairs, run, 6 * part)
    w_gate, places, slot_shares = lax.optimization_barrier((w_gate, places, slot_shares))
    packed = call(
        pack,
        [shape(block)] * near_count,
        [VMEM] * 3,
        [pltpu.VMEM((near_count,) + block, BF16)],
    )(w_gate, w_up, w_down.transpose(0, 2, 1))

    def flipped(x, flip):
        return lax.ppermute(x, NEAR, [(a, a ^ flip) for a in range(near_count)])

    early = {i: flipped(packed[i], i) for i in (2, 3, 4, 5, 1)}
    moved = [packed[0]] + [early[i] for i in range(1, 6)]

    wide_q = jnp.pad(queries.transpose(1, 0, 2), ((0, 0), (0, pad_rows), (0, 0)))
    wide_q = wide_q.reshape(heads * TOK, key_width)
    q_low, q_high = wide_q[:, :half], wide_q[:, half:]
    v_low = value_up[:, :half]
    v_high = jnp.pad(value_up[:, half:], ((0, 0), (0, key_width - latent_width), (0, 0)))
    flip = core == 1
    runs = D // run
    out_weights = out_proj.T.reshape(runs // 2, 2, run, heads * value_width)
    out_mine = jnp.where(flip, out_weights[:, 1], out_weights[:, 0])
    out_theirs = jnp.where(flip, out_weights[:, 0], out_weights[:, 1])
    out_theirs = lax.ppermute(out_theirs, "core", [(0, 1), (1, 0)])
    operands = (
        jnp.where(flip, q_high, q_low),
        jnp.where(flip, q_low, q_high),
        jnp.where(flip, v_high, v_low),
        jnp.where(flip, v_low, v_high),
        out_mine,
        out_theirs,
    )
    resid = jnp.pad(residual.T, ((0, 0), (0, pad_rows)))
    gain = norm_gain.astype(F32)[:, None]
    keys_a, operands, moved, places, slot_shares, resid, gain = lax.optimization_barrier(
        (keys_a, operands, moved, places, slot_shares, resid, gain)
    )
    keys_b = lax.ppermute(keys_a, "core", [(0, 1), (1, 0)])
    q_a, q_b, v_a, v_b, out_mine, out_theirs = operands
    values = call(
        functools.partial(attend, block_rows, key_width),
        shape((heads * value_width, TOK)),
        [SMEM] + [VMEM] * 6,
        [
            pltpu.VMEM((2 * TOK, 1), F32),
            pltpu.VMEM((2 * TOK, 1), F32),
            pltpu.VMEM((2 * TOK, half), F32),
            pltpu.VMEM((2 * TOK, half), F32),
        ],
    )(block_mask, q_a, q_b, keys_a, keys_b, v_a, v_b)
    other_values = lax.ppermute(values, "core", [(0, 1), (1, 0)])
    summed = call(project_out, shape((runs // 2, run, TOK)), [VMEM] * 4)(
        values, other_values, out_mine, out_theirs
    )
    summed, late = lax.optimization_barrier((summed, packed[6:]))
    parts = exchange(summed, ZX)
    moved += [flipped(x, i + 6) for i, x in enumerate(late)]

    hidden, sent = call(make_rows, [shape((run, TOK)), shape((slots, TOK))], [VMEM] * 5)(
        parts,
        resid,
        gain,
        places,
        slot_shares,
    )
    got = exchange(sent.reshape(ctx_count, SLOT, TOK), CTX).reshape(slots, TOK)
    spread, keep, pick_weight = call(
        functools.partial(spread_rows, run + 16, first_share),
        [
            shape((near_count, run + 16, slots)),
            shape((2 * local_experts, slots), F32),
            shape((2, slots), F32),
        ],
        [VMEM],
    )(got)
    spread, moved = lax.optimization_barrier((spread, moved))
    inputs = exchange(spread, NEAR)
    weights_in, weights_back = call(
        functools.partial(unpack, part),
        [
            shape((pairs * 4 * part, near_count * run)),
            shape((near_count, run, local_experts * part)),
        ],
        [VMEM] * near_count,
    )(*moved)
    partial_sums = call(
        functools.partial(project_up, run, sub),
        shape((far_count, 4 * sub + 16, slots)),
        [VMEM] * 3,
    )(inputs, weights_in, keep)
    acts = call(functools.partial(activate, sub), shape((far_count, 2 * sub, slots)), [VMEM] * 2)(
        exchange(partial_sums, FAR), pick_weight
    )
    outputs = call(
        functools.partial(project_down, sub),
        shape((near_count, run, slots)),
        [VMEM] * 3,
    )(exchange(acts, FAR), keep, weights_back)
    returned = call(finish_rows, shape((slots, TOK)), [VMEM])(exchange(outputs, NEAR))
    returned = exchange(returned.reshape(ctx_count, SLOT, TOK), CTX).reshape(slots, TOK)
    out = call(combine, shape((run, block_rows)), [VMEM] * 3)(returned, places, hidden)
    return out.T


def solution(mesh):
    names = ("y", "xh", "za", "zb", "xl", "core")
    fine = Mesh(mesh.devices.reshape(8, 2, 4, 2, 2, 2), names)
    return jax.shard_map(
        on_device,
        mesh=fine,
        in_specs=(
            P(CTX, EXP, None),
            P(CTX, None),
            P(),
            P(EXP, None, None),
            P(EXP, None),
            P(CTX, EXP),
            P(EXP),
            P(CTX, None),
            P(CTX, None, None),
            P(CTX, None, None),
            P(CTX, EXP, None),
            P(CTX, EXP, None),
            P(CTX, None, EXP),
        ),
        out_specs=P(CTX, EXP),
        check_vma=False,
    )
```

```python
import functools

import jax
import jax.numpy as jnp
from jax import lax
from jax.experimental import pallas as pl
from jax.experimental.pallas import tpu as pltpu
from jax.sharding import Mesh
from jax.sharding import PartitionSpec as P

D = 2560
EPSILON = 1e-06
MASKED_SCORE = -1e30
CTX = ("y", "xh")
EXP = ("za", "zb", "xl", "core")
ZX = ("za", "zb", "xl")
NEAR = ("zb", "xl", "core")
FAR = "za"
TOK = 128
SLOT = 32
F32 = jnp.float32
BF16 = jnp.bfloat16
VMEM = pl.BlockSpec(memory_space=pltpu.VMEM)
SMEM = pl.BlockSpec(memory_space=pltpu.SMEM)


def call(body, out_shape, in_specs, scratch=(), flops=0, limit=40):
    many = isinstance(out_shape, (tuple, list))
    return pl.pallas_call(
        body,
        out_shape=out_shape,
        in_specs=in_specs,
        out_specs=[VMEM] * len(out_shape) if many else VMEM,
        scratch_shapes=scratch,
        compiler_params=pltpu.CompilerParams(vmem_limit_bytes=limit << 20),
    )


def shape(dims, dtype=BF16):
    return jax.ShapeDtypeStruct(dims, dtype)


def dot(a, b):
    return jnp.dot(a, b, preferred_element_type=F32)


def dot_nt(a, b):
    return lax.dot_general(a, b, (((1,), (1,)), ((), ())), preferred_element_type=F32)


def spread_keys(keys, out):
    count, half, _ = out.shape
    width, rows = keys.shape
    own = keys[pl.ds(pl.multiple_of(lax.axis_index("core") * half, half), half), :]
    own = jnp.concatenate([own, jnp.zeros((half, TOK - rows), BF16)], axis=1)
    for i in range(count):
        out[i] = own


def route(first, groups, experts, weights, places, shares):
    picks, rows = groups.shape
    slots = places.shape[0]
    count = slots // SLOT
    group = lax.broadcasted_iota(jnp.int32, (count, rows), 0)
    hits = [jnp.where(groups[k : k + 1, :] == group, 1.0, 0.0) for k in range(picks)]
    upto = lax.broadcasted_iota(jnp.int32, (rows, rows), 0)
    upto = jnp.where(upto <= lax.broadcasted_iota(jnp.int32, (rows, rows), 1), 1.0, 0.0)
    rank = dot(sum(hits).astype(BF16), upto.astype(BF16)) - 1.0
    spot = lax.broadcasted_iota(jnp.int32, (count, SLOT, rows), 1).astype(F32)
    here = jnp.where(rank[:, None, :] == spot, 1.0, 0.0)
    lane = lax.broadcasted_iota(jnp.int32, (TOK, rows), 0)
    every = jnp.zeros((slots, rows), F32)
    share = jnp.zeros((slots, TOK), F32)
    for k in range(picks):
        placed = (hits[k][:, None, :] * here).reshape(slots, rows)
        every = every + placed
        table = jnp.zeros((TOK, rows), F32)
        for m in range(experts.shape[1]):
            weight = weights[k, m : m + 1, :].astype(F32)
            table = table + jnp.where(lane == first + experts[k, m : m + 1, :], weight, 0.0)
        share = share + dot_nt(placed.astype(BF16), table.astype(BF16))
    every = jnp.concatenate([every, jnp.zeros((slots, TOK - rows), F32)], axis=1)
    places[...] = every.astype(BF16)
    shares[...] = share.astype(BF16)


def attend(rows, width, mask, qa, qb, ka, kb, va, vb, out, top, total, acc_a, acc_b):
    block = lax.axis_index(CTX)
    inverse_root = width**-0.5
    q_a, q_b = qa[...], qb[...]
    query = lax.broadcasted_iota(jnp.int32, (2 * TOK, TOK), 0) % TOK
    key = lax.broadcasted_iota(jnp.int32, (2 * TOK, TOK), 1)

    def scores_of(b):
        return (dot(q_a, ka[b]) + dot(q_b, kb[b])) * inverse_root

    own = (key <= query) & (key < rows)
    masked = jnp.where(own, scores_of(block), MASKED_SCORE)
    best = jnp.max(masked, axis=1, keepdims=True)
    terms = jnp.where(own, jnp.exp(masked - best), 0.0)
    top[...] = best
    total[...] = jnp.sum(terms, axis=1, keepdims=True)
    acc_a[...] = dot_nt(terms.astype(BF16), ka[block])
    acc_b[...] = dot_nt(terms.astype(BF16), kb[block])

    def step(b, carry):
        @pl.when((mask[block, b] == 1) & (b != block))
        def _():
            inside = key < rows
            masked = jnp.where(inside, scores_of(b), MASKED_SCORE)
            old = top[...]
            best = jnp.maximum(old, jnp.max(masked, axis=1, keepdims=True))
            terms = jnp.where(inside, jnp.exp(masked - best), 0.0)
            shrink = jnp.exp(old - best)
            top[...] = best
            total[...] = total[...] * shrink + jnp.sum(terms, axis=1, keepdims=True)
            rounded = terms.astype(BF16)
            acc_a[...] = acc_a[...] * shrink + dot_nt(rounded, ka[b])
            acc_b[...] = acc_b[...] * shrink + dot_nt(rounded, kb[b])

        return carry

    lax.fori_loop(0, mask.shape[1], step, 0)
    inverse = 1.0 / total[...]
    values = []
    for head in range(2):
        span = slice(head * TOK, (head + 1) * TOK)
        value = jnp.zeros((TOK, TOK), F32)
        for acc, up in ((acc_a, va), (acc_b, vb)):
            latent = acc[span, :] * inverse[span, :]
            high = latent.astype(BF16)
            low = (latent - high.astype(F32)).astype(BF16)
            value = value + dot(high, up[head]) + dot(low, up[head])
        values.append(value.T.astype(BF16))
    out[...] = jnp.concatenate(values, axis=0)


def project_out(mine, theirs, weights_mine, weights_theirs, out):
    runs, run, depth = weights_mine.shape
    total = dot(weights_mine[...].reshape(runs * run, depth), mine[...])
    total = total + dot(weights_theirs[...].reshape(runs * run, depth), theirs[...])
    out[...] = total.reshape(runs, run, TOK).astype(BF16)


def split_pair(value):
    high = value.astype(BF16).astype(F32)
    return high, (value - high).astype(BF16).astype(F32)


def tail_rows(value, count):
    high, low = split_pair(value)
    row = lax.broadcasted_iota(jnp.int32, (count, value.shape[1]), 0)
    return jnp.where(row == 0, high, jnp.where(row == 1, low, 0.0))


def make_rows(parts, residual, gain, places, shares, hidden, sent):
    mixed = jnp.sum(parts[...].astype(F32), axis=0)
    held = (residual[...].astype(F32) + mixed).astype(BF16)
    hidden[...] = held
    wide = held.astype(F32)
    square = jnp.sum(wide * wide, axis=0, keepdims=True)
    run = wide.shape[0]
    rows = jnp.concatenate([wide * gain[...], tail_rows(square, TOK - run)], axis=0).astype(BF16)
    sent[...] = (dot_nt(places[...], rows) + shares[...].astype(F32)).astype(BF16)


def spread_rows(keep_rows, first, got, out, keep, weight):
    turned = got[...].T
    kept = turned[:keep_rows]
    for i in range(out.shape[0]):
        out[i] = kept
    count = keep.shape[0] // 2
    weights = turned[first : first + 16].astype(F32)
    seen = jnp.zeros((1, weights.shape[1]), F32)
    picked = [jnp.zeros((1, weights.shape[1]), F32) for _ in range(2)]
    for expert in range(count):
        row = weights[expert : expert + 1]
        chosen = jnp.where(row > 0.0, 1.0, 0.0)
        for pick in range(2):
            flag = jnp.where(seen == pick, chosen, 0.0)
            keep[2 * expert + pick : 2 * expert + pick + 1, :] = flag
            picked[pick] = picked[pick] + flag * row
        seen = seen + chosen
    weight[...] = jnp.concatenate(picked, axis=0)


def pack(gate, up, down, *refs):
    outs, held = refs[:-1], refs[-1]
    count = held.shape[0]
    part = gate.shape[2] // count
    for pair in range(held.shape[1]):
        for near in range(count):
            span = slice(near * part, (near + 1) * part)
            pieces = []
            for expert in (2 * pair, 2 * pair + 1):
                pieces += [gate[expert, :, span], up[expert, :, span]]
            pieces += [down[2 * pair, :, span], down[2 * pair + 1, :, span]]
            held[near, pair] = jnp.concatenate(pieces, axis=1)
    for flip in range(count):
        outs[flip][...] = held[lax.axis_index(NEAR) ^ flip]


def unpack(part, *refs):
    got, into, back = refs[:-2], refs[-2], refs[-1]
    pairs = got[0].shape[0]
    for pair in range(pairs):
        wide = jnp.concatenate([g[pair, :, : 4 * part] for g in got], axis=0)
        into[pair * 4 * part : (pair + 1) * 4 * part, :] = wide.T
    for flip, g in enumerate(got):
        back[flip] = jnp.concatenate([g[pair, :, 4 * part :] for pair in range(pairs)], axis=1)


def project_up(run, sub, inputs, weights, keep, out):
    count, _, slots = inputs.shape
    features = jnp.concatenate(
        [inputs[lax.axis_index(NEAR) ^ flip, :run, :] for flip in range(count)], axis=0
    )
    ends = jnp.sum(inputs[...].astype(F32)[:, run:], axis=0)
    square = ends[0:1] + ends[1:2]
    unit = 2 * sub * out.shape[0]
    sums = [jnp.zeros((unit, slots), F32) for _ in range(2)]
    for expert in range(weights.shape[0] // unit):
        part = dot(weights[expert * unit : (expert + 1) * unit, :], features)
        for pick in range(2):
            sums[pick] = sums[pick] + keep[2 * expert + pick : 2 * expert + pick + 1, :] * part
    tail = tail_rows(square, 8)
    for dest in range(out.shape[0]):
        pieces = []
        for pick in range(2):
            for kind in range(2):
                start = kind * unit // 2 + dest * sub
                pieces.append(sums[pick][start : start + sub])
        out[dest] = jnp.concatenate(pieces + [tail], axis=0).astype(BF16)


def activate(sub, got, weight, out):
    total = jnp.sum(got[...].astype(F32), axis=0)
    square = total[4 * sub : 4 * sub + 1] + total[4 * sub + 1 : 4 * sub + 2]
    scale = lax.rsqrt(square / D + EPSILON)
    pieces = []
    for pick in range(2):
        gate = total[2 * pick * sub : (2 * pick + 1) * sub] * scale
        up = total[(2 * pick + 1) * sub : (2 * pick + 2) * sub] * scale
        act = gate / (1.0 + jnp.exp(-gate)) * up
        pieces.append(act * weight[pick : pick + 1, :])
    rounded = jnp.concatenate(pieces, axis=0).astype(BF16)
    for i in range(out.shape[0]):
        out[i] = rounded


def project_down(sub, acts, keep, weights, out):
    count, _, slots = acts.shape
    wide = acts[...].astype(F32)
    first = wide[:, :sub].reshape(count * sub, slots)
    second = wide[:, sub:].reshape(count * sub, slots)
    picked = []
    for expert in range(keep.shape[0] // 2):
        picked.append(
            (
                keep[2 * expert : 2 * expert + 1, :] * first
                + keep[2 * expert + 1 : 2 * expert + 2, :] * second
            ).astype(BF16)
        )
    stacked = jnp.concatenate(picked, axis=0)
    for flip in range(weights.shape[0]):
        out[lax.axis_index(NEAR) ^ flip] = dot(weights[flip], stacked).astype(BF16)


def finish_rows(got, out):
    total = jnp.sum(got[...].astype(F32), axis=0).astype(BF16)
    run, slots = total.shape
    padded = jnp.concatenate([total, jnp.zeros((TOK - run, slots), BF16)], axis=0)
    out[...] = padded.T


def combine(got, places, hidden, out):
    run, rows = out.shape
    turned = got[...].T[:run]
    added = dot(turned, places[...])
    out[...] = (hidden[...].astype(F32) + added)[:, :rows].astype(BF16)


def exchange(x, axes):
    return lax.all_to_all(x, axes, split_axis=0, concat_axis=0, tiled=True)


def on_device(
    queries,
    latents,
    block_mask,
    value_up,
    out_proj,
    residual,
    norm_gain,
    group_ids,
    expert_ids,
    route_weights,
    w_gate,
    w_up,
    w_down,
):
    ctx_count = lax.axis_size(CTX)
    near_count = lax.axis_size(NEAR)
    far_count = lax.axis_size(FAR)
    core = lax.axis_index("core")
    block_rows, key_width = latents.shape
    heads = queries.shape[1]
    latent_width, value_width = value_up.shape[1:]
    run = residual.shape[1]
    local_experts, _, hidden_units = w_gate.shape
    half = key_width // 2
    pad_rows = TOK - block_rows
    slots = ctx_count * SLOT
    part = hidden_units // near_count
    sub = part // far_count

    spread = call(spread_keys, shape((ctx_count, half, TOK)), [VMEM])(latents.T)
    keys_a = exchange(spread, CTX)

    first_share = run + 16
    places, slot_shares = call(
        functools.partial(route, first_share), [shape((slots, TOK))] * 2, [VMEM] * 3
    )(group_ids.T, expert_ids.transpose(1, 2, 0), route_weights.transpose(1, 2, 0))

    pairs = local_experts // 2
    block = (pairs, run, 6 * part)
    w_gate, places, slot_shares = lax.optimization_barrier((w_gate, places, slot_shares))
    packed = call(
        pack,
        [shape(block)] * near_count,
        [VMEM] * 3,
        [pltpu.VMEM((near_count,) + block, BF16)],
    )(w_gate, w_up, w_down.transpose(0, 2, 1))

    def flipped(x, flip):
        return lax.ppermute(x, NEAR, [(a, a ^ flip) for a in range(near_count)])

    moved = {i: flipped(packed[i], i) for i in (1, 2, 4, 5)}

    wide_q = jnp.pad(queries.transpose(1, 0, 2), ((0, 0), (0, pad_rows), (0, 0)))
    wide_q = wide_q.reshape(heads * TOK, key_width)
    q_low, q_high = wide_q[:, :half], wide_q[:, half:]
    v_low = value_up[:, :half]
    v_high = jnp.pad(value_up[:, half:], ((0, 0), (0, key_width - latent_width), (0, 0)))
    flip = core == 1
    runs = D // run
    out_weights = out_proj.T.reshape(runs // 2, 2, run, heads * value_width)
    out_mine = jnp.where(flip, out_weights[:, 1], out_weights[:, 0])
    out_theirs = jnp.where(flip, out_weights[:, 0], out_weights[:, 1])
    out_theirs = lax.ppermute(out_theirs, "core", [(0, 1), (1, 0)])
    operands = (
        jnp.where(flip, q_high, q_low),
        jnp.where(flip, q_low, q_high),
        jnp.where(flip, v_high, v_low),
        jnp.where(flip, v_low, v_high),
        out_mine,
        out_theirs,
    )
    resid = jnp.pad(residual.T, ((0, 0), (0, pad_rows)))
    gain = norm_gain.astype(F32)[:, None]
    keys_a, operands, moved, places, slot_shares, resid, gain = lax.optimization_barrier(
        (keys_a, operands, moved, places, slot_shares, resid, gain)
    )
    keys_b = lax.ppermute(keys_a, "core", [(0, 1), (1, 0)])
    q_a, q_b, v_a, v_b, out_mine, out_theirs = operands
    values = call(
        functools.partial(attend, block_rows, key_width),
        shape((heads * value_width, TOK)),
        [SMEM] + [VMEM] * 6,
        [
            pltpu.VMEM((2 * TOK, 1), F32),
            pltpu.VMEM((2 * TOK, 1), F32),
            pltpu.VMEM((2 * TOK, half), F32),
            pltpu.VMEM((2 * TOK, half), F32),
        ],
    )(block_mask, q_a, q_b, keys_a, keys_b, v_a, v_b)
    other_values = lax.ppermute(values, "core", [(0, 1), (1, 0)])
    summed = call(project_out, shape((runs // 2, run, TOK)), [VMEM] * 4)(
        values, other_values, out_mine, out_theirs
    )
    summed, *late = lax.optimization_barrier((summed, packed[3], packed[6], packed[7]))
    parts = exchange(summed, ZX)
    for flip, x in zip((3, 6, 7), late):
        moved[flip] = flipped(x, flip)
    moved = [packed[0]] + [moved[flip] for flip in range(1, near_count)]

    hidden, sent = call(make_rows, [shape((run, TOK)), shape((slots, TOK))], [VMEM] * 5)(
        parts,
        resid,
        gain,
        places,
        slot_shares,
    )
    got = exchange(sent.reshape(ctx_count, SLOT, TOK), CTX).reshape(slots, TOK)
    spread, keep, pick_weight = call(
        functools.partial(spread_rows, run + 8, first_share),
        [
            shape((near_count, run + 8, slots)),
            shape((2 * local_experts, slots), F32),
            shape((2, slots), F32),
        ],
        [VMEM],
    )(got)
    spread, moved = lax.optimization_barrier((spread, moved))
    inputs = exchange(spread, NEAR)
    weights_in, weights_back = call(
        functools.partial(unpack, part),
        [
            shape((pairs * 4 * part, near_count * run)),
            shape((near_count, run, local_experts * part)),
        ],
        [VMEM] * near_count,
    )(*moved)
    partial_sums = call(
        functools.partial(project_up, run, sub),
        shape((far_count, 4 * sub + 8, slots)),
        [VMEM] * 3,
    )(inputs, weights_in, keep)
    acts = call(functools.partial(activate, sub), shape((far_count, 2 * sub, slots)), [VMEM] * 2)(
        exchange(partial_sums, FAR), pick_weight
    )
    outputs = call(
        functools.partial(project_down, sub),
        shape((near_count, run, slots)),
        [VMEM] * 3,
    )(exchange(acts, FAR), keep, weights_back)
    returned = call(finish_rows, shape((slots, TOK)), [VMEM])(exchange(outputs, NEAR))
    returned = exchange(returned.reshape(ctx_count, SLOT, TOK), CTX).reshape(slots, TOK)
    out = call(combine, shape((run, block_rows)), [VMEM] * 3)(returned, places, hidden)
    return out.T


def solution(mesh):
    names = ("y", "xh", "za", "zb", "xl", "core")
    fine = Mesh(mesh.devices.reshape(8, 2, 4, 2, 2, 2), names)
    return jax.shard_map(
        on_device,
        mesh=fine,
        in_specs=(
            P(CTX, EXP, None),
            P(CTX, None),
            P(),
            P(EXP, None, None),
            P(EXP, None),
            P(CTX, EXP),
            P(EXP),
            P(CTX, None),
            P(CTX, None, None),
            P(CTX, None, None),
            P(CTX, EXP, None),
            P(CTX, EXP, None),
            P(CTX, None, EXP),
        ),
        out_specs=P(CTX, EXP),
        check_vma=False,
    )
```

```python
import functools

import jax
import jax.numpy as jnp
from jax import lax
from jax.experimental import pallas as pl
from jax.experimental.pallas import tpu as pltpu
from jax.sharding import Mesh
from jax.sharding import PartitionSpec as P

D = 2560
EPSILON = 1e-06
MASKED_SCORE = -1e30
CTX = ("y", "xh")
EXP = ("za", "zb", "xl", "core")
ZX = ("za", "zb", "xl")
XC = ("xl", "core")
NEAR = ("zb", "xl", "core")
FAR = "za"
TOK = 128
SLOT = 32
FEW = 5
F32 = jnp.float32
BF16 = jnp.bfloat16
VMEM = pl.BlockSpec(memory_space=pltpu.VMEM)
SMEM = pl.BlockSpec(memory_space=pltpu.SMEM)


def call(body, out_shape, in_specs, scratch=(), flops=0, limit=40):
    many = isinstance(out_shape, (tuple, list))
    return pl.pallas_call(
        body,
        out_shape=out_shape,
        in_specs=in_specs,
        out_specs=[VMEM] * len(out_shape) if many else VMEM,
        scratch_shapes=scratch,
        compiler_params=pltpu.CompilerParams(vmem_limit_bytes=limit << 20),
    )


def shape(dims, dtype=BF16):
    return jax.ShapeDtypeStruct(dims, dtype)


def dot(a, b):
    return jnp.dot(a, b, preferred_element_type=F32)


def dot_nt(a, b):
    return lax.dot_general(a, b, (((1,), (1,)), ((), ())), preferred_element_type=F32)


def spread_keys(keys, out):
    count, part, _ = out.shape
    rows = keys.shape[1]
    own = keys[pl.ds(pl.multiple_of(lax.axis_index(XC) * part, part), part), :]
    own = jnp.concatenate([own, jnp.zeros((part, TOK - rows), BF16)], axis=1)
    for i in range(count):
        out[i] = own


def pick_keys(mask, pieces, out):
    block = lax.axis_index(CTX)
    out[...] = jnp.zeros_like(out)

    def step(b, filled):
        wanted = (mask[block, b] == 1) & (b != block)

        @pl.when(wanted)
        def _():
            out[filled] = pieces[b]

        return filled + wanted.astype(jnp.int32)

    lax.fori_loop(0, mask.shape[1], step, 0)


def prepare(queries, weights, wide, mine, theirs, turned):
    heads, width, rows = queries.shape
    for head in range(heads):
        lanes = jnp.concatenate([queries[head], jnp.zeros((width, TOK - rows), BF16)], axis=1)
        wide[head * TOK : (head + 1) * TOK, :] = lanes.T
    for i in range(weights.shape[1] // TOK):
        turned[i * TOK : (i + 1) * TOK, :] = weights[:, i * TOK : (i + 1) * TOK].T
    core = lax.axis_index("core")
    runs, run, _ = mine.shape
    for i in range(runs):
        for out, at in ((mine, 2 * i + core), (theirs, 2 * i + 1 - core)):
            out[i] = turned[pl.ds(pl.multiple_of(at * run, run), run), :]


def route(first, groups, experts, weights, places, shares):
    picks, rows = groups.shape
    slots = places.shape[0]
    count = slots // SLOT
    group = lax.broadcasted_iota(jnp.int32, (count, rows), 0)
    hits = [jnp.where(groups[k : k + 1, :] == group, 1.0, 0.0) for k in range(picks)]
    upto = lax.broadcasted_iota(jnp.int32, (rows, rows), 0)
    upto = jnp.where(upto <= lax.broadcasted_iota(jnp.int32, (rows, rows), 1), 1.0, 0.0)
    rank = dot(sum(hits).astype(BF16), upto.astype(BF16)) - 1.0
    spot = lax.broadcasted_iota(jnp.int32, (count, SLOT, rows), 1).astype(F32)
    here = jnp.where(rank[:, None, :] == spot, 1.0, 0.0)
    lane = lax.broadcasted_iota(jnp.int32, (TOK, rows), 0)
    every = jnp.zeros((slots, rows), F32)
    share = jnp.zeros((slots, TOK), F32)
    for k in range(picks):
        placed = (hits[k][:, None, :] * here).reshape(slots, rows)
        every = every + placed
        table = jnp.zeros((TOK, rows), F32)
        for m in range(experts.shape[1]):
            weight = weights[k, m : m + 1, :].astype(F32)
            table = table + jnp.where(lane == first + experts[k, m : m + 1, :], weight, 0.0)
        share = share + dot_nt(placed.astype(BF16), table.astype(BF16))
    every = jnp.concatenate([every, jnp.zeros((slots, TOK - rows), F32)], axis=1)
    places[...] = every.astype(BF16)
    shares[...] = share.astype(BF16)


def attend(mask, queries, own, up, *refs):
    pieces, (out, held, top, total, acc) = refs[:4], refs[4:]
    block, column = lax.axis_index(CTX), lax.axis_index(XC)
    width, rows = own.shape
    part = pieces[0].shape[1]
    inverse_root = width**-0.5
    wide = queries[...]
    query = lax.broadcasted_iota(jnp.int32, (2 * TOK, TOK), 0) % TOK
    key = lax.broadcasted_iota(jnp.int32, (2 * TOK, TOK), 1)

    keys = jnp.concatenate([own[...], jnp.zeros((width, TOK - rows), BF16)], axis=1)
    inside = (key <= query) & (key < rows)
    masked = jnp.where(inside, dot(wide, keys) * inverse_root, MASKED_SCORE)
    best = jnp.max(masked, axis=1, keepdims=True)
    terms = jnp.where(inside, jnp.exp(masked - best), 0.0)
    top[...] = best
    total[...] = jnp.sum(terms, axis=1, keepdims=True)
    acc[...] = dot_nt(terms.astype(BF16), keys)

    def count(b, filled):
        return filled + ((mask[block, b] == 1) & (b != block)).astype(jnp.int32)

    def step(slot, carry):
        for flip, piece in enumerate(pieces):
            start = pl.multiple_of((column ^ flip) * part, part)
            held[pl.ds(start, part), :] = piece[slot]
        inside = key < rows
        masked = jnp.where(inside, dot(wide, held[...]) * inverse_root, MASKED_SCORE)
        old = top[...]
        best = jnp.maximum(old, jnp.max(masked, axis=1, keepdims=True))
        terms = jnp.where(inside, jnp.exp(masked - best), 0.0)
        shrink = jnp.exp(old - best)
        top[...] = best
        total[...] = total[...] * shrink + jnp.sum(terms, axis=1, keepdims=True)
        acc[...] = acc[...] * shrink + dot_nt(terms.astype(BF16), held[...])
        return carry

    lax.fori_loop(0, lax.fori_loop(0, mask.shape[1], count, 0), step, 0)
    inverse = 1.0 / total[...]
    values = []
    for head in range(up.shape[0]):
        span = slice(head * TOK, (head + 1) * TOK)
        latent = acc[span, : up.shape[1]] * inverse[span, :]
        high = latent.astype(BF16)
        low = (latent - high.astype(F32)).astype(BF16)
        values.append((dot(high, up[head]) + dot(low, up[head])).T.astype(BF16))
    out[...] = jnp.concatenate(values, axis=0)


def project_out(mine, theirs, weights_mine, weights_theirs, out):
    runs, run, depth = weights_mine.shape
    total = dot(weights_mine[...].reshape(runs * run, depth), mine[...])
    total = total + dot(weights_theirs[...].reshape(runs * run, depth), theirs[...])
    out[...] = total.reshape(runs, run, TOK).astype(BF16)


def split_pair(value):
    high = value.astype(BF16).astype(F32)
    return high, (value - high).astype(BF16).astype(F32)


def tail_rows(value, count):
    high, low = split_pair(value)
    row = lax.broadcasted_iota(jnp.int32, (count, value.shape[1]), 0)
    return jnp.where(row == 0, high, jnp.where(row == 1, low, 0.0))


def make_rows(parts, residual, gain, places, shares, hidden, sent):
    mixed = jnp.sum(parts[...].astype(F32), axis=0)
    held = (residual[...].astype(F32) + mixed).astype(BF16)
    hidden[...] = held
    wide = held.astype(F32)
    square = jnp.sum(wide * wide, axis=0, keepdims=True)
    run = wide.shape[0]
    rows = jnp.concatenate([wide * gain[...], tail_rows(square, TOK - run)], axis=0).astype(BF16)
    sent[...] = (dot_nt(places[...], rows) + shares[...].astype(F32)).astype(BF16)


def spread_rows(keep_rows, first, got, out, keep, weight):
    turned = got[...].T
    kept = turned[:keep_rows]
    for i in range(out.shape[0]):
        out[i] = kept
    count = keep.shape[0] // 2
    weights = turned[first : first + 16].astype(F32)
    seen = jnp.zeros((1, weights.shape[1]), F32)
    picked = [jnp.zeros((1, weights.shape[1]), F32) for _ in range(2)]
    for expert in range(count):
        row = weights[expert : expert + 1]
        chosen = jnp.where(row > 0.0, 1.0, 0.0)
        for pick in range(2):
            flag = jnp.where(seen == pick, chosen, 0.0)
            keep[2 * expert + pick : 2 * expert + pick + 1, :] = flag
            picked[pick] = picked[pick] + flag * row
        seen = seen + chosen
    weight[...] = jnp.concatenate(picked, axis=0)


def pack(gate, up, down, *refs):
    outs, held = refs[:-1], refs[-1]
    count = held.shape[0]
    part = gate.shape[2] // count
    for pair in range(held.shape[1]):
        for near in range(count):
            span = slice(near * part, (near + 1) * part)
            pieces = []
            for expert in (2 * pair, 2 * pair + 1):
                pieces += [gate[expert, :, span], up[expert, :, span]]
            pieces += [down[2 * pair, :, span], down[2 * pair + 1, :, span]]
            held[near, pair] = jnp.concatenate(pieces, axis=1)
    for flip in range(count):
        outs[flip][...] = held[lax.axis_index(NEAR) ^ flip]


def unpack(part, *refs):
    got, into, back = refs[:-2], refs[-2], refs[-1]
    pairs = got[0].shape[0]
    for pair in range(pairs):
        wide = jnp.concatenate([g[pair, :, : 4 * part] for g in got], axis=0)
        into[pair * 4 * part : (pair + 1) * 4 * part, :] = wide.T
    for flip, g in enumerate(got):
        back[flip] = jnp.concatenate([g[pair, :, 4 * part :] for pair in range(pairs)], axis=1)


def project_up(run, sub, inputs, weights, keep, out):
    count, _, slots = inputs.shape
    features = jnp.concatenate(
        [inputs[lax.axis_index(NEAR) ^ flip, :run, :] for flip in range(count)], axis=0
    )
    ends = jnp.sum(inputs[...].astype(F32)[:, run:], axis=0)
    square = ends[0:1] + ends[1:2]
    unit = 2 * sub * out.shape[0]
    sums = [jnp.zeros((unit, slots), F32) for _ in range(2)]
    for expert in range(weights.shape[0] // unit):
        part = dot(weights[expert * unit : (expert + 1) * unit, :], features)
        for pick in range(2):
            sums[pick] = sums[pick] + keep[2 * expert + pick : 2 * expert + pick + 1, :] * part
    tail = tail_rows(square, 8)
    for dest in range(out.shape[0]):
        pieces = []
        for pick in range(2):
            for kind in range(2):
                start = kind * unit // 2 + dest * sub
                pieces.append(sums[pick][start : start + sub])
        out[dest] = jnp.concatenate(pieces + [tail], axis=0).astype(BF16)


def activate(sub, got, weight, out):
    total = jnp.sum(got[...].astype(F32), axis=0)
    square = total[4 * sub : 4 * sub + 1] + total[4 * sub + 1 : 4 * sub + 2]
    scale = lax.rsqrt(square / D + EPSILON)
    pieces = []
    for pick in range(2):
        gate = total[2 * pick * sub : (2 * pick + 1) * sub] * scale
        up = total[(2 * pick + 1) * sub : (2 * pick + 2) * sub] * scale
        act = gate / (1.0 + jnp.exp(-gate)) * up
        pieces.append(act * weight[pick : pick + 1, :])
    rounded = jnp.concatenate(pieces, axis=0).astype(BF16)
    for i in range(out.shape[0]):
        out[i] = rounded


def project_down(sub, acts, keep, weights, out):
    count, _, slots = acts.shape
    wide = acts[...].astype(F32)
    first = wide[:, :sub].reshape(count * sub, slots)
    second = wide[:, sub:].reshape(count * sub, slots)
    picked = []
    for expert in range(keep.shape[0] // 2):
        picked.append(
            (
                keep[2 * expert : 2 * expert + 1, :] * first
                + keep[2 * expert + 1 : 2 * expert + 2, :] * second
            ).astype(BF16)
        )
    stacked = jnp.concatenate(picked, axis=0)
    for flip in range(weights.shape[0]):
        out[lax.axis_index(NEAR) ^ flip] = dot(weights[flip], stacked).astype(BF16)


def finish_rows(got, out):
    total = jnp.sum(got[...].astype(F32), axis=0).astype(BF16)
    run, slots = total.shape
    padded = jnp.concatenate([total, jnp.zeros((TOK - run, slots), BF16)], axis=0)
    out[...] = padded.T


def combine(got, places, hidden, out):
    run, rows = out.shape
    turned = got[...].T[:run]
    added = dot(turned, places[...])
    out[...] = (hidden[...].astype(F32) + added)[:, :rows].astype(BF16)


def exchange(x, axes):
    return lax.all_to_all(x, axes, split_axis=0, concat_axis=0, tiled=True)


def on_device(
    queries,
    latents,
    block_mask,
    value_up,
    out_proj,
    residual,
    norm_gain,
    group_ids,
    expert_ids,
    route_weights,
    w_gate,
    w_up,
    w_down,
):
    ctx_count = lax.axis_size(CTX)
    near_count = lax.axis_size(NEAR)
    far_count = lax.axis_size(FAR)
    block_rows, key_width = latents.shape
    heads = queries.shape[1]
    value_width = value_up.shape[2]
    run = residual.shape[1]
    local_experts, _, hidden_units = w_gate.shape
    pad_rows = TOK - block_rows
    slots = ctx_count * SLOT
    part = hidden_units // near_count
    sub = part // far_count

    quarter = key_width // lax.axis_size(XC)
    turned_keys = latents.T
    spread = call(spread_keys, shape((ctx_count, quarter, TOK)), [VMEM])(turned_keys)
    pieces = exchange(spread, CTX)
    apart = jnp.arange(ctx_count)[:, None] != jnp.arange(ctx_count)[None, :]
    named = jnp.sum(jnp.where((block_mask == 1) & apart, 1, 0), axis=1)
    few = jnp.max(named) <= FEW

    first_share = run + 16
    places, slot_shares = call(
        functools.partial(route, first_share), [shape((slots, TOK))] * 2, [VMEM] * 3
    )(group_ids.T, expert_ids.transpose(1, 2, 0), route_weights.transpose(1, 2, 0))

    pairs = local_experts // 2
    block = (pairs, run, 6 * part)
    w_gate, places, slot_shares = lax.optimization_barrier((w_gate, places, slot_shares))
    packed = call(
        pack,
        [shape(block)] * near_count,
        [VMEM] * 3,
        [pltpu.VMEM((near_count,) + block, BF16)],
    )(w_gate, w_up, w_down.transpose(0, 2, 1))

    def flipped(x, flip):
        return lax.ppermute(x, NEAR, [(a, a ^ flip) for a in range(near_count)])

    out_proj, *packed = lax.optimization_barrier((out_proj, *packed))
    moved = {i: flipped(packed[i], i) for i in (1, 2, 4, 5)}

    runs = D // run
    depth = heads * value_width
    wide_q, out_mine, out_theirs = call(
        prepare,
        [shape((heads * TOK, key_width))] + [shape((runs // 2, run, depth))] * 2,
        [VMEM] * 2,
        [pltpu.VMEM((D, depth), BF16)],
    )(queries.transpose(1, 2, 0), out_proj)
    out_theirs = lax.ppermute(out_theirs, "core", [(0, 1), (1, 0)])
    resid = jnp.pad(residual.T, ((0, 0), (0, pad_rows)))
    gain = norm_gain.astype(F32)[:, None]
    pieces, few, wide_q, out_mine, out_theirs, moved[1], places, slot_shares, resid, gain = (
        lax.optimization_barrier(
            (pieces, few, wide_q, out_mine, out_theirs, moved[1], places, slot_shares, resid, gain)
        )
    )

    def attention(held_slots, mask, pieces, wide_q, turned_keys, value_up):
        picked = call(pick_keys, shape((held_slots, quarter, TOK)), [SMEM, VMEM])(mask, pieces)
        across = lax.ppermute(picked, "xl", [(0, 1), (1, 0)])
        beside = lax.ppermute(picked, "core", [(0, 1), (1, 0)])
        corner = lax.ppermute(across, "core", [(0, 1), (1, 0)])
        return call(
            attend,
            shape((depth, TOK)),
            [SMEM] + [VMEM] * 7,
            [
                pltpu.VMEM((key_width, TOK), BF16),
                pltpu.VMEM((heads * TOK, 1), F32),
                pltpu.VMEM((heads * TOK, 1), F32),
                pltpu.VMEM((heads * TOK, key_width), F32),
            ],
        )(mask, wide_q, turned_keys, value_up, picked, beside, across, corner)

    values = lax.cond(
        few,
        functools.partial(attention, FEW),
        functools.partial(attention, ctx_count - 1),
        block_mask,
        pieces,
        wide_q,
        turned_keys,
        value_up,
    )
    values, moved = lax.optimization_barrier((values, moved))
    other_values = lax.ppermute(values, "core", [(0, 1), (1, 0)])
    summed = call(project_out, shape((runs // 2, run, TOK)), [VMEM] * 4)(
        values, other_values, out_mine, out_theirs
    )
    summed, *late = lax.optimization_barrier((summed, packed[3], packed[6], packed[7]))
    parts = exchange(summed, ZX)
    for flip, x in zip((3, 6, 7), late):
        moved[flip] = flipped(x, flip)
    moved = [packed[0]] + [moved[flip] for flip in range(1, near_count)]

    hidden, sent = call(make_rows, [shape((run, TOK)), shape((slots, TOK))], [VMEM] * 5)(
        parts,
        resid,
        gain,
        places,
        slot_shares,
    )
    got = exchange(sent.reshape(ctx_count, SLOT, TOK), CTX).reshape(slots, TOK)
    spread, keep, pick_weight = call(
        functools.partial(spread_rows, run + 8, first_share),
        [
            shape((near_count, run + 8, slots)),
            shape((2 * local_experts, slots), F32),
            shape((2, slots), F32),
        ],
        [VMEM],
    )(got)
    spread, moved = lax.optimization_barrier((spread, moved))
    inputs = exchange(spread, NEAR)
    weights_in, weights_back = call(
        functools.partial(unpack, part),
        [
            shape((pairs * 4 * part, near_count * run)),
            shape((near_count, run, local_experts * part)),
        ],
        [VMEM] * near_count,
    )(*moved)
    partial_sums = call(
        functools.partial(project_up, run, sub),
        shape((far_count, 4 * sub + 8, slots)),
        [VMEM] * 3,
    )(inputs, weights_in, keep)
    acts = call(functools.partial(activate, sub), shape((far_count, 2 * sub, slots)), [VMEM] * 2)(
        exchange(partial_sums, FAR), pick_weight
    )
    outputs = call(
        functools.partial(project_down, sub),
        shape((near_count, run, slots)),
        [VMEM] * 3,
    )(exchange(acts, FAR), keep, weights_back)
    returned = call(finish_rows, shape((slots, TOK)), [VMEM])(exchange(outputs, NEAR))
    returned = exchange(returned.reshape(ctx_count, SLOT, TOK), CTX).reshape(slots, TOK)
    out = call(combine, shape((run, block_rows)), [VMEM] * 3)(returned, places, hidden)
    return out.T


def solution(mesh):
    names = ("y", "xh", "za", "zb", "xl", "core")
    fine = Mesh(mesh.devices.reshape(8, 2, 4, 2, 2, 2), names)
    return jax.shard_map(
        on_device,
        mesh=fine,
        in_specs=(
            P(CTX, EXP, None),
            P(CTX, None),
            P(),
            P(EXP, None, None),
            P(EXP, None),
            P(CTX, EXP),
            P(EXP),
            P(CTX, None),
            P(CTX, None, None),
            P(CTX, None, None),
            P(CTX, EXP, None),
            P(CTX, EXP, None),
            P(CTX, None, EXP),
        ),
        out_specs=P(CTX, EXP),
        check_vma=False,
    )
```

```python
import functools

import jax
import jax.numpy as jnp
from jax import lax
from jax.experimental import pallas as pl
from jax.experimental.pallas import tpu as pltpu
from jax.sharding import Mesh
from jax.sharding import PartitionSpec as P

D = 2560
EPSILON = 1e-06
MASKED_SCORE = -1e30
CTX = ("y", "xh")
EXP = ("za", "zb", "xl", "core")
ZX = ("za", "zb", "xl")
PAIR = ("zb", "core")
NEAR = ("zb", "xl", "core")
FAR = "za"
TOK = 128
SLOT = 32
FEW = 5
F32 = jnp.float32
BF16 = jnp.bfloat16
VMEM = pl.BlockSpec(memory_space=pltpu.VMEM)
SMEM = pl.BlockSpec(memory_space=pltpu.SMEM)


def call(body, out_shape, in_specs, scratch=(), flops=0, limit=40):
    many = isinstance(out_shape, (tuple, list))
    return pl.pallas_call(
        body,
        out_shape=out_shape,
        in_specs=in_specs,
        out_specs=[VMEM] * len(out_shape) if many else VMEM,
        scratch_shapes=scratch,
        compiler_params=pltpu.CompilerParams(vmem_limit_bytes=limit << 20),
    )


def shape(dims, dtype=BF16):
    return jax.ShapeDtypeStruct(dims, dtype)


def dot(a, b):
    return jnp.dot(a, b, preferred_element_type=F32)


def dot_nt(a, b):
    return lax.dot_general(a, b, (((1,), (1,)), ((), ())), preferred_element_type=F32)


def spread_keys(keys, out):
    count, part, _ = out.shape
    rows = keys.shape[1]
    own = keys[pl.ds(pl.multiple_of(lax.axis_index(PAIR) * part, part), part), :]
    own = jnp.concatenate([own, jnp.zeros((part, TOK - rows), BF16)], axis=1)
    for i in range(count):
        out[i] = own


def pick_keys(mask, pieces, out):
    block = lax.axis_index(CTX)
    out[...] = jnp.zeros_like(out)

    def step(b, filled):
        wanted = (mask[block, b] == 1) & (b != block)

        @pl.when(wanted)
        def _():
            out[filled] = pieces[b]

        return filled + wanted.astype(jnp.int32)

    lax.fori_loop(0, mask.shape[1], step, 0)


def prepare(queries, weights, wide, mine, theirs, turned):
    heads, width, rows = queries.shape
    for head in range(heads):
        lanes = jnp.concatenate([queries[head], jnp.zeros((width, TOK - rows), BF16)], axis=1)
        wide[head * TOK : (head + 1) * TOK, :] = lanes.T
    for i in range(weights.shape[1] // TOK):
        turned[i * TOK : (i + 1) * TOK, :] = weights[:, i * TOK : (i + 1) * TOK].T
    core = lax.axis_index("core")
    runs, run, _ = mine.shape
    for i in range(runs):
        for out, at in ((mine, 2 * i + core), (theirs, 2 * i + 1 - core)):
            out[i] = turned[pl.ds(pl.multiple_of(at * run, run), run), :]


def route(first, groups, experts, weights, places, shares):
    picks, rows = groups.shape
    slots = places.shape[0]
    count = slots // SLOT
    group = lax.broadcasted_iota(jnp.int32, (count, rows), 0)
    hits = [jnp.where(groups[k : k + 1, :] == group, 1.0, 0.0) for k in range(picks)]
    upto = lax.broadcasted_iota(jnp.int32, (rows, rows), 0)
    upto = jnp.where(upto <= lax.broadcasted_iota(jnp.int32, (rows, rows), 1), 1.0, 0.0)
    rank = dot(sum(hits).astype(BF16), upto.astype(BF16)) - 1.0
    spot = lax.broadcasted_iota(jnp.int32, (count, SLOT, rows), 1).astype(F32)
    here = jnp.where(rank[:, None, :] == spot, 1.0, 0.0)
    lane = lax.broadcasted_iota(jnp.int32, (TOK, rows), 0)
    every = jnp.zeros((slots, rows), F32)
    share = jnp.zeros((slots, TOK), F32)
    for k in range(picks):
        placed = (hits[k][:, None, :] * here).reshape(slots, rows)
        every = every + placed
        table = jnp.zeros((TOK, rows), F32)
        for m in range(experts.shape[1]):
            weight = weights[k, m : m + 1, :].astype(F32)
            table = table + jnp.where(lane == first + experts[k, m : m + 1, :], weight, 0.0)
        share = share + dot_nt(placed.astype(BF16), table.astype(BF16))
    every = jnp.concatenate([every, jnp.zeros((slots, TOK - rows), F32)], axis=1)
    places[...] = every.astype(BF16)
    shares[...] = share.astype(BF16)


def attend(mask, queries, own, up, *refs):
    pieces, (out, held, top, total, acc) = refs[:4], refs[4:]
    block, column = lax.axis_index(CTX), lax.axis_index(PAIR)
    width, rows = own.shape
    part = pieces[0].shape[1]
    inverse_root = width**-0.5
    wide = queries[...]
    query = lax.broadcasted_iota(jnp.int32, (2 * TOK, TOK), 0) % TOK
    key = lax.broadcasted_iota(jnp.int32, (2 * TOK, TOK), 1)

    keys = jnp.concatenate([own[...], jnp.zeros((width, TOK - rows), BF16)], axis=1)
    inside = (key <= query) & (key < rows)
    masked = jnp.where(inside, dot(wide, keys) * inverse_root, MASKED_SCORE)
    best = jnp.max(masked, axis=1, keepdims=True)
    terms = jnp.where(inside, jnp.exp(masked - best), 0.0)
    top[...] = best
    total[...] = jnp.sum(terms, axis=1, keepdims=True)
    acc[...] = dot_nt(terms.astype(BF16), keys)

    def count(b, filled):
        return filled + ((mask[block, b] == 1) & (b != block)).astype(jnp.int32)

    def step(slot, carry):
        for flip, piece in enumerate(pieces):
            start = pl.multiple_of((column ^ flip) * part, part)
            held[pl.ds(start, part), :] = piece[slot]
        inside = key < rows
        masked = jnp.where(inside, dot(wide, held[...]) * inverse_root, MASKED_SCORE)
        old = top[...]
        best = jnp.maximum(old, jnp.max(masked, axis=1, keepdims=True))
        terms = jnp.where(inside, jnp.exp(masked - best), 0.0)
        shrink = jnp.exp(old - best)
        top[...] = best
        total[...] = total[...] * shrink + jnp.sum(terms, axis=1, keepdims=True)
        acc[...] = acc[...] * shrink + dot_nt(terms.astype(BF16), held[...])
        return carry

    lax.fori_loop(0, lax.fori_loop(0, mask.shape[1], count, 0), step, 0)
    inverse = 1.0 / total[...]
    values = []
    for head in range(up.shape[0]):
        span = slice(head * TOK, (head + 1) * TOK)
        latent = acc[span, : up.shape[1]] * inverse[span, :]
        high = latent.astype(BF16)
        low = (latent - high.astype(F32)).astype(BF16)
        values.append((dot(high, up[head]) + dot(low, up[head])).T.astype(BF16))
    out[...] = jnp.concatenate(values, axis=0)


def project_out(mine, theirs, weights_mine, weights_theirs, out):
    runs, run, depth = weights_mine.shape
    total = dot(weights_mine[...].reshape(runs * run, depth), mine[...])
    total = total + dot(weights_theirs[...].reshape(runs * run, depth), theirs[...])
    out[...] = total.reshape(runs, run, TOK).astype(BF16)


def split_pair(value):
    high = value.astype(BF16).astype(F32)
    return high, (value - high).astype(BF16).astype(F32)


def tail_rows(value, count):
    high, low = split_pair(value)
    row = lax.broadcasted_iota(jnp.int32, (count, value.shape[1]), 0)
    return jnp.where(row == 0, high, jnp.where(row == 1, low, 0.0))


def make_rows(parts, residual, gain, places, shares, hidden, sent):
    mixed = jnp.sum(parts[...].astype(F32), axis=0)
    held = (residual[...].astype(F32) + mixed).astype(BF16)
    hidden[...] = held
    wide = held.astype(F32)
    square = jnp.sum(wide * wide, axis=0, keepdims=True)
    run = wide.shape[0]
    rows = jnp.concatenate([wide * gain[...], tail_rows(square, TOK - run)], axis=0).astype(BF16)
    sent[...] = (dot_nt(places[...], rows) + shares[...].astype(F32)).astype(BF16)


def spread_rows(keep_rows, first, got, out, keep, weight):
    turned = got[...].T
    kept = turned[:keep_rows]
    for i in range(out.shape[0]):
        out[i] = kept
    count = keep.shape[0] // 2
    weights = turned[first : first + 16].astype(F32)
    seen = jnp.zeros((1, weights.shape[1]), F32)
    picked = [jnp.zeros((1, weights.shape[1]), F32) for _ in range(2)]
    for expert in range(count):
        row = weights[expert : expert + 1]
        chosen = jnp.where(row > 0.0, 1.0, 0.0)
        for pick in range(2):
            flag = jnp.where(seen == pick, chosen, 0.0)
            keep[2 * expert + pick : 2 * expert + pick + 1, :] = flag
            picked[pick] = picked[pick] + flag * row
        seen = seen + chosen
    weight[...] = jnp.concatenate(picked, axis=0)


def pack(gate, up, down, *refs):
    outs, held = refs[:-1], refs[-1]
    count = held.shape[0]
    part = gate.shape[2] // count
    for pair in range(held.shape[1]):
        for near in range(count):
            span = slice(near * part, (near + 1) * part)
            pieces = []
            for expert in (2 * pair, 2 * pair + 1):
                pieces += [gate[expert, :, span], up[expert, :, span]]
            pieces += [down[2 * pair, :, span], down[2 * pair + 1, :, span]]
            held[near, pair] = jnp.concatenate(pieces, axis=1)
    for flip in range(count):
        outs[flip][...] = held[lax.axis_index(NEAR) ^ flip]


def unpack(part, *refs):
    got, into, back = refs[:-2], refs[-2], refs[-1]
    pairs = got[0].shape[0]
    for pair in range(pairs):
        wide = jnp.concatenate([g[pair, :, : 4 * part] for g in got], axis=0)
        into[pair * 4 * part : (pair + 1) * 4 * part, :] = wide.T
    for flip, g in enumerate(got):
        back[flip] = jnp.concatenate([g[pair, :, 4 * part :] for pair in range(pairs)], axis=1)


def project_up(run, sub, inputs, weights, keep, out):
    count, _, slots = inputs.shape
    features = jnp.concatenate(
        [inputs[lax.axis_index(NEAR) ^ flip, :run, :] for flip in range(count)], axis=0
    )
    ends = jnp.sum(inputs[...].astype(F32)[:, run:], axis=0)
    square = ends[0:1] + ends[1:2]
    unit = 2 * sub * out.shape[0]
    sums = [jnp.zeros((unit, slots), F32) for _ in range(2)]
    for expert in range(weights.shape[0] // unit):
        part = dot(weights[expert * unit : (expert + 1) * unit, :], features)
        for pick in range(2):
            sums[pick] = sums[pick] + keep[2 * expert + pick : 2 * expert + pick + 1, :] * part
    tail = tail_rows(square, 8)
    for dest in range(out.shape[0]):
        pieces = []
        for pick in range(2):
            for kind in range(2):
                start = kind * unit // 2 + dest * sub
                pieces.append(sums[pick][start : start + sub])
        out[dest] = jnp.concatenate(pieces + [tail], axis=0).astype(BF16)


def activate(sub, got, weight, out):
    total = jnp.sum(got[...].astype(F32), axis=0)
    square = total[4 * sub : 4 * sub + 1] + total[4 * sub + 1 : 4 * sub + 2]
    scale = lax.rsqrt(square / D + EPSILON)
    pieces = []
    for pick in range(2):
        gate = total[2 * pick * sub : (2 * pick + 1) * sub] * scale
        up = total[(2 * pick + 1) * sub : (2 * pick + 2) * sub] * scale
        act = gate / (1.0 + jnp.exp(-gate)) * up
        pieces.append(act * weight[pick : pick + 1, :])
    rounded = jnp.concatenate(pieces, axis=0).astype(BF16)
    for i in range(out.shape[0]):
        out[i] = rounded


def project_down(sub, acts, keep, weights, out):
    count, _, slots = acts.shape
    wide = acts[...].astype(F32)
    first = wide[:, :sub].reshape(count * sub, slots)
    second = wide[:, sub:].reshape(count * sub, slots)
    picked = []
    for expert in range(keep.shape[0] // 2):
        picked.append(
            (
                keep[2 * expert : 2 * expert + 1, :] * first
                + keep[2 * expert + 1 : 2 * expert + 2, :] * second
            ).astype(BF16)
        )
    stacked = jnp.concatenate(picked, axis=0)
    for flip in range(weights.shape[0]):
        out[lax.axis_index(NEAR) ^ flip] = dot(weights[flip], stacked).astype(BF16)


def finish_rows(got, out):
    total = jnp.sum(got[...].astype(F32), axis=0).astype(BF16)
    run, slots = total.shape
    padded = jnp.concatenate([total, jnp.zeros((TOK - run, slots), BF16)], axis=0)
    out[...] = padded.T


def combine(got, places, hidden, out):
    run, rows = out.shape
    turned = got[...].T[:run]
    added = dot(turned, places[...])
    out[...] = (hidden[...].astype(F32) + added)[:, :rows].astype(BF16)


def exchange(x, axes):
    return lax.all_to_all(x, axes, split_axis=0, concat_axis=0, tiled=True)


def on_device(
    queries,
    latents,
    block_mask,
    value_up,
    out_proj,
    residual,
    norm_gain,
    group_ids,
    expert_ids,
    route_weights,
    w_gate,
    w_up,
    w_down,
):
    ctx_count = lax.axis_size(CTX)
    near_count = lax.axis_size(NEAR)
    far_count = lax.axis_size(FAR)
    block_rows, key_width = latents.shape
    heads = queries.shape[1]
    value_width = value_up.shape[2]
    run = residual.shape[1]
    local_experts, _, hidden_units = w_gate.shape
    pad_rows = TOK - block_rows
    slots = ctx_count * SLOT
    part = hidden_units // near_count
    sub = part // far_count

    quarter = key_width // lax.axis_size(PAIR)
    turned_keys = latents.T
    spread = call(spread_keys, shape((ctx_count, quarter, TOK)), [VMEM])(turned_keys)
    pieces = exchange(spread, CTX)
    apart = jnp.arange(ctx_count)[:, None] != jnp.arange(ctx_count)[None, :]
    named = jnp.sum(jnp.where((block_mask == 1) & apart, 1, 0), axis=1)
    few = jnp.max(named) <= FEW

    first_share = run + 16
    places, slot_shares = call(
        functools.partial(route, first_share), [shape((slots, TOK))] * 2, [VMEM] * 3
    )(group_ids.T, expert_ids.transpose(1, 2, 0), route_weights.transpose(1, 2, 0))

    pairs = local_experts // 2
    block = (pairs, run, 6 * part)
    w_gate, places, slot_shares = lax.optimization_barrier((w_gate, places, slot_shares))
    packed = call(
        pack,
        [shape(block)] * near_count,
        [VMEM] * 3,
        [pltpu.VMEM((near_count,) + block, BF16)],
    )(w_gate, w_up, w_down.transpose(0, 2, 1))

    def flipped(x, flip):
        return lax.ppermute(x, NEAR, [(a, a ^ flip) for a in range(near_count)])

    out_proj, *packed = lax.optimization_barrier((out_proj, *packed))
    moved = {i: flipped(packed[i], i) for i in (2, 3, 6)}

    runs = D // run
    depth = heads * value_width
    wide_q, out_mine, out_theirs = call(
        prepare,
        [shape((heads * TOK, key_width))] + [shape((runs // 2, run, depth))] * 2,
        [VMEM] * 2,
        [pltpu.VMEM((D, depth), BF16)],
    )(queries.transpose(1, 2, 0), out_proj)
    out_theirs = lax.ppermute(out_theirs, "core", [(0, 1), (1, 0)])
    resid = jnp.pad(residual.T, ((0, 0), (0, pad_rows)))
    gain = norm_gain.astype(F32)[:, None]
    pieces, few, wide_q, out_mine, out_theirs, places, slot_shares, resid, gain = (
        lax.optimization_barrier(
            (pieces, few, wide_q, out_mine, out_theirs, places, slot_shares, resid, gain)
        )
    )

    def attention(held_slots, mask, pieces, wide_q, turned_keys, value_up):
        picked = call(pick_keys, shape((held_slots, quarter, TOK)), [SMEM, VMEM])(mask, pieces)
        across = lax.ppermute(picked, "zb", [(0, 1), (1, 0)])
        beside = lax.ppermute(picked, "core", [(0, 1), (1, 0)])
        corner = lax.ppermute(across, "core", [(0, 1), (1, 0)])
        return call(
            attend,
            shape((depth, TOK)),
            [SMEM] + [VMEM] * 7,
            [
                pltpu.VMEM((key_width, TOK), BF16),
                pltpu.VMEM((heads * TOK, 1), F32),
                pltpu.VMEM((heads * TOK, 1), F32),
                pltpu.VMEM((heads * TOK, key_width), F32),
            ],
        )(mask, wide_q, turned_keys, value_up, picked, beside, across, corner)

    values = lax.cond(
        few,
        functools.partial(attention, FEW),
        functools.partial(attention, ctx_count - 1),
        block_mask,
        pieces,
        wide_q,
        turned_keys,
        value_up,
    )
    values, moved = lax.optimization_barrier((values, moved))
    other_values = lax.ppermute(values, "core", [(0, 1), (1, 0)])
    summed = call(project_out, shape((runs // 2, run, TOK)), [VMEM] * 4)(
        values, other_values, out_mine, out_theirs
    )
    summed, *late = lax.optimization_barrier((summed, packed[7], packed[4], packed[5], packed[1]))
    parts = exchange(summed, ZX)
    for flip, x in zip((7, 4, 5, 1), late):
        moved[flip] = flipped(x, flip)

    hidden, sent = call(make_rows, [shape((run, TOK)), shape((slots, TOK))], [VMEM] * 5)(
        parts,
        resid,
        gain,
        places,
        slot_shares,
    )
    got = exchange(sent.reshape(ctx_count, SLOT, TOK), CTX).reshape(slots, TOK)
    moved = [packed[0]] + [moved[flip] for flip in range(1, near_count)]
    spread, keep, pick_weight = call(
        functools.partial(spread_rows, run + 8, first_share),
        [
            shape((near_count, run + 8, slots)),
            shape((2 * local_experts, slots), F32),
            shape((2, slots), F32),
        ],
        [VMEM],
    )(got)
    spread, moved = lax.optimization_barrier((spread, moved))
    inputs = exchange(spread, NEAR)
    weights_in, weights_back = call(
        functools.partial(unpack, part),
        [
            shape((pairs * 4 * part, near_count * run)),
            shape((near_count, run, local_experts * part)),
        ],
        [VMEM] * near_count,
    )(*moved)
    partial_sums = call(
        functools.partial(project_up, run, sub),
        shape((far_count, 4 * sub + 8, slots)),
        [VMEM] * 3,
    )(inputs, weights_in, keep)
    acts = call(functools.partial(activate, sub), shape((far_count, 2 * sub, slots)), [VMEM] * 2)(
        exchange(partial_sums, FAR), pick_weight
    )
    outputs = call(
        functools.partial(project_down, sub),
        shape((near_count, run, slots)),
        [VMEM] * 3,
    )(exchange(acts, FAR), keep, weights_back)
    returned = call(finish_rows, shape((slots, TOK)), [VMEM])(exchange(outputs, NEAR))
    returned = exchange(returned.reshape(ctx_count, SLOT, TOK), CTX).reshape(slots, TOK)
    out = call(combine, shape((run, block_rows)), [VMEM] * 3)(returned, places, hidden)
    return out.T


def solution(mesh):
    names = ("y", "xh", "za", "zb", "xl", "core")
    fine = Mesh(mesh.devices.reshape(8, 2, 4, 2, 2, 2), names)
    return jax.shard_map(
        on_device,
        mesh=fine,
        in_specs=(
            P(CTX, EXP, None),
            P(CTX, None),
            P(),
            P(EXP, None, None),
            P(EXP, None),
            P(CTX, EXP),
            P(EXP),
            P(CTX, None),
            P(CTX, None, None),
            P(CTX, None, None),
            P(CTX, EXP, None),
            P(CTX, EXP, None),
            P(CTX, None, EXP),
        ),
        out_specs=P(CTX, EXP),
        check_vma=False,
    )
```

```python
import functools

import jax
import jax.numpy as jnp
from jax import lax
from jax.experimental import pallas as pl
from jax.experimental.pallas import tpu as pltpu
from jax.sharding import Mesh
from jax.sharding import PartitionSpec as P

D = 2560
EPSILON = 1e-06
MASKED_SCORE = -1e30
CTX = ("y", "xh")
EXP = ("za", "zb", "xl", "core")
ZX = ("za", "zb", "xl")
PAIR = ("zb", "core")
NEAR = ("zb", "xl", "core")
FAR = "za"
TOK = 128
SLOT = 32
FEW = 5
F32 = jnp.float32
BF16 = jnp.bfloat16
VMEM = pl.BlockSpec(memory_space=pltpu.VMEM)
SMEM = pl.BlockSpec(memory_space=pltpu.SMEM)


def call(body, out_shape, in_specs, scratch=(), flops=0, limit=40):
    many = isinstance(out_shape, (tuple, list))
    return pl.pallas_call(
        body,
        out_shape=out_shape,
        in_specs=in_specs,
        out_specs=[VMEM] * len(out_shape) if many else VMEM,
        scratch_shapes=scratch,
        compiler_params=pltpu.CompilerParams(vmem_limit_bytes=limit << 20),
    )


def shape(dims, dtype=BF16):
    return jax.ShapeDtypeStruct(dims, dtype)


def dot(a, b):
    return jnp.dot(a, b, preferred_element_type=F32)


def dot_nt(a, b):
    return lax.dot_general(a, b, (((1,), (1,)), ((), ())), preferred_element_type=F32)


def spread_keys(keys, out):
    count, part, _ = out.shape
    rows = keys.shape[1]
    column = lax.axis_index(PAIR)
    own = keys[:part]
    for i in range(1, keys.shape[0] // part):
        own = jnp.where(column == i, keys[i * part : (i + 1) * part], own)
    own = jnp.concatenate([own, jnp.zeros((part, TOK - rows), BF16)], axis=1)
    for i in range(count):
        out[i] = own


def pick_keys(mask, pieces, out):
    block = lax.axis_index(CTX)
    out[...] = jnp.zeros_like(out)

    def step(b, filled):
        wanted = (mask[block, b] == 1) & (b != block)

        @pl.when(wanted)
        def _():
            out[filled] = pieces[b]

        return filled + wanted.astype(jnp.int32)

    lax.fori_loop(0, mask.shape[1], step, 0)


def prepare(queries, weights, wide, mine, theirs, turned):
    heads, width, rows = queries.shape
    for head in range(heads):
        lanes = jnp.concatenate([queries[head], jnp.zeros((width, TOK - rows), BF16)], axis=1)
        wide[head * TOK : (head + 1) * TOK, :] = lanes.T
    for i in range(weights.shape[1] // TOK):
        turned[i * TOK : (i + 1) * TOK, :] = weights[:, i * TOK : (i + 1) * TOK].T
    core = lax.axis_index("core")
    runs, run, _ = mine.shape
    for i in range(runs):
        for out, at in ((mine, 2 * i + core), (theirs, 2 * i + 1 - core)):
            out[i] = turned[pl.ds(pl.multiple_of(at * run, run), run), :]


def route(first, groups, experts, weights, places, shares):
    picks, rows = groups.shape
    slots = places.shape[0]
    count = slots // SLOT
    group = lax.broadcasted_iota(jnp.int32, (count, rows), 0)
    hits = [jnp.where(groups[k : k + 1, :] == group, 1.0, 0.0) for k in range(picks)]
    upto = lax.broadcasted_iota(jnp.int32, (rows, rows), 0)
    upto = jnp.where(upto <= lax.broadcasted_iota(jnp.int32, (rows, rows), 1), 1.0, 0.0)
    rank = dot(sum(hits).astype(BF16), upto.astype(BF16)) - 1.0
    spot = lax.broadcasted_iota(jnp.int32, (count, SLOT, rows), 1).astype(F32)
    here = jnp.where(rank[:, None, :] == spot, 1.0, 0.0)
    lane = lax.broadcasted_iota(jnp.int32, (TOK, rows), 0)
    every = jnp.zeros((slots, rows), F32)
    share = jnp.zeros((slots, TOK), F32)
    for k in range(picks):
        placed = (hits[k][:, None, :] * here).reshape(slots, rows)
        every = every + placed
        table = jnp.zeros((TOK, rows), F32)
        for m in range(experts.shape[1]):
            weight = weights[k, m : m + 1, :].astype(F32)
            table = table + jnp.where(lane == first + experts[k, m : m + 1, :], weight, 0.0)
        share = share + dot_nt(placed.astype(BF16), table.astype(BF16))
    every = jnp.concatenate([every, jnp.zeros((slots, TOK - rows), F32)], axis=1)
    places[...] = every.astype(BF16)
    shares[...] = share.astype(BF16)


def attend(mask, queries, own, up, *refs):
    pieces, (out, held, top, total, acc) = refs[:4], refs[4:]
    block, column = lax.axis_index(CTX), lax.axis_index(PAIR)
    width, rows = own.shape
    part = pieces[0].shape[1]
    inverse_root = width**-0.5
    wide = queries[...]
    query = lax.broadcasted_iota(jnp.int32, (2 * TOK, TOK), 0) % TOK
    key = lax.broadcasted_iota(jnp.int32, (2 * TOK, TOK), 1)

    keys = jnp.concatenate([own[...], jnp.zeros((width, TOK - rows), BF16)], axis=1)
    inside = (key <= query) & (key < rows)
    masked = jnp.where(inside, dot(wide, keys) * inverse_root, MASKED_SCORE)
    best = jnp.max(masked, axis=1, keepdims=True)
    terms = jnp.where(inside, jnp.exp(masked - best), 0.0)
    top[...] = best
    total[...] = jnp.sum(terms, axis=1, keepdims=True)
    acc[...] = dot_nt(terms.astype(BF16), keys)

    def count(b, filled):
        return filled + ((mask[block, b] == 1) & (b != block)).astype(jnp.int32)

    def step(slot, carry):
        for flip, piece in enumerate(pieces):
            start = pl.multiple_of((column ^ flip) * part, part)
            held[pl.ds(start, part), :] = piece[slot]
        inside = key < rows
        masked = jnp.where(inside, dot(wide, held[...]) * inverse_root, MASKED_SCORE)
        old = top[...]
        best = jnp.maximum(old, jnp.max(masked, axis=1, keepdims=True))
        terms = jnp.where(inside, jnp.exp(masked - best), 0.0)
        shrink = jnp.exp(old - best)
        top[...] = best
        total[...] = total[...] * shrink + jnp.sum(terms, axis=1, keepdims=True)
        acc[...] = acc[...] * shrink + dot_nt(terms.astype(BF16), held[...])
        return carry

    lax.fori_loop(0, lax.fori_loop(0, mask.shape[1], count, 0), step, 0)
    inverse = 1.0 / total[...]
    values = []
    for head in range(up.shape[0]):
        span = slice(head * TOK, (head + 1) * TOK)
        latent = acc[span, : up.shape[1]] * inverse[span, :]
        high = latent.astype(BF16)
        low = (latent - high.astype(F32)).astype(BF16)
        values.append((dot(high, up[head]) + dot(low, up[head])).T.astype(BF16))
    out[...] = jnp.concatenate(values, axis=0)


def project_out(mine, theirs, weights_mine, weights_theirs, out):
    runs, run, depth = weights_mine.shape
    total = dot(weights_mine[...].reshape(runs * run, depth), mine[...])
    total = total + dot(weights_theirs[...].reshape(runs * run, depth), theirs[...])
    out[...] = total.reshape(runs, run, TOK).astype(BF16)


def split_pair(value):
    high = value.astype(BF16).astype(F32)
    return high, (value - high).astype(BF16).astype(F32)


def tail_rows(value, count):
    high, low = split_pair(value)
    row = lax.broadcasted_iota(jnp.int32, (count, value.shape[1]), 0)
    return jnp.where(row == 0, high, jnp.where(row == 1, low, 0.0))


def make_rows(parts, residual, gain, places, shares, hidden, sent):
    mixed = jnp.sum(parts[...].astype(F32), axis=0)
    held = (residual[...].astype(F32) + mixed).astype(BF16)
    hidden[...] = held
    wide = held.astype(F32)
    square = jnp.sum(wide * wide, axis=0, keepdims=True)
    run = wide.shape[0]
    rows = jnp.concatenate([wide * gain[...], tail_rows(square, TOK - run)], axis=0).astype(BF16)
    sent[...] = (dot_nt(places[...], rows) + shares[...].astype(F32)).astype(BF16)


def spread_rows(keep_rows, first, got, out, keep, weight):
    turned = got[...].T
    kept = turned[:keep_rows]
    for i in range(out.shape[0]):
        out[i] = kept
    count = keep.shape[0] // 2
    weights = turned[first : first + 16].astype(F32)
    seen = jnp.zeros((1, weights.shape[1]), F32)
    picked = [jnp.zeros((1, weights.shape[1]), F32) for _ in range(2)]
    for expert in range(count):
        row = weights[expert : expert + 1]
        chosen = jnp.where(row > 0.0, 1.0, 0.0)
        for pick in range(2):
            flag = jnp.where(seen == pick, chosen, 0.0)
            keep[2 * expert + pick : 2 * expert + pick + 1, :] = flag
            picked[pick] = picked[pick] + flag * row
        seen = seen + chosen
    weight[...] = jnp.concatenate(picked, axis=0)


def pack(gate, up, down, mine, swapped, far_x, far_z, far_xz, held):
    count = held.shape[0]
    part = gate.shape[2] // count
    for pair in range(held.shape[1]):
        for near in range(count):
            span = slice(near * part, (near + 1) * part)
            pieces = []
            for expert in (2 * pair, 2 * pair + 1):
                pieces += [gate[expert, :, span], up[expert, :, span]]
            pieces += [down[2 * pair, :, span], down[2 * pair + 1, :, span]]
            held[near, pair] = jnp.concatenate(pieces, axis=1)
    near = lax.axis_index(NEAR)
    mine[...] = held[near]
    swapped[...] = held[near ^ 1]
    for out, flip in ((far_x, 2), (far_z, 4), (far_xz, 6)):
        out[0] = held[near ^ flip]
        out[1] = held[near ^ flip ^ 1]


def gather_swap(swapped, far_x, far_z, far_xz, low, high):
    low[0] = swapped[...]
    low[1] = far_x[1]
    high[0] = far_z[1]
    high[1] = far_xz[1]


def unpack(part, mine, far_x, far_z, far_xz, low, high, into, back):
    pairs = mine.shape[0]
    for pair in range(pairs):
        rows = []
        for i, own in enumerate((mine, far_x, far_z, far_xz)):
            rows.append(own[pair] if i == 0 else own[0, pair])
            rows.append((low, low, high, high)[i][i % 2, pair])
        wide = jnp.concatenate([row[:, : 4 * part] for row in rows], axis=0)
        into[pair * 4 * part : (pair + 1) * 4 * part, :] = wide.T
        for flip, row in enumerate(rows):
            back[flip, :, pair * 2 * part : (pair + 1) * 2 * part] = row[:, 4 * part :]


def project_up(run, sub, inputs, weights, keep, out):
    count, _, slots = inputs.shape
    features = jnp.concatenate(
        [inputs[lax.axis_index(NEAR) ^ flip, :run, :] for flip in range(count)], axis=0
    )
    ends = jnp.sum(inputs[...].astype(F32)[:, run:], axis=0)
    square = ends[0:1] + ends[1:2]
    unit = 2 * sub * out.shape[0]
    sums = [jnp.zeros((unit, slots), F32) for _ in range(2)]
    for expert in range(weights.shape[0] // unit):
        part = dot(weights[expert * unit : (expert + 1) * unit, :], features)
        for pick in range(2):
            sums[pick] = sums[pick] + keep[2 * expert + pick : 2 * expert + pick + 1, :] * part
    tail = tail_rows(square, 8)
    for dest in range(out.shape[0]):
        pieces = []
        for pick in range(2):
            for kind in range(2):
                start = kind * unit // 2 + dest * sub
                pieces.append(sums[pick][start : start + sub])
        out[dest] = jnp.concatenate(pieces + [tail], axis=0).astype(BF16)


def activate(sub, got, weight, out):
    total = jnp.sum(got[...].astype(F32), axis=0)
    square = total[4 * sub : 4 * sub + 1] + total[4 * sub + 1 : 4 * sub + 2]
    scale = lax.rsqrt(square / D + EPSILON)
    pieces = []
    for pick in range(2):
        gate = total[2 * pick * sub : (2 * pick + 1) * sub] * scale
        up = total[(2 * pick + 1) * sub : (2 * pick + 2) * sub] * scale
        act = gate / (1.0 + jnp.exp(-gate)) * up
        pieces.append(act * weight[pick : pick + 1, :])
    rounded = jnp.concatenate(pieces, axis=0).astype(BF16)
    for i in range(out.shape[0]):
        out[i] = rounded


def project_down(sub, acts, keep, weights, out):
    count, _, slots = acts.shape
    wide = acts[...].astype(F32)
    first = wide[:, :sub].reshape(count * sub, slots)
    second = wide[:, sub:].reshape(count * sub, slots)
    picked = []
    for expert in range(keep.shape[0] // 2):
        picked.append(
            (
                keep[2 * expert : 2 * expert + 1, :] * first
                + keep[2 * expert + 1 : 2 * expert + 2, :] * second
            ).astype(BF16)
        )
    stacked = jnp.concatenate(picked, axis=0)
    for flip in range(weights.shape[0]):
        out[lax.axis_index(NEAR) ^ flip] = dot(weights[flip], stacked).astype(BF16)


def finish_rows(got, out):
    total = jnp.sum(got[...].astype(F32), axis=0).astype(BF16)
    run, slots = total.shape
    padded = jnp.concatenate([total, jnp.zeros((TOK - run, slots), BF16)], axis=0)
    out[...] = padded.T


def combine(got, places, hidden, out):
    run, rows = out.shape
    turned = got[...].T[:run]
    added = dot(turned, places[...])
    out[...] = (hidden[...].astype(F32) + added)[:, :rows].astype(BF16)


def exchange(x, axes):
    return lax.all_to_all(x, axes, split_axis=0, concat_axis=0, tiled=True)


def on_device(
    queries,
    latents,
    block_mask,
    value_up,
    out_proj,
    residual,
    norm_gain,
    group_ids,
    expert_ids,
    route_weights,
    w_gate,
    w_up,
    w_down,
):
    ctx_count = lax.axis_size(CTX)
    near_count = lax.axis_size(NEAR)
    far_count = lax.axis_size(FAR)
    block_rows, key_width = latents.shape
    heads = queries.shape[1]
    value_width = value_up.shape[2]
    run = residual.shape[1]
    local_experts, _, hidden_units = w_gate.shape
    pad_rows = TOK - block_rows
    slots = ctx_count * SLOT
    part = hidden_units // near_count
    sub = part // far_count

    quarter = key_width // lax.axis_size(PAIR)
    turned_keys = latents.T
    spread = call(spread_keys, shape((ctx_count, quarter, TOK)), [VMEM])(turned_keys)
    pieces = exchange(spread, CTX)
    apart = jnp.arange(ctx_count)[:, None] != jnp.arange(ctx_count)[None, :]
    named = jnp.sum(jnp.where((block_mask == 1) & apart, 1, 0), axis=1)
    few = jnp.max(named) <= FEW

    first_share = run + 16
    places, slot_shares = call(
        functools.partial(route, first_share), [shape((slots, TOK))] * 2, [VMEM] * 3
    )(group_ids.T, expert_ids.transpose(1, 2, 0), route_weights.transpose(1, 2, 0))

    pairs = local_experts // 2
    block = (pairs, run, 6 * part)
    mine, swapped, *far = call(
        pack,
        [shape(block)] * 2 + [shape((2,) + block)] * 3,
        [VMEM] * 3,
        [pltpu.VMEM((near_count,) + block, BF16)],
    )(w_gate, w_up, w_down.transpose(0, 2, 1))
    out_proj, *far = lax.optimization_barrier((out_proj, *far))

    def flipped(x, flip):
        return lax.ppermute(x, NEAR, [(a, a ^ flip) for a in range(near_count)])

    far = [flipped(x, flip) for x, flip in zip(far, (2, 4, 6))]

    runs = D // run
    depth = heads * value_width
    wide_q, out_mine, out_theirs = call(
        prepare,
        [shape((heads * TOK, key_width))] + [shape((runs // 2, run, depth))] * 2,
        [VMEM] * 2,
        [pltpu.VMEM((D, depth), BF16)],
    )(queries.transpose(1, 2, 0), out_proj)
    out_theirs = lax.ppermute(out_theirs, "core", [(0, 1), (1, 0)])
    resid = jnp.pad(residual.T, ((0, 0), (0, pad_rows)))
    gain = norm_gain.astype(F32)[:, None]
    pieces, few, wide_q, out_mine, out_theirs, places, slot_shares, resid, gain = (
        lax.optimization_barrier(
            (pieces, few, wide_q, out_mine, out_theirs, places, slot_shares, resid, gain)
        )
    )

    def attention(held_slots, mask, pieces, wide_q, turned_keys, value_up):
        picked = call(pick_keys, shape((held_slots, quarter, TOK)), [SMEM, VMEM])(mask, pieces)
        across = lax.ppermute(picked, "zb", [(0, 1), (1, 0)])
        beside = lax.ppermute(picked, "core", [(0, 1), (1, 0)])
        corner = lax.ppermute(across, "core", [(0, 1), (1, 0)])
        return call(
            attend,
            shape((depth, TOK)),
            [SMEM] + [VMEM] * 7,
            [
                pltpu.VMEM((key_width, TOK), BF16),
                pltpu.VMEM((heads * TOK, 1), F32),
                pltpu.VMEM((heads * TOK, 1), F32),
                pltpu.VMEM((heads * TOK, key_width), F32),
            ],
        )(mask, wide_q, turned_keys, value_up, picked, beside, across, corner)

    values = lax.cond(
        few,
        functools.partial(attention, FEW),
        functools.partial(attention, ctx_count - 1),
        block_mask,
        pieces,
        wide_q,
        turned_keys,
        value_up,
    )
    other_values = lax.ppermute(values, "core", [(0, 1), (1, 0)])
    summed = call(project_out, shape((runs // 2, run, TOK)), [VMEM] * 4)(
        values, other_values, out_mine, out_theirs
    )
    summed, swapped = lax.optimization_barrier((summed, swapped))
    parts = exchange(summed, ZX)
    swap = [
        flipped(x, 1)
        for x in call(gather_swap, [shape((2,) + block)] * 2, [VMEM] * 4)(swapped, *far)
    ]

    hidden, sent = call(make_rows, [shape((run, TOK)), shape((slots, TOK))], [VMEM] * 5)(
        parts,
        resid,
        gain,
        places,
        slot_shares,
    )
    got = exchange(sent.reshape(ctx_count, SLOT, TOK), CTX).reshape(slots, TOK)
    spread, keep, pick_weight = call(
        functools.partial(spread_rows, run + 8, first_share),
        [
            shape((near_count, run + 8, slots)),
            shape((2 * local_experts, slots), F32),
            shape((2, slots), F32),
        ],
        [VMEM],
    )(got)
    spread, swap = lax.optimization_barrier((spread, swap))
    inputs = exchange(spread, NEAR)
    weights_in, weights_back = call(
        functools.partial(unpack, part),
        [
            shape((pairs * 4 * part, near_count * run)),
            shape((near_count, run, local_experts * part)),
        ],
        [VMEM] * 6,
    )(mine, *far, *swap)
    partial_sums = call(
        functools.partial(project_up, run, sub),
        shape((far_count, 4 * sub + 8, slots)),
        [VMEM] * 3,
    )(inputs, weights_in, keep)
    acts = call(functools.partial(activate, sub), shape((far_count, 2 * sub, slots)), [VMEM] * 2)(
        exchange(partial_sums, FAR), pick_weight
    )
    outputs = call(
        functools.partial(project_down, sub),
        shape((near_count, run, slots)),
        [VMEM] * 3,
    )(exchange(acts, FAR), keep, weights_back)
    returned = call(finish_rows, shape((slots, TOK)), [VMEM])(exchange(outputs, NEAR))
    returned = exchange(returned.reshape(ctx_count, SLOT, TOK), CTX).reshape(slots, TOK)
    out = call(combine, shape((run, block_rows)), [VMEM] * 3)(returned, places, hidden)
    return out.T


def solution(mesh):
    names = ("y", "xh", "za", "zb", "xl", "core")
    fine = Mesh(mesh.devices.reshape(8, 2, 4, 2, 2, 2), names)
    return jax.shard_map(
        on_device,
        mesh=fine,
        in_specs=(
            P(CTX, EXP, None),
            P(CTX, None),
            P(),
            P(EXP, None, None),
            P(EXP, None),
            P(CTX, EXP),
            P(EXP),
            P(CTX, None),
            P(CTX, None, None),
            P(CTX, None, None),
            P(CTX, EXP, None),
            P(CTX, EXP, None),
            P(CTX, None, EXP),
        ),
        out_specs=P(CTX, EXP),
        check_vma=False,
    )
```

```python
import functools

import jax
import jax.numpy as jnp
from jax import lax
from jax.experimental import pallas as pl
from jax.experimental.pallas import tpu as pltpu
from jax.sharding import Mesh
from jax.sharding import PartitionSpec as P

D = 2560
EPSILON = 1e-06
MASKED_SCORE = -1e30
CTX = ("y", "xh")
EXP = ("za", "zb", "xl", "core")
ZX = ("za", "zb", "xl")
PAIR = ("zb", "core")
NEAR = ("zb", "xl", "core")
FAR = "za"
TOK = 128
SLOT = 32
FEW = 5
F32 = jnp.float32
BF16 = jnp.bfloat16
VMEM = pl.BlockSpec(memory_space=pltpu.VMEM)
SMEM = pl.BlockSpec(memory_space=pltpu.SMEM)


def call(body, out_shape, in_specs, scratch=(), flops=0, limit=40):
    many = isinstance(out_shape, (tuple, list))
    return pl.pallas_call(
        body,
        out_shape=out_shape,
        in_specs=in_specs,
        out_specs=[VMEM] * len(out_shape) if many else VMEM,
        scratch_shapes=scratch,
        compiler_params=pltpu.CompilerParams(vmem_limit_bytes=limit << 20),
    )


def shape(dims, dtype=BF16):
    return jax.ShapeDtypeStruct(dims, dtype)


def dot(a, b):
    return jnp.dot(a, b, preferred_element_type=F32)


def dot_nt(a, b):
    return lax.dot_general(a, b, (((1,), (1,)), ((), ())), preferred_element_type=F32)


def spread_keys(keys, out):
    count, part, _ = out.shape
    rows = keys.shape[1]
    column = lax.axis_index(PAIR)
    own = keys[:part]
    for i in range(1, keys.shape[0] // part):
        own = jnp.where(column == i, keys[i * part : (i + 1) * part], own)
    own = jnp.concatenate([own, jnp.zeros((part, TOK - rows), BF16)], axis=1)
    for i in range(count):
        out[i] = own


def pick_keys(mask, pieces, out):
    block = lax.axis_index(CTX)
    out[...] = jnp.zeros_like(out)

    def step(b, filled):
        wanted = (mask[block, b] == 1) & (b != block)

        @pl.when(wanted)
        def _():
            out[filled] = pieces[b]

        return filled + wanted.astype(jnp.int32)

    lax.fori_loop(0, mask.shape[1], step, 0)


def prepare(queries, weights, wide, mine, low, high, turned):
    heads, width, rows = queries.shape
    for head in range(heads):
        lanes = jnp.concatenate([queries[head], jnp.zeros((width, TOK - rows), BF16)], axis=1)
        wide[head * TOK : (head + 1) * TOK, :] = lanes.T
    for i in range(weights.shape[1] // TOK):
        turned[i * TOK : (i + 1) * TOK, :] = weights[:, i * TOK : (i + 1) * TOK].T
    core = lax.axis_index("core")
    runs, run, _ = mine.shape
    for i in range(runs):
        mine[i] = turned[pl.ds(pl.multiple_of((2 * i + core) * run, run), run), :]
        theirs = turned[pl.ds(pl.multiple_of((2 * i + 1 - core) * run, run), run), :]
        if i < runs // 2:
            low[i] = theirs
        else:
            high[i - runs // 2] = theirs


def route(first, groups, experts, weights, places, shares):
    picks, rows = groups.shape
    slots = places.shape[0]
    count = slots // SLOT
    group = lax.broadcasted_iota(jnp.int32, (count, rows), 0)
    hits = [jnp.where(groups[k : k + 1, :] == group, 1.0, 0.0) for k in range(picks)]
    upto = lax.broadcasted_iota(jnp.int32, (rows, rows), 0)
    upto = jnp.where(upto <= lax.broadcasted_iota(jnp.int32, (rows, rows), 1), 1.0, 0.0)
    rank = dot(sum(hits).astype(BF16), upto.astype(BF16)) - 1.0
    spot = lax.broadcasted_iota(jnp.int32, (count, SLOT, rows), 1).astype(F32)
    here = jnp.where(rank[:, None, :] == spot, 1.0, 0.0)
    lane = lax.broadcasted_iota(jnp.int32, (TOK, rows), 0)
    every = jnp.zeros((slots, rows), F32)
    share = jnp.zeros((slots, TOK), F32)
    for k in range(picks):
        placed = (hits[k][:, None, :] * here).reshape(slots, rows)
        every = every + placed
        table = jnp.zeros((TOK, rows), F32)
        for m in range(experts.shape[1]):
            weight = weights[k, m : m + 1, :].astype(F32)
            table = table + jnp.where(lane == first + experts[k, m : m + 1, :], weight, 0.0)
        share = share + dot_nt(placed.astype(BF16), table.astype(BF16))
    every = jnp.concatenate([every, jnp.zeros((slots, TOK - rows), F32)], axis=1)
    places[...] = every.astype(BF16)
    shares[...] = share.astype(BF16)


def attend(mask, queries, own, up, *refs):
    pieces, (out, held, top, total, acc) = refs[:4], refs[4:]
    block, column = lax.axis_index(CTX), lax.axis_index(PAIR)
    width, rows = own.shape
    part = pieces[0].shape[1]
    inverse_root = width**-0.5
    wide = queries[...]
    query = lax.broadcasted_iota(jnp.int32, (2 * TOK, TOK), 0) % TOK
    key = lax.broadcasted_iota(jnp.int32, (2 * TOK, TOK), 1)

    keys = jnp.concatenate([own[...], jnp.zeros((width, TOK - rows), BF16)], axis=1)
    inside = (key <= query) & (key < rows)
    masked = jnp.where(inside, dot(wide, keys) * inverse_root, MASKED_SCORE)
    best = jnp.max(masked, axis=1, keepdims=True)
    terms = jnp.where(inside, jnp.exp(masked - best), 0.0)
    top[...] = best
    total[...] = jnp.sum(terms, axis=1, keepdims=True)
    acc[...] = dot_nt(terms.astype(BF16), keys)

    def count(b, filled):
        return filled + ((mask[block, b] == 1) & (b != block)).astype(jnp.int32)

    def step(slot, carry):
        for flip, piece in enumerate(pieces):
            start = pl.multiple_of((column ^ flip) * part, part)
            held[pl.ds(start, part), :] = piece[slot]
        inside = key < rows
        masked = jnp.where(inside, dot(wide, held[...]) * inverse_root, MASKED_SCORE)
        old = top[...]
        best = jnp.maximum(old, jnp.max(masked, axis=1, keepdims=True))
        terms = jnp.where(inside, jnp.exp(masked - best), 0.0)
        shrink = jnp.exp(old - best)
        top[...] = best
        total[...] = total[...] * shrink + jnp.sum(terms, axis=1, keepdims=True)
        acc[...] = acc[...] * shrink + dot_nt(terms.astype(BF16), held[...])
        return carry

    lax.fori_loop(0, lax.fori_loop(0, mask.shape[1], count, 0), step, 0)
    inverse = 1.0 / total[...]
    values = []
    for head in range(up.shape[0]):
        span = slice(head * TOK, (head + 1) * TOK)
        latent = acc[span, : up.shape[1]] * inverse[span, :]
        high = latent.astype(BF16)
        low = (latent - high.astype(F32)).astype(BF16)
        values.append((dot(high, up[head]) + dot(low, up[head])).T.astype(BF16))
    out[...] = jnp.concatenate(values, axis=0)


def project_out(mine, theirs, weights_mine, low, high, out):
    half, run, depth = low.shape
    for i, weights_theirs in enumerate((low, high)):
        own = weights_mine[i * half : (i + 1) * half].reshape(half * run, depth)
        total = dot(own, mine[...])
        total = total + dot(weights_theirs[...].reshape(half * run, depth), theirs[...])
        out[i * half : (i + 1) * half] = total.reshape(half, run, TOK).astype(BF16)


def split_pair(value):
    high = value.astype(BF16).astype(F32)
    return high, (value - high).astype(BF16).astype(F32)


def tail_rows(value, count):
    high, low = split_pair(value)
    row = lax.broadcasted_iota(jnp.int32, (count, value.shape[1]), 0)
    return jnp.where(row == 0, high, jnp.where(row == 1, low, 0.0))


def make_rows(parts, residual, gain, places, shares, hidden, sent):
    mixed = jnp.sum(parts[...].astype(F32), axis=0)
    held = (residual[...].astype(F32) + mixed).astype(BF16)
    hidden[...] = held
    wide = held.astype(F32)
    square = jnp.sum(wide * wide, axis=0, keepdims=True)
    run = wide.shape[0]
    rows = jnp.concatenate([wide * gain[...], tail_rows(square, TOK - run)], axis=0).astype(BF16)
    sent[...] = (dot_nt(places[...], rows) + shares[...].astype(F32)).astype(BF16)


def spread_rows(keep_rows, first, got, out, keep, weight):
    turned = got[...].T
    kept = turned[:keep_rows]
    for i in range(out.shape[0]):
        out[i] = kept
    count = keep.shape[0] // 2
    weights = turned[first : first + 16].astype(F32)
    seen = jnp.zeros((1, weights.shape[1]), F32)
    picked = [jnp.zeros((1, weights.shape[1]), F32) for _ in range(2)]
    for expert in range(count):
        row = weights[expert : expert + 1]
        chosen = jnp.where(row > 0.0, 1.0, 0.0)
        for pick in range(2):
            flag = jnp.where(seen == pick, chosen, 0.0)
            keep[2 * expert + pick : 2 * expert + pick + 1, :] = flag
            picked[pick] = picked[pick] + flag * row
        seen = seen + chosen
    weight[...] = jnp.concatenate(picked, axis=0)


def pack(gate, up, down, mine, swapped, far_x, far_z, far_xz, held):
    count = held.shape[0]
    part = gate.shape[2] // count
    for pair in range(held.shape[1]):
        for near in range(count):
            span = slice(near * part, (near + 1) * part)
            pieces = []
            for expert in (2 * pair, 2 * pair + 1):
                pieces += [gate[expert, :, span], up[expert, :, span]]
            pieces += [down[2 * pair, :, span], down[2 * pair + 1, :, span]]
            held[near, pair] = jnp.concatenate(pieces, axis=1)
    near = lax.axis_index(NEAR)
    mine[...] = held[near]
    swapped[...] = held[near ^ 1]
    for out, flip in ((far_x, 2), (far_z, 4), (far_xz, 6)):
        out[0] = held[near ^ flip]
        out[1] = held[near ^ flip ^ 1]


def gather_swap(swapped, far_x, far_z, low, high):
    low[0] = swapped[...]
    low[1] = far_x[1]
    high[...] = far_z[1]


def second_half(got, out):
    out[...] = got[1]


def unpack(part, mine, far_x, far_z, far_xz, low, high, last, into, back):
    pairs = mine.shape[0]
    for pair in range(pairs):
        rows = []
        for i, own in enumerate((mine, far_x, far_z, far_xz)):
            rows.append(own[pair] if i == 0 else own[0, pair])
            rows.append(low[i, pair] if i < 2 else (high, last)[i - 2][pair])
        wide = jnp.concatenate([row[:, : 4 * part] for row in rows], axis=0)
        into[pair * 4 * part : (pair + 1) * 4 * part, :] = wide.T
        for flip, row in enumerate(rows):
            back[flip, :, pair * 2 * part : (pair + 1) * 2 * part] = row[:, 4 * part :]


def project_up(run, sub, inputs, weights, keep, out):
    count, _, slots = inputs.shape
    features = jnp.concatenate(
        [inputs[lax.axis_index(NEAR) ^ flip, :run, :] for flip in range(count)], axis=0
    )
    ends = jnp.sum(inputs[...].astype(F32)[:, run:], axis=0)
    square = ends[0:1] + ends[1:2]
    unit = 2 * sub * out.shape[0]
    sums = [jnp.zeros((unit, slots), F32) for _ in range(2)]
    for expert in range(weights.shape[0] // unit):
        part = dot(weights[expert * unit : (expert + 1) * unit, :], features)
        for pick in range(2):
            sums[pick] = sums[pick] + keep[2 * expert + pick : 2 * expert + pick + 1, :] * part
    tail = tail_rows(square, 8)
    for dest in range(out.shape[0]):
        pieces = []
        for pick in range(2):
            for kind in range(2):
                start = kind * unit // 2 + dest * sub
                pieces.append(sums[pick][start : start + sub])
        out[dest] = jnp.concatenate(pieces + [tail], axis=0).astype(BF16)


def activate(sub, got, weight, out):
    total = jnp.sum(got[...].astype(F32), axis=0)
    square = total[4 * sub : 4 * sub + 1] + total[4 * sub + 1 : 4 * sub + 2]
    scale = lax.rsqrt(square / D + EPSILON)
    pieces = []
    for pick in range(2):
        gate = total[2 * pick * sub : (2 * pick + 1) * sub] * scale
        up = total[(2 * pick + 1) * sub : (2 * pick + 2) * sub] * scale
        act = gate / (1.0 + jnp.exp(-gate)) * up
        pieces.append(act * weight[pick : pick + 1, :])
    rounded = jnp.concatenate(pieces, axis=0).astype(BF16)
    for i in range(out.shape[0]):
        out[i] = rounded


def project_down(sub, acts, keep, weights, out):
    count, _, slots = acts.shape
    wide = acts[...].astype(F32)
    first = wide[:, :sub].reshape(count * sub, slots)
    second = wide[:, sub:].reshape(count * sub, slots)
    picked = []
    for expert in range(keep.shape[0] // 2):
        picked.append(
            (
                keep[2 * expert : 2 * expert + 1, :] * first
                + keep[2 * expert + 1 : 2 * expert + 2, :] * second
            ).astype(BF16)
        )
    stacked = jnp.concatenate(picked, axis=0)
    for flip in range(weights.shape[0]):
        out[lax.axis_index(NEAR) ^ flip] = dot(weights[flip], stacked).astype(BF16)


def finish_rows(got, out):
    total = jnp.sum(got[...].astype(F32), axis=0).astype(BF16)
    run, slots = total.shape
    padded = jnp.concatenate([total, jnp.zeros((TOK - run, slots), BF16)], axis=0)
    out[...] = padded.T


def combine(got, places, hidden, out):
    run, rows = out.shape
    turned = got[...].T[:run]
    added = dot(turned, places[...])
    out[...] = (hidden[...].astype(F32) + added)[:, :rows].astype(BF16)


def exchange(x, axes):
    return lax.all_to_all(x, axes, split_axis=0, concat_axis=0, tiled=True)


def on_device(
    queries,
    latents,
    block_mask,
    value_up,
    out_proj,
    residual,
    norm_gain,
    group_ids,
    expert_ids,
    route_weights,
    w_gate,
    w_up,
    w_down,
):
    ctx_count = lax.axis_size(CTX)
    near_count = lax.axis_size(NEAR)
    far_count = lax.axis_size(FAR)
    block_rows, key_width = latents.shape
    heads = queries.shape[1]
    value_width = value_up.shape[2]
    run = residual.shape[1]
    local_experts, _, hidden_units = w_gate.shape
    pad_rows = TOK - block_rows
    slots = ctx_count * SLOT
    part = hidden_units // near_count
    sub = part // far_count

    quarter = key_width // lax.axis_size(PAIR)
    turned_keys = latents.T
    spread = call(spread_keys, shape((ctx_count, quarter, TOK)), [VMEM])(turned_keys)
    pieces = exchange(spread, CTX)
    apart = jnp.arange(ctx_count)[:, None] != jnp.arange(ctx_count)[None, :]
    named = jnp.sum(jnp.where((block_mask == 1) & apart, 1, 0), axis=1)
    few = jnp.max(named) <= FEW

    first_share = run + 16
    places, slot_shares = call(
        functools.partial(route, first_share), [shape((slots, TOK))] * 2, [VMEM] * 3
    )(group_ids.T, expert_ids.transpose(1, 2, 0), route_weights.transpose(1, 2, 0))

    pairs = local_experts // 2
    block = (pairs, run, 6 * part)
    mine, swapped, far_x, far_z, far_xz = call(
        pack,
        [shape(block)] * 2 + [shape((2,) + block)] * 3,
        [VMEM] * 3,
        [pltpu.VMEM((near_count,) + block, BF16)],
    )(w_gate, w_up, w_down.transpose(0, 2, 1))
    out_proj, far_x, far_z, far_xz = lax.optimization_barrier((out_proj, far_x, far_z, far_xz))

    def flipped(x, flip):
        return lax.ppermute(x, NEAR, [(a, a ^ flip) for a in range(near_count)])

    far_z = flipped(far_z, 4)
    far_x = flipped(far_x, 2)

    runs = D // run
    depth = heads * value_width
    wide_q, out_mine, *out_theirs = call(
        prepare,
        [shape((heads * TOK, key_width)), shape((runs // 2, run, depth))]
        + [shape((runs // 4, run, depth))] * 2,
        [VMEM] * 2,
        [pltpu.VMEM((D, depth), BF16)],
    )(queries.transpose(1, 2, 0), out_proj)
    out_theirs = [lax.ppermute(x, "core", [(0, 1), (1, 0)]) for x in out_theirs]
    resid = jnp.pad(residual.T, ((0, 0), (0, pad_rows)))
    gain = norm_gain.astype(F32)[:, None]
    pieces, few, wide_q, out_mine, out_theirs, far_z, places, slot_shares, resid, gain = (
        lax.optimization_barrier(
            (pieces, few, wide_q, out_mine, out_theirs, far_z, places, slot_shares, resid, gain)
        )
    )

    def attention(held_slots, mask, pieces, wide_q, turned_keys, value_up):
        picked = call(pick_keys, shape((held_slots, quarter, TOK)), [SMEM, VMEM])(mask, pieces)
        across = lax.ppermute(picked, "zb", [(0, 1), (1, 0)])
        beside = lax.ppermute(picked, "core", [(0, 1), (1, 0)])
        corner = lax.ppermute(across, "core", [(0, 1), (1, 0)])
        return call(
            attend,
            shape((depth, TOK)),
            [SMEM] + [VMEM] * 7,
            [
                pltpu.VMEM((key_width, TOK), BF16),
                pltpu.VMEM((heads * TOK, 1), F32),
                pltpu.VMEM((heads * TOK, 1), F32),
                pltpu.VMEM((heads * TOK, key_width), F32),
            ],
        )(mask, wide_q, turned_keys, value_up, picked, beside, across, corner)

    values = lax.cond(
        few,
        functools.partial(attention, FEW),
        functools.partial(attention, ctx_count - 1),
        block_mask,
        pieces,
        wide_q,
        turned_keys,
        value_up,
    )
    other_values = lax.ppermute(values, "core", [(0, 1), (1, 0)])
    summed = call(project_out, shape((runs // 2, run, TOK)), [VMEM] * 5)(
        values, other_values, out_mine, *out_theirs
    )
    summed, swapped, far_xz = lax.optimization_barrier((summed, swapped, far_xz))
    parts = exchange(summed, ZX)
    far_xz = flipped(far_xz, 6)
    low, high = call(gather_swap, [shape((2,) + block), shape(block)], [VMEM] * 3)(
        swapped, far_x, far_z
    )
    low, high = flipped(low, 1), flipped(high, 1)

    hidden, sent = call(make_rows, [shape((run, TOK)), shape((slots, TOK))], [VMEM] * 5)(
        parts,
        resid,
        gain,
        places,
        slot_shares,
    )
    got = exchange(sent.reshape(ctx_count, SLOT, TOK), CTX).reshape(slots, TOK)
    spread, keep, pick_weight = call(
        functools.partial(spread_rows, run + 8, first_share),
        [
            shape((near_count, run + 8, slots)),
            shape((2 * local_experts, slots), F32),
            shape((2, slots), F32),
        ],
        [VMEM],
    )(got)
    spread, low, high, far_xz = lax.optimization_barrier((spread, low, high, far_xz))
    inputs = exchange(spread, NEAR)
    last = flipped(call(second_half, shape(block), [VMEM])(far_xz), 1)
    weights_in, weights_back = call(
        functools.partial(unpack, part),
        [
            shape((pairs * 4 * part, near_count * run)),
            shape((near_count, run, local_experts * part)),
        ],
        [VMEM] * 7,
    )(mine, far_x, far_z, far_xz, low, high, last)
    partial_sums = call(
        functools.partial(project_up, run, sub),
        shape((far_count, 4 * sub + 8, slots)),
        [VMEM] * 3,
    )(inputs, weights_in, keep)
    acts = call(functools.partial(activate, sub), shape((far_count, 2 * sub, slots)), [VMEM] * 2)(
        exchange(partial_sums, FAR), pick_weight
    )
    outputs = call(
        functools.partial(project_down, sub),
        shape((near_count, run, slots)),
        [VMEM] * 3,
    )(exchange(acts, FAR), keep, weights_back)
    returned = call(finish_rows, shape((slots, TOK)), [VMEM])(exchange(outputs, NEAR))
    returned = exchange(returned.reshape(ctx_count, SLOT, TOK), CTX).reshape(slots, TOK)
    out = call(combine, shape((run, block_rows)), [VMEM] * 3)(returned, places, hidden)
    return out.T


def solution(mesh):
    names = ("y", "xh", "za", "zb", "xl", "core")
    fine = Mesh(mesh.devices.reshape(8, 2, 4, 2, 2, 2), names)
    return jax.shard_map(
        on_device,
        mesh=fine,
        in_specs=(
            P(CTX, EXP, None),
            P(CTX, None),
            P(),
            P(EXP, None, None),
            P(EXP, None),
            P(CTX, EXP),
            P(EXP),
            P(CTX, None),
            P(CTX, None, None),
            P(CTX, None, None),
            P(CTX, EXP, None),
            P(CTX, EXP, None),
            P(CTX, None, EXP),
        ),
        out_specs=P(CTX, EXP),
        check_vma=False,
    )
```

```python
import functools

import jax
import jax.numpy as jnp
from jax import lax
from jax.experimental import pallas as pl
from jax.experimental.pallas import tpu as pltpu
from jax.sharding import Mesh
from jax.sharding import PartitionSpec as P

D = 2560
EPSILON = 1e-06
MASKED_SCORE = -1e30
CTX = ("y", "xh")
EXP = ("za", "zb", "xl", "core")
ZX = ("za", "zb", "xl")
PAIR = ("zb", "core")
NEAR = ("zb", "xl", "core")
FAR = "za"
TOK = 128
SLOT = 32
FEW = 5
F32 = jnp.float32
BF16 = jnp.bfloat16
VMEM = pl.BlockSpec(memory_space=pltpu.VMEM)
SMEM = pl.BlockSpec(memory_space=pltpu.SMEM)


def call(body, out_shape, in_specs, scratch=(), flops=0, limit=40):
    many = isinstance(out_shape, (tuple, list))
    return pl.pallas_call(
        body,
        out_shape=out_shape,
        in_specs=in_specs,
        out_specs=[VMEM] * len(out_shape) if many else VMEM,
        scratch_shapes=scratch,
        compiler_params=pltpu.CompilerParams(vmem_limit_bytes=limit << 20),
    )


def shape(dims, dtype=BF16):
    return jax.ShapeDtypeStruct(dims, dtype)


def dot(a, b):
    return jnp.dot(a, b, preferred_element_type=F32)


def dot_nt(a, b):
    return lax.dot_general(a, b, (((1,), (1,)), ((), ())), preferred_element_type=F32)


def spread_keys(keys, out):
    count, part, _ = out.shape
    rows = keys.shape[1]
    column = lax.axis_index(PAIR)
    own = keys[:part]
    for i in range(1, keys.shape[0] // part):
        own = jnp.where(column == i, keys[i * part : (i + 1) * part], own)
    own = jnp.concatenate([own, jnp.zeros((part, TOK - rows), BF16)], axis=1)
    for i in range(count):
        out[i] = own


def pick_keys(mask, pieces, out):
    block = lax.axis_index(CTX)
    out[...] = jnp.zeros_like(out)

    def step(b, filled):
        wanted = (mask[block, b] == 1) & (b != block)

        @pl.when(wanted)
        def _():
            out[filled] = pieces[b]

        return filled + wanted.astype(jnp.int32)

    lax.fori_loop(0, mask.shape[1], step, 0)


def prepare(queries, weights, wide, mine, low, high, turned):
    heads, width, rows = queries.shape
    for head in range(heads):
        lanes = jnp.concatenate([queries[head], jnp.zeros((width, TOK - rows), BF16)], axis=1)
        wide[head * TOK : (head + 1) * TOK, :] = lanes.T
    for i in range(weights.shape[1] // TOK):
        turned[i * TOK : (i + 1) * TOK, :] = weights[:, i * TOK : (i + 1) * TOK].T
    core = lax.axis_index("core")
    runs, run, _ = mine.shape
    for i in range(runs):
        mine[i] = turned[pl.ds(pl.multiple_of((2 * i + core) * run, run), run), :]
        theirs = turned[pl.ds(pl.multiple_of((2 * i + 1 - core) * run, run), run), :]
        if i < runs // 2:
            low[i] = theirs
        else:
            high[i - runs // 2] = theirs


def route(first, groups, experts, weights, places, shares):
    picks, rows = groups.shape
    slots = places.shape[0]
    count = slots // SLOT
    group = lax.broadcasted_iota(jnp.int32, (count, rows), 0)
    hits = [jnp.where(groups[k : k + 1, :] == group, 1.0, 0.0) for k in range(picks)]
    upto = lax.broadcasted_iota(jnp.int32, (rows, rows), 0)
    upto = jnp.where(upto <= lax.broadcasted_iota(jnp.int32, (rows, rows), 1), 1.0, 0.0)
    rank = dot(sum(hits).astype(BF16), upto.astype(BF16)) - 1.0
    spot = lax.broadcasted_iota(jnp.int32, (count, SLOT, rows), 1).astype(F32)
    here = jnp.where(rank[:, None, :] == spot, 1.0, 0.0)
    lane = lax.broadcasted_iota(jnp.int32, (TOK, rows), 0)
    every = jnp.zeros((slots, rows), F32)
    share = jnp.zeros((slots, TOK), F32)
    for k in range(picks):
        placed = (hits[k][:, None, :] * here).reshape(slots, rows)
        every = every + placed
        table = jnp.zeros((TOK, rows), F32)
        for m in range(experts.shape[1]):
            weight = weights[k, m : m + 1, :].astype(F32)
            table = table + jnp.where(lane == first + experts[k, m : m + 1, :], weight, 0.0)
        share = share + dot_nt(placed.astype(BF16), table.astype(BF16))
    every = jnp.concatenate([every, jnp.zeros((slots, TOK - rows), F32)], axis=1)
    places[...] = every.astype(BF16)
    shares[...] = share.astype(BF16)


def attend(mask, queries, own, up, *refs):
    pieces, (out, held) = refs[:4], refs[4:]
    block, column = lax.axis_index(CTX), lax.axis_index(PAIR)
    width, rows = own.shape
    slots, part, _ = pieces[0].shape
    keys = TOK * (slots + 1)

    def count(b, filled):
        return filled + ((mask[block, b] == 1) & (b != block)).astype(jnp.int32)

    filled = lax.fori_loop(0, mask.shape[1], count, 0)
    held[:, :TOK] = jnp.concatenate([own[...], jnp.zeros((width, TOK - rows), BF16)], axis=1)
    for slot in range(slots):
        for flip, piece in enumerate(pieces):
            start = pl.multiple_of((column ^ flip) * part, part)
            held[pl.ds(start, part), (slot + 1) * TOK : (slot + 2) * TOK] = piece[slot]
    query = lax.broadcasted_iota(jnp.int32, (2 * TOK, keys), 0) % TOK
    lane = lax.broadcasted_iota(jnp.int32, (2 * TOK, keys), 1)
    key = lane % TOK
    limit = jnp.where(lane < TOK, query + 1, jnp.where(lane < (filled + 1) * TOK, rows, 0))
    inside = key < jnp.minimum(limit, rows)
    masked = jnp.where(inside, dot(queries[...], held[...]) * width**-0.5, MASKED_SCORE)
    terms = jnp.where(inside, jnp.exp(masked - jnp.max(masked, axis=1, keepdims=True)), 0.0)
    inverse = 1.0 / jnp.sum(terms, axis=1, keepdims=True)
    latent = dot_nt(terms.astype(BF16), held[: up.shape[1], :]) * inverse
    high = latent.astype(BF16)
    low = (latent - high.astype(F32)).astype(BF16)
    values = []
    for head in range(up.shape[0]):
        span = slice(head * TOK, (head + 1) * TOK)
        values.append((dot(high[span], up[head]) + dot(low[span], up[head])).T.astype(BF16))
    out[...] = jnp.concatenate(values, axis=0)


def project_out(mine, theirs, weights_mine, low, high, out):
    half, run, depth = low.shape
    for i, weights_theirs in enumerate((low, high)):
        own = weights_mine[i * half : (i + 1) * half].reshape(half * run, depth)
        total = dot(own, mine[...])
        total = total + dot(weights_theirs[...].reshape(half * run, depth), theirs[...])
        out[i * half : (i + 1) * half] = total.reshape(half, run, TOK).astype(BF16)


def split_pair(value):
    high = value.astype(BF16).astype(F32)
    return high, (value - high).astype(BF16).astype(F32)


def tail_rows(value, count):
    high, low = split_pair(value)
    row = lax.broadcasted_iota(jnp.int32, (count, value.shape[1]), 0)
    return jnp.where(row == 0, high, jnp.where(row == 1, low, 0.0))


def make_rows(parts, residual, gain, places, shares, hidden, sent):
    mixed = jnp.sum(parts[...].astype(F32), axis=0)
    held = (residual[...].astype(F32) + mixed).astype(BF16)
    hidden[...] = held
    wide = held.astype(F32)
    square = jnp.sum(wide * wide, axis=0, keepdims=True)
    run = wide.shape[0]
    rows = jnp.concatenate([wide * gain[...], tail_rows(square, TOK - run)], axis=0).astype(BF16)
    sent[...] = (dot_nt(places[...], rows) + shares[...].astype(F32)).astype(BF16)


def spread_rows(keep_rows, first, got, out, keep, weight):
    turned = got[...].T
    kept = turned[:keep_rows]
    for i in range(out.shape[0]):
        out[i] = kept
    count = keep.shape[0] // 2
    weights = turned[first : first + 16].astype(F32)
    seen = jnp.zeros((1, weights.shape[1]), F32)
    picked = [jnp.zeros((1, weights.shape[1]), F32) for _ in range(2)]
    for expert in range(count):
        row = weights[expert : expert + 1]
        chosen = jnp.where(row > 0.0, 1.0, 0.0)
        for pick in range(2):
            flag = jnp.where(seen == pick, chosen, 0.0)
            keep[2 * expert + pick : 2 * expert + pick + 1, :] = flag
            picked[pick] = picked[pick] + flag * row
        seen = seen + chosen
    weight[...] = jnp.concatenate(picked, axis=0)


def pack(gate, up, down, mine, swapped, far_x, far_z, far_xz, held):
    count = held.shape[0]
    part = gate.shape[2] // count
    for pair in range(held.shape[1]):
        for near in range(count):
            span = slice(near * part, (near + 1) * part)
            pieces = []
            for expert in (2 * pair, 2 * pair + 1):
                pieces += [gate[expert, :, span], up[expert, :, span]]
            pieces += [down[2 * pair, :, span], down[2 * pair + 1, :, span]]
            held[near, pair] = jnp.concatenate(pieces, axis=1)
    near = lax.axis_index(NEAR)
    mine[...] = held[near]
    swapped[...] = held[near ^ 1]
    for out, flip in ((far_x, 2), (far_z, 4), (far_xz, 6)):
        out[0] = held[near ^ flip]
        out[1] = held[near ^ flip ^ 1]


def gather_swap(swapped, far_x, far_z, low, high):
    low[0] = swapped[...]
    low[1] = far_x[1]
    high[...] = far_z[1]


def second_half(got, out):
    out[...] = got[1]


def unpack(part, mine, far_x, far_z, far_xz, low, high, last, into, back):
    pairs = mine.shape[0]
    for pair in range(pairs):
        rows = []
        for i, own in enumerate((mine, far_x, far_z, far_xz)):
            rows.append(own[pair] if i == 0 else own[0, pair])
            rows.append(low[i, pair] if i < 2 else (high, last)[i - 2][pair])
        wide = jnp.concatenate([row[:, : 4 * part] for row in rows], axis=0)
        into[pair * 4 * part : (pair + 1) * 4 * part, :] = wide.T
        for flip, row in enumerate(rows):
            back[flip, :, pair * 2 * part : (pair + 1) * 2 * part] = row[:, 4 * part :]


def project_up(run, sub, inputs, weights, keep, out):
    count, _, slots = inputs.shape
    features = jnp.concatenate(
        [inputs[lax.axis_index(NEAR) ^ flip, :run, :] for flip in range(count)], axis=0
    )
    ends = jnp.sum(inputs[...].astype(F32)[:, run:], axis=0)
    square = ends[0:1] + ends[1:2]
    unit = 2 * sub * out.shape[0]
    sums = [jnp.zeros((unit, slots), F32) for _ in range(2)]
    for expert in range(weights.shape[0] // unit):
        part = dot(weights[expert * unit : (expert + 1) * unit, :], features)
        for pick in range(2):
            sums[pick] = sums[pick] + keep[2 * expert + pick : 2 * expert + pick + 1, :] * part
    tail = tail_rows(square, 8)
    for dest in range(out.shape[0]):
        pieces = []
        for pick in range(2):
            for kind in range(2):
                start = kind * unit // 2 + dest * sub
                pieces.append(sums[pick][start : start + sub])
        out[dest] = jnp.concatenate(pieces + [tail], axis=0).astype(BF16)


def activate(sub, got, weight, out):
    total = jnp.sum(got[...].astype(F32), axis=0)
    square = total[4 * sub : 4 * sub + 1] + total[4 * sub + 1 : 4 * sub + 2]
    scale = lax.rsqrt(square / D + EPSILON)
    pieces = []
    for pick in range(2):
        gate = total[2 * pick * sub : (2 * pick + 1) * sub] * scale
        up = total[(2 * pick + 1) * sub : (2 * pick + 2) * sub] * scale
        act = gate / (1.0 + jnp.exp(-gate)) * up
        pieces.append(act * weight[pick : pick + 1, :])
    rounded = jnp.concatenate(pieces, axis=0).astype(BF16)
    for i in range(out.shape[0]):
        out[i] = rounded


def project_down(sub, acts, keep, weights, out):
    count, _, slots = acts.shape
    wide = acts[...].astype(F32)
    first = wide[:, :sub].reshape(count * sub, slots)
    second = wide[:, sub:].reshape(count * sub, slots)
    picked = []
    for expert in range(keep.shape[0] // 2):
        picked.append(
            (
                keep[2 * expert : 2 * expert + 1, :] * first
                + keep[2 * expert + 1 : 2 * expert + 2, :] * second
            ).astype(BF16)
        )
    stacked = jnp.concatenate(picked, axis=0)
    for flip in range(weights.shape[0]):
        out[lax.axis_index(NEAR) ^ flip] = dot(weights[flip], stacked).astype(BF16)


def finish_rows(got, out):
    total = jnp.sum(got[...].astype(F32), axis=0).astype(BF16)
    run, slots = total.shape
    padded = jnp.concatenate([total, jnp.zeros((TOK - run, slots), BF16)], axis=0)
    out[...] = padded.T


def combine(got, places, hidden, out):
    run, rows = out.shape
    turned = got[...].T[:run]
    added = dot(turned, places[...])
    out[...] = (hidden[...].astype(F32) + added)[:, :rows].astype(BF16)


def exchange(x, axes):
    return lax.all_to_all(x, axes, split_axis=0, concat_axis=0, tiled=True)


def on_device(
    queries,
    latents,
    block_mask,
    value_up,
    out_proj,
    residual,
    norm_gain,
    group_ids,
    expert_ids,
    route_weights,
    w_gate,
    w_up,
    w_down,
):
    ctx_count = lax.axis_size(CTX)
    near_count = lax.axis_size(NEAR)
    far_count = lax.axis_size(FAR)
    block_rows, key_width = latents.shape
    heads = queries.shape[1]
    value_width = value_up.shape[2]
    run = residual.shape[1]
    local_experts, _, hidden_units = w_gate.shape
    pad_rows = TOK - block_rows
    slots = ctx_count * SLOT
    part = hidden_units // near_count
    sub = part // far_count

    quarter = key_width // lax.axis_size(PAIR)
    turned_keys = latents.T
    spread = call(spread_keys, shape((ctx_count, quarter, TOK)), [VMEM])(turned_keys)
    pieces = exchange(spread, CTX)
    apart = jnp.arange(ctx_count)[:, None] != jnp.arange(ctx_count)[None, :]
    named = jnp.sum(jnp.where((block_mask == 1) & apart, 1, 0), axis=1)
    few = jnp.max(named) <= FEW

    first_share = run + 16
    places, slot_shares = call(
        functools.partial(route, first_share), [shape((slots, TOK))] * 2, [VMEM] * 3
    )(group_ids.T, expert_ids.transpose(1, 2, 0), route_weights.transpose(1, 2, 0))

    pairs = local_experts // 2
    block = (pairs, run, 6 * part)
    mine, swapped, far_x, far_z, far_xz = call(
        pack,
        [shape(block)] * 2 + [shape((2,) + block)] * 3,
        [VMEM] * 3,
        [pltpu.VMEM((near_count,) + block, BF16)],
    )(w_gate, w_up, w_down.transpose(0, 2, 1))
    out_proj, far_x, far_z, far_xz = lax.optimization_barrier((out_proj, far_x, far_z, far_xz))

    def flipped(x, flip):
        return lax.ppermute(x, NEAR, [(a, a ^ flip) for a in range(near_count)])

    far_z = flipped(far_z, 4)
    far_x = flipped(far_x, 2)

    runs = D // run
    depth = heads * value_width
    wide_q, out_mine, *out_theirs = call(
        prepare,
        [shape((heads * TOK, key_width)), shape((runs // 2, run, depth))]
        + [shape((runs // 4, run, depth))] * 2,
        [VMEM] * 2,
        [pltpu.VMEM((D, depth), BF16)],
    )(queries.transpose(1, 2, 0), out_proj)
    out_theirs = [lax.ppermute(x, "core", [(0, 1), (1, 0)]) for x in out_theirs]
    resid = jnp.pad(residual.T, ((0, 0), (0, pad_rows)))
    gain = norm_gain.astype(F32)[:, None]
    pieces, few, wide_q, out_mine, out_theirs, places, slot_shares, resid, gain = (
        lax.optimization_barrier(
            (pieces, few, wide_q, out_mine, out_theirs, places, slot_shares, resid, gain)
        )
    )

    def attention(held_slots, mask, pieces, wide_q, turned_keys, value_up):
        picked = call(pick_keys, shape((held_slots, quarter, TOK)), [SMEM, VMEM])(mask, pieces)
        across = lax.ppermute(picked, "zb", [(0, 1), (1, 0)])
        beside = lax.ppermute(picked, "core", [(0, 1), (1, 0)])
        corner = lax.ppermute(across, "core", [(0, 1), (1, 0)])
        return call(
            attend,
            shape((depth, TOK)),
            [SMEM] + [VMEM] * 7,
            [pltpu.VMEM((key_width, TOK * (held_slots + 1)), BF16)],
        )(mask, wide_q, turned_keys, value_up, picked, beside, across, corner)

    values = lax.cond(
        few,
        functools.partial(attention, FEW),
        functools.partial(attention, ctx_count - 1),
        block_mask,
        pieces,
        wide_q,
        turned_keys,
        value_up,
    )
    values, far_z = lax.optimization_barrier((values, far_z))
    other_values = lax.ppermute(values, "core", [(0, 1), (1, 0)])
    summed = call(project_out, shape((runs // 2, run, TOK)), [VMEM] * 5)(
        values, other_values, out_mine, *out_theirs
    )
    summed, swapped, far_xz = lax.optimization_barrier((summed, swapped, far_xz))
    parts = exchange(summed, ZX)
    far_xz = flipped(far_xz, 6)
    low, high = call(gather_swap, [shape((2,) + block), shape(block)], [VMEM] * 3)(
        swapped, far_x, far_z
    )
    low, high = flipped(low, 1), flipped(high, 1)

    hidden, sent = call(make_rows, [shape((run, TOK)), shape((slots, TOK))], [VMEM] * 5)(
        parts,
        resid,
        gain,
        places,
        slot_shares,
    )
    got = exchange(sent.reshape(ctx_count, SLOT, TOK), CTX).reshape(slots, TOK)
    spread, keep, pick_weight = call(
        functools.partial(spread_rows, run + 8, first_share),
        [
            shape((near_count, run + 8, slots)),
            shape((2 * local_experts, slots), F32),
            shape((2, slots), F32),
        ],
        [VMEM],
    )(got)
    spread, low, high, far_xz = lax.optimization_barrier((spread, low, high, far_xz))
    inputs = exchange(spread, NEAR)
    last = flipped(call(second_half, shape(block), [VMEM])(far_xz), 1)
    weights_in, weights_back = call(
        functools.partial(unpack, part),
        [
            shape((pairs * 4 * part, near_count * run)),
            shape((near_count, run, local_experts * part)),
        ],
        [VMEM] * 7,
    )(mine, far_x, far_z, far_xz, low, high, last)
    partial_sums = call(
        functools.partial(project_up, run, sub),
        shape((far_count, 4 * sub + 8, slots)),
        [VMEM] * 3,
    )(inputs, weights_in, keep)
    acts = call(functools.partial(activate, sub), shape((far_count, 2 * sub, slots)), [VMEM] * 2)(
        exchange(partial_sums, FAR), pick_weight
    )
    outputs = call(
        functools.partial(project_down, sub),
        shape((near_count, run, slots)),
        [VMEM] * 3,
    )(exchange(acts, FAR), keep, weights_back)
    returned = call(finish_rows, shape((slots, TOK)), [VMEM])(exchange(outputs, NEAR))
    returned = exchange(returned.reshape(ctx_count, SLOT, TOK), CTX).reshape(slots, TOK)
    out = call(combine, shape((run, block_rows)), [VMEM] * 3)(returned, places, hidden)
    return out.T


def solution(mesh):
    names = ("y", "xh", "za", "zb", "xl", "core")
    fine = Mesh(mesh.devices.reshape(8, 2, 4, 2, 2, 2), names)
    return jax.shard_map(
        on_device,
        mesh=fine,
        in_specs=(
            P(CTX, EXP, None),
            P(CTX, None),
            P(),
            P(EXP, None, None),
            P(EXP, None),
            P(CTX, EXP),
            P(EXP),
            P(CTX, None),
            P(CTX, None, None),
            P(CTX, None, None),
            P(CTX, EXP, None),
            P(CTX, EXP, None),
            P(CTX, None, EXP),
        ),
        out_specs=P(CTX, EXP),
        check_vma=False,
    )
```

```python
import functools

import jax
import jax.numpy as jnp
from jax import lax
from jax.experimental import pallas as pl
from jax.experimental.pallas import tpu as pltpu
from jax.sharding import Mesh
from jax.sharding import PartitionSpec as P

D = 2560
EPSILON = 1e-06
MASKED_SCORE = -1e30
CTX = ("y", "xh")
EXP = ("za", "zb", "xl", "core")
ZX = ("za", "zb", "xl")
PAIR = ("zb", "core")
NEAR = ("zb", "xl", "core")
FAR = "za"
TOK = 128
SLOT = 32
FEW = 5
F32 = jnp.float32
BF16 = jnp.bfloat16
VMEM = pl.BlockSpec(memory_space=pltpu.VMEM)
SMEM = pl.BlockSpec(memory_space=pltpu.SMEM)


def call(body, out_shape, in_specs, scratch=(), flops=0, limit=40):
    many = isinstance(out_shape, (tuple, list))
    return pl.pallas_call(
        body,
        out_shape=out_shape,
        in_specs=in_specs,
        out_specs=[VMEM] * len(out_shape) if many else VMEM,
        scratch_shapes=scratch,
        compiler_params=pltpu.CompilerParams(vmem_limit_bytes=limit << 20),
    )


def shape(dims, dtype=BF16):
    return jax.ShapeDtypeStruct(dims, dtype)


def dot(a, b):
    return jnp.dot(a, b, preferred_element_type=F32)


def dot_nt(a, b):
    return lax.dot_general(a, b, (((1,), (1,)), ((), ())), preferred_element_type=F32)


def spread_keys(keys, out):
    count, part, _ = out.shape
    rows = keys.shape[1]
    column = lax.axis_index(PAIR)
    own = keys[:part]
    for i in range(1, keys.shape[0] // part):
        own = jnp.where(column == i, keys[i * part : (i + 1) * part], own)
    own = jnp.concatenate([own, jnp.zeros((part, TOK - rows), BF16)], axis=1)
    for i in range(count):
        out[i] = own


def pick_keys(mask, pieces, out):
    block = lax.axis_index(CTX)
    out[...] = jnp.zeros_like(out)

    def step(b, filled):
        wanted = (mask[block, b] == 1) & (b != block)

        @pl.when(wanted)
        def _():
            out[filled] = pieces[b]

        return filled + wanted.astype(jnp.int32)

    lax.fori_loop(0, mask.shape[1], step, 0)


def prepare(queries, weights, wide, mine, low, high, turned):
    heads, width, rows = queries.shape
    for head in range(heads):
        lanes = jnp.concatenate([queries[head], jnp.zeros((width, TOK - rows), BF16)], axis=1)
        wide[head * TOK : (head + 1) * TOK, :] = lanes.T
    for i in range(weights.shape[1] // TOK):
        turned[i * TOK : (i + 1) * TOK, :] = weights[:, i * TOK : (i + 1) * TOK].T
    core = lax.axis_index("core")
    runs, run, _ = mine.shape
    for i in range(runs):
        mine[i] = turned[pl.ds(pl.multiple_of((2 * i + core) * run, run), run), :]
        theirs = turned[pl.ds(pl.multiple_of((2 * i + 1 - core) * run, run), run), :]
        if i < runs // 2:
            low[i] = theirs
        else:
            high[i - runs // 2] = theirs


def route(first, groups, experts, weights, places, shares):
    picks, rows = groups.shape
    slots = places.shape[0]
    count = slots // SLOT
    group = lax.broadcasted_iota(jnp.int32, (count, rows), 0)
    hits = [jnp.where(groups[k : k + 1, :] == group, 1.0, 0.0) for k in range(picks)]
    upto = lax.broadcasted_iota(jnp.int32, (rows, rows), 0)
    upto = jnp.where(upto <= lax.broadcasted_iota(jnp.int32, (rows, rows), 1), 1.0, 0.0)
    rank = dot(sum(hits).astype(BF16), upto.astype(BF16)) - 1.0
    spot = lax.broadcasted_iota(jnp.int32, (count, SLOT, rows), 1).astype(F32)
    here = jnp.where(rank[:, None, :] == spot, 1.0, 0.0)
    lane = lax.broadcasted_iota(jnp.int32, (TOK, rows), 0)
    every = jnp.zeros((slots, rows), F32)
    share = jnp.zeros((slots, TOK), F32)
    for k in range(picks):
        placed = (hits[k][:, None, :] * here).reshape(slots, rows)
        every = every + placed
        table = jnp.zeros((TOK, rows), F32)
        for m in range(experts.shape[1]):
            weight = weights[k, m : m + 1, :].astype(F32)
            table = table + jnp.where(lane == first + experts[k, m : m + 1, :], weight, 0.0)
        share = share + dot_nt(placed.astype(BF16), table.astype(BF16))
    every = jnp.concatenate([every, jnp.zeros((slots, TOK - rows), F32)], axis=1)
    places[...] = every.astype(BF16)
    shares[...] = share.astype(BF16)


def attend(mask, queries, own, up, *refs):
    pieces, (out, held) = refs[:4], refs[4:]
    block, column = lax.axis_index(CTX), lax.axis_index(PAIR)
    width, rows = own.shape
    slots, part, _ = pieces[0].shape
    keys = TOK * (slots + 1)

    def count(b, filled):
        return filled + ((mask[block, b] == 1) & (b != block)).astype(jnp.int32)

    filled = lax.fori_loop(0, mask.shape[1], count, 0)
    held[:, :TOK] = jnp.concatenate([own[...], jnp.zeros((width, TOK - rows), BF16)], axis=1)
    for slot in range(slots):
        for flip, piece in enumerate(pieces):
            start = pl.multiple_of((column ^ flip) * part, part)
            held[pl.ds(start, part), (slot + 1) * TOK : (slot + 2) * TOK] = piece[slot]
    query = lax.broadcasted_iota(jnp.int32, (2 * TOK, keys), 0) % TOK
    lane = lax.broadcasted_iota(jnp.int32, (2 * TOK, keys), 1)
    key = lane % TOK
    limit = jnp.where(lane < TOK, query + 1, jnp.where(lane < (filled + 1) * TOK, rows, 0))
    inside = key < jnp.minimum(limit, rows)
    masked = jnp.where(inside, dot(queries[...], held[...]) * width**-0.5, MASKED_SCORE)
    terms = jnp.where(inside, jnp.exp(masked - jnp.max(masked, axis=1, keepdims=True)), 0.0)
    inverse = 1.0 / jnp.sum(terms, axis=1, keepdims=True)
    latent = dot_nt(terms.astype(BF16), held[: up.shape[1], :]) * inverse
    high = latent.astype(BF16)
    low = (latent - high.astype(F32)).astype(BF16)
    values = []
    for head in range(up.shape[0]):
        span = slice(head * TOK, (head + 1) * TOK)
        values.append((dot(high[span], up[head]) + dot(low[span], up[head])).T.astype(BF16))
    out[...] = jnp.concatenate(values, axis=0)


def project_out(mine, theirs, weights_mine, low, high, out):
    half, run, depth = low.shape
    for i, weights_theirs in enumerate((low, high)):
        own = weights_mine[i * half : (i + 1) * half].reshape(half * run, depth)
        total = dot(own, mine[...])
        total = total + dot(weights_theirs[...].reshape(half * run, depth), theirs[...])
        out[i * half : (i + 1) * half] = total.reshape(half, run, TOK).astype(BF16)


def split_pair(value):
    high = value.astype(BF16).astype(F32)
    return high, (value - high).astype(BF16).astype(F32)


def tail_rows(value, count):
    high, low = split_pair(value)
    row = lax.broadcasted_iota(jnp.int32, (count, value.shape[1]), 0)
    return jnp.where(row == 0, high, jnp.where(row == 1, low, 0.0))


def make_rows(parts, residual, gain, places, shares, hidden, sent):
    mixed = jnp.sum(parts[...].astype(F32), axis=0)
    held = (residual[...].astype(F32) + mixed).astype(BF16)
    hidden[...] = held
    wide = held.astype(F32)
    square = jnp.sum(wide * wide, axis=0, keepdims=True)
    run = wide.shape[0]
    rows = jnp.concatenate([wide * gain[...], tail_rows(square, TOK - run)], axis=0).astype(BF16)
    sent[...] = (dot_nt(places[...], rows) + shares[...].astype(F32)).astype(BF16)


def spread_rows(keep_rows, first, got, out, keep, weight):
    turned = got[...].T
    kept = turned[:keep_rows]
    for i in range(out.shape[0]):
        out[i] = kept
    count = keep.shape[0] // 2
    weights = turned[first : first + 16].astype(F32)
    seen = jnp.zeros((1, weights.shape[1]), F32)
    picked = [jnp.zeros((1, weights.shape[1]), F32) for _ in range(2)]
    for expert in range(count):
        row = weights[expert : expert + 1]
        chosen = jnp.where(row > 0.0, 1.0, 0.0)
        for pick in range(2):
            flag = jnp.where(seen == pick, chosen, 0.0)
            keep[2 * expert + pick : 2 * expert + pick + 1, :] = flag
            picked[pick] = picked[pick] + flag * row
        seen = seen + chosen
    weight[...] = jnp.concatenate(picked, axis=0)


def pack(gate, up, down, mine, swapped, far_x, far_z, far_xz, held):
    count = held.shape[0]
    part = gate.shape[2] // count
    for pair in range(held.shape[1]):
        for near in range(count):
            span = slice(near * part, (near + 1) * part)
            pieces = []
            for expert in (2 * pair, 2 * pair + 1):
                pieces += [gate[expert, :, span], up[expert, :, span]]
            pieces += [down[2 * pair, :, span], down[2 * pair + 1, :, span]]
            held[near, pair] = jnp.concatenate(pieces, axis=1)
    near = lax.axis_index(NEAR)
    mine[...] = held[near]
    swapped[...] = held[near ^ 1]
    for out, flip in ((far_x, 2), (far_z, 4), (far_xz, 6)):
        out[0] = held[near ^ flip]
        out[1] = held[near ^ flip ^ 1]


def gather_swap(swapped, far_x, far_z, low, high):
    low[0] = swapped[...]
    low[1] = far_x[1]
    high[...] = far_z[1]


def second_half(got, out):
    out[...] = got[1]


def unpack(part, mine, far_x, far_z, far_xz, low, high, last, into, back):
    pairs = mine.shape[0]
    for pair in range(pairs):
        rows = []
        for i, own in enumerate((mine, far_x, far_z, far_xz)):
            rows.append(own[pair] if i == 0 else own[0, pair])
            rows.append(low[i, pair] if i < 2 else (high, last)[i - 2][pair])
        wide = jnp.concatenate([row[:, : 4 * part] for row in rows], axis=0)
        into[pair * 4 * part : (pair + 1) * 4 * part, :] = wide.T
        for flip, row in enumerate(rows):
            back[flip, :, pair * 2 * part : (pair + 1) * 2 * part] = row[:, 4 * part :]


def project_up(run, sub, inputs, weights, keep, out):
    count, _, slots = inputs.shape
    features = jnp.concatenate(
        [inputs[lax.axis_index(NEAR) ^ flip, :run, :] for flip in range(count)], axis=0
    )
    ends = jnp.sum(inputs[...].astype(F32)[:, run:], axis=0)
    square = ends[0:1] + ends[1:2]
    unit = 2 * sub * out.shape[0]
    sums = [jnp.zeros((unit, slots), F32) for _ in range(2)]
    for expert in range(weights.shape[0] // unit):
        part = dot(weights[expert * unit : (expert + 1) * unit, :], features)
        for pick in range(2):
            sums[pick] = sums[pick] + keep[2 * expert + pick : 2 * expert + pick + 1, :] * part
    tail = tail_rows(square, 8)
    for dest in range(out.shape[0]):
        pieces = []
        for pick in range(2):
            for kind in range(2):
                start = kind * unit // 2 + dest * sub
                pieces.append(sums[pick][start : start + sub])
        out[dest] = jnp.concatenate(pieces + [tail], axis=0).astype(BF16)


def activate(sub, got, weight, out):
    total = jnp.sum(got[...].astype(F32), axis=0)
    square = total[4 * sub : 4 * sub + 1] + total[4 * sub + 1 : 4 * sub + 2]
    scale = lax.rsqrt(square / D + EPSILON)
    pieces = []
    for pick in range(2):
        gate = total[2 * pick * sub : (2 * pick + 1) * sub] * scale
        up = total[(2 * pick + 1) * sub : (2 * pick + 2) * sub] * scale
        act = gate / (1.0 + jnp.exp(-gate)) * up
        pieces.append(act * weight[pick : pick + 1, :])
    rounded = jnp.concatenate(pieces, axis=0).astype(BF16)
    for i in range(out.shape[0]):
        out[i] = rounded


def project_down(sub, acts, keep, weights, out):
    count, _, slots = acts.shape
    wide = acts[...].astype(F32)
    first = wide[:, :sub].reshape(count * sub, slots)
    second = wide[:, sub:].reshape(count * sub, slots)
    picked = []
    for expert in range(keep.shape[0] // 2):
        picked.append(
            (
                keep[2 * expert : 2 * expert + 1, :] * first
                + keep[2 * expert + 1 : 2 * expert + 2, :] * second
            ).astype(BF16)
        )
    stacked = jnp.concatenate(picked, axis=0)
    for flip in range(weights.shape[0]):
        out[lax.axis_index(NEAR) ^ flip] = dot(weights[flip], stacked).astype(BF16)


def finish_rows(got, out):
    total = jnp.sum(got[...].astype(F32), axis=0).astype(BF16)
    run, slots = total.shape
    padded = jnp.concatenate([total, jnp.zeros((TOK - run, slots), BF16)], axis=0)
    out[...] = padded.T


def combine(got, places, hidden, out):
    run, rows = out.shape
    turned = got[...].T[:run]
    added = dot(turned, places[...])
    out[...] = (hidden[...].astype(F32) + added)[:, :rows].astype(BF16)


def exchange(x, axes):
    return lax.all_to_all(x, axes, split_axis=0, concat_axis=0, tiled=True)


def on_device(
    queries,
    latents,
    block_mask,
    value_up,
    out_proj,
    residual,
    norm_gain,
    group_ids,
    expert_ids,
    route_weights,
    w_gate,
    w_up,
    w_down,
):
    ctx_count = lax.axis_size(CTX)
    near_count = lax.axis_size(NEAR)
    far_count = lax.axis_size(FAR)
    block_rows, key_width = latents.shape
    heads = queries.shape[1]
    value_width = value_up.shape[2]
    run = residual.shape[1]
    local_experts, _, hidden_units = w_gate.shape
    pad_rows = TOK - block_rows
    slots = ctx_count * SLOT
    part = hidden_units // near_count
    sub = part // far_count

    quarter = key_width // lax.axis_size(PAIR)
    turned_keys = latents.T
    spread = call(spread_keys, shape((ctx_count, quarter, TOK)), [VMEM])(turned_keys)
    pieces = exchange(spread, CTX)
    apart = jnp.arange(ctx_count)[:, None] != jnp.arange(ctx_count)[None, :]
    named = jnp.sum(jnp.where((block_mask == 1) & apart, 1, 0), axis=1)
    few = jnp.max(named) <= FEW

    first_share = run + 16
    places, slot_shares = call(
        functools.partial(route, first_share), [shape((slots, TOK))] * 2, [VMEM] * 3
    )(group_ids.T, expert_ids.transpose(1, 2, 0), route_weights.transpose(1, 2, 0))

    pairs = local_experts // 2
    block = (pairs, run, 6 * part)
    mine, swapped, far_x, far_z, far_xz = call(
        pack,
        [shape(block)] * 2 + [shape((2,) + block)] * 3,
        [VMEM] * 3,
        [pltpu.VMEM((near_count,) + block, BF16)],
    )(w_gate, w_up, w_down.transpose(0, 2, 1))
    out_proj, far_x, far_z, far_xz = lax.optimization_barrier((out_proj, far_x, far_z, far_xz))

    def flipped(x, flip):
        return lax.ppermute(x, NEAR, [(a, a ^ flip) for a in range(near_count)])

    far_z = flipped(far_z, 4)
    far_x = flipped(far_x, 2)

    runs = D // run
    depth = heads * value_width
    wide_q, out_mine, *out_theirs = call(
        prepare,
        [shape((heads * TOK, key_width)), shape((runs // 2, run, depth))]
        + [shape((runs // 4, run, depth))] * 2,
        [VMEM] * 2,
        [pltpu.VMEM((D, depth), BF16)],
    )(queries.transpose(1, 2, 0), out_proj)
    out_theirs = [lax.ppermute(x, "core", [(0, 1), (1, 0)]) for x in out_theirs]
    resid = jnp.pad(residual.T, ((0, 0), (0, pad_rows)))
    gain = norm_gain.astype(F32)[:, None]
    pieces, few, wide_q, out_mine, out_theirs, places, slot_shares, resid, gain = (
        lax.optimization_barrier(
            (pieces, few, wide_q, out_mine, out_theirs, places, slot_shares, resid, gain)
        )
    )

    def attention(held_slots, mask, pieces, wide_q, turned_keys, value_up):
        picked = call(pick_keys, shape((held_slots, quarter, TOK)), [SMEM, VMEM])(mask, pieces)
        across = lax.ppermute(picked, "zb", [(0, 1), (1, 0)])
        beside = lax.ppermute(picked, "core", [(0, 1), (1, 0)])
        corner = lax.ppermute(picked, PAIR, [(a, a ^ 3) for a in range(4)])
        return call(
            attend,
            shape((depth, TOK)),
            [SMEM] + [VMEM] * 7,
            [pltpu.VMEM((key_width, TOK * (held_slots + 1)), BF16)],
        )(mask, wide_q, turned_keys, value_up, picked, beside, across, corner)

    values = lax.cond(
        few,
        functools.partial(attention, FEW),
        functools.partial(attention, ctx_count - 1),
        block_mask,
        pieces,
        wide_q,
        turned_keys,
        value_up,
    )
    values, far_z = lax.optimization_barrier((values, far_z))
    other_values = lax.ppermute(values, "core", [(0, 1), (1, 0)])
    summed = call(project_out, shape((runs // 2, run, TOK)), [VMEM] * 5)(
        values, other_values, out_mine, *out_theirs
    )
    summed, swapped, far_xz = lax.optimization_barrier((summed, swapped, far_xz))
    parts = exchange(summed, ZX)
    far_xz = flipped(far_xz, 6)
    low, high = call(gather_swap, [shape((2,) + block), shape(block)], [VMEM] * 3)(
        swapped, far_x, far_z
    )
    low, high = flipped(low, 1), flipped(high, 1)

    hidden, sent = call(make_rows, [shape((run, TOK)), shape((slots, TOK))], [VMEM] * 5)(
        parts,
        resid,
        gain,
        places,
        slot_shares,
    )
    got = exchange(sent.reshape(ctx_count, SLOT, TOK), CTX).reshape(slots, TOK)
    spread, keep, pick_weight = call(
        functools.partial(spread_rows, run + 8, first_share),
        [
            shape((near_count, run + 8, slots)),
            shape((2 * local_experts, slots), F32),
            shape((2, slots), F32),
        ],
        [VMEM],
    )(got)
    spread, low, high, far_xz = lax.optimization_barrier((spread, low, high, far_xz))
    inputs = exchange(spread, NEAR)
    last = flipped(call(second_half, shape(block), [VMEM])(far_xz), 1)
    weights_in, weights_back = call(
        functools.partial(unpack, part),
        [
            shape((pairs * 4 * part, near_count * run)),
            shape((near_count, run, local_experts * part)),
        ],
        [VMEM] * 7,
    )(mine, far_x, far_z, far_xz, low, high, last)
    partial_sums = call(
        functools.partial(project_up, run, sub),
        shape((far_count, 4 * sub + 8, slots)),
        [VMEM] * 3,
    )(inputs, weights_in, keep)
    acts = call(functools.partial(activate, sub), shape((far_count, 2 * sub, slots)), [VMEM] * 2)(
        exchange(partial_sums, FAR), pick_weight
    )
    outputs = call(
        functools.partial(project_down, sub),
        shape((near_count, run, slots)),
        [VMEM] * 3,
    )(exchange(acts, FAR), keep, weights_back)
    returned = call(finish_rows, shape((slots, TOK)), [VMEM])(exchange(outputs, NEAR))
    returned = exchange(returned.reshape(ctx_count, SLOT, TOK), CTX).reshape(slots, TOK)
    out = call(combine, shape((run, block_rows)), [VMEM] * 3)(returned, places, hidden)
    return out.T


def solution(mesh):
    names = ("y", "xh", "za", "zb", "xl", "core")
    fine = Mesh(mesh.devices.reshape(8, 2, 4, 2, 2, 2), names)
    return jax.shard_map(
        on_device,
        mesh=fine,
        in_specs=(
            P(CTX, EXP, None),
            P(CTX, None),
            P(),
            P(EXP, None, None),
            P(EXP, None),
            P(CTX, EXP),
            P(EXP),
            P(CTX, None),
            P(CTX, None, None),
            P(CTX, None, None),
            P(CTX, EXP, None),
            P(CTX, EXP, None),
            P(CTX, None, EXP),
        ),
        out_specs=P(CTX, EXP),
        check_vma=False,
    )
```

```python
import functools

import jax
import jax.numpy as jnp
from jax import lax
from jax.experimental import pallas as pl
from jax.experimental.pallas import tpu as pltpu
from jax.sharding import Mesh
from jax.sharding import PartitionSpec as P

D = 2560
EPSILON = 1e-06
MASKED_SCORE = -1e30
CTX = ("y", "xh")
EXP = ("za", "zb", "xl", "core")
ZX = ("za", "zb", "xl")
PAIR = ("zb", "core")
NEAR = ("zb", "xl", "core")
FAR = "za"
TOK = 128
SLOT = 32
FEW = 5
F32 = jnp.float32
BF16 = jnp.bfloat16
VMEM = pl.BlockSpec(memory_space=pltpu.VMEM)
SMEM = pl.BlockSpec(memory_space=pltpu.SMEM)


def call(body, out_shape, in_specs, scratch=(), flops=0, limit=40):
    many = isinstance(out_shape, (tuple, list))
    return pl.pallas_call(
        body,
        out_shape=out_shape,
        in_specs=in_specs,
        out_specs=[VMEM] * len(out_shape) if many else VMEM,
        scratch_shapes=scratch,
        compiler_params=pltpu.CompilerParams(vmem_limit_bytes=limit << 20),
    )


def shape(dims, dtype=BF16):
    return jax.ShapeDtypeStruct(dims, dtype)


def dot(a, b):
    return jnp.dot(a, b, preferred_element_type=F32)


def dot_nt(a, b):
    return lax.dot_general(a, b, (((1,), (1,)), ((), ())), preferred_element_type=F32)


def spread_keys(keys, out):
    count, part, _ = out.shape
    rows = keys.shape[1]
    column = lax.axis_index(PAIR)
    own = keys[:part]
    for i in range(1, keys.shape[0] // part):
        own = jnp.where(column == i, keys[i * part : (i + 1) * part], own)
    own = jnp.concatenate([own, jnp.zeros((part, TOK - rows), BF16)], axis=1)
    for i in range(count):
        out[i] = own


def pick_keys(mask, pieces, out):
    block = lax.axis_index(CTX)
    out[...] = jnp.zeros_like(out)

    def step(b, filled):
        wanted = (mask[block, b] == 1) & (b != block)

        @pl.when(wanted)
        def _():
            out[filled] = pieces[b]

        return filled + wanted.astype(jnp.int32)

    lax.fori_loop(0, mask.shape[1], step, 0)


def prepare(queries, weights, wide, mine, low, high, turned):
    heads, width, rows = queries.shape
    for head in range(heads):
        lanes = jnp.concatenate([queries[head], jnp.zeros((width, TOK - rows), BF16)], axis=1)
        wide[head * TOK : (head + 1) * TOK, :] = lanes.T
    for i in range(weights.shape[1] // TOK):
        turned[i * TOK : (i + 1) * TOK, :] = weights[:, i * TOK : (i + 1) * TOK].T
    core = lax.axis_index("core")
    runs, run, _ = mine.shape
    for i in range(runs):
        mine[i] = turned[pl.ds(pl.multiple_of((2 * i + core) * run, run), run), :]
        theirs = turned[pl.ds(pl.multiple_of((2 * i + 1 - core) * run, run), run), :]
        if i < runs // 2:
            low[i] = theirs
        else:
            high[i - runs // 2] = theirs


def route(first, groups, experts, weights, places, shares):
    picks, rows = groups.shape
    slots = places.shape[0]
    count = slots // SLOT
    group = lax.broadcasted_iota(jnp.int32, (count, rows), 0)
    hits = [jnp.where(groups[k : k + 1, :] == group, 1.0, 0.0) for k in range(picks)]
    upto = lax.broadcasted_iota(jnp.int32, (rows, rows), 0)
    upto = jnp.where(upto <= lax.broadcasted_iota(jnp.int32, (rows, rows), 1), 1.0, 0.0)
    rank = dot(sum(hits).astype(BF16), upto.astype(BF16)) - 1.0
    spot = lax.broadcasted_iota(jnp.int32, (count, SLOT, rows), 1).astype(F32)
    here = jnp.where(rank[:, None, :] == spot, 1.0, 0.0)
    lane = lax.broadcasted_iota(jnp.int32, (TOK, rows), 0)
    every = jnp.zeros((slots, rows), F32)
    share = jnp.zeros((slots, TOK), F32)
    for k in range(picks):
        placed = (hits[k][:, None, :] * here).reshape(slots, rows)
        every = every + placed
        table = jnp.zeros((TOK, rows), F32)
        for m in range(experts.shape[1]):
            weight = weights[k, m : m + 1, :].astype(F32)
            table = table + jnp.where(lane == first + experts[k, m : m + 1, :], weight, 0.0)
        share = share + dot_nt(placed.astype(BF16), table.astype(BF16))
    every = jnp.concatenate([every, jnp.zeros((slots, TOK - rows), F32)], axis=1)
    places[...] = every.astype(BF16)
    shares[...] = share.astype(BF16)


def attend(mask, queries, own, up, *refs):
    pieces, (out, held) = refs[:4], refs[4:]
    block, column = lax.axis_index(CTX), lax.axis_index(PAIR)
    width, rows = own.shape
    slots, part, _ = pieces[0].shape
    keys = TOK * (slots + 1)

    def count(b, filled):
        return filled + ((mask[block, b] == 1) & (b != block)).astype(jnp.int32)

    filled = lax.fori_loop(0, mask.shape[1], count, 0)
    held[:, :TOK] = jnp.concatenate([own[...], jnp.zeros((width, TOK - rows), BF16)], axis=1)
    for slot in range(slots):
        for flip, piece in enumerate(pieces):
            start = pl.multiple_of((column ^ flip) * part, part)
            held[pl.ds(start, part), (slot + 1) * TOK : (slot + 2) * TOK] = piece[slot]
    query = lax.broadcasted_iota(jnp.int32, (2 * TOK, keys), 0) % TOK
    lane = lax.broadcasted_iota(jnp.int32, (2 * TOK, keys), 1)
    key = lane % TOK
    limit = jnp.where(lane < TOK, query + 1, jnp.where(lane < (filled + 1) * TOK, rows, 0))
    inside = key < jnp.minimum(limit, rows)
    masked = jnp.where(inside, dot(queries[...], held[...]) * width**-0.5, MASKED_SCORE)
    terms = jnp.where(inside, jnp.exp(masked - jnp.max(masked, axis=1, keepdims=True)), 0.0)
    inverse = 1.0 / jnp.sum(terms, axis=1, keepdims=True)
    latent = dot_nt(terms.astype(BF16), held[: up.shape[1], :]) * inverse
    high = latent.astype(BF16)
    low = (latent - high.astype(F32)).astype(BF16)
    values = []
    for head in range(up.shape[0]):
        span = slice(head * TOK, (head + 1) * TOK)
        values.append((dot(high[span], up[head]) + dot(low[span], up[head])).T.astype(BF16))
    out[...] = jnp.concatenate(values, axis=0)


def project_out(mine, theirs, weights_mine, low, high, out):
    half, run, depth = low.shape
    for i, weights_theirs in enumerate((low, high)):
        own = weights_mine[i * half : (i + 1) * half].reshape(half * run, depth)
        total = dot(own, mine[...])
        total = total + dot(weights_theirs[...].reshape(half * run, depth), theirs[...])
        out[i * half : (i + 1) * half] = total.reshape(half, run, TOK).astype(BF16)


def split_pair(value):
    high = value.astype(BF16).astype(F32)
    return high, (value - high).astype(BF16).astype(F32)


def tail_rows(value, count):
    high, low = split_pair(value)
    row = lax.broadcasted_iota(jnp.int32, (count, value.shape[1]), 0)
    return jnp.where(row == 0, high, jnp.where(row == 1, low, 0.0))


def make_rows(parts, residual, gain, places, shares, hidden, sent):
    mixed = jnp.sum(parts[...].astype(F32), axis=0)
    held = (residual[...].astype(F32) + mixed).astype(BF16)
    hidden[...] = held
    wide = held.astype(F32)
    square = jnp.sum(wide * wide, axis=0, keepdims=True)
    run = wide.shape[0]
    rows = jnp.concatenate([wide * gain[...], tail_rows(square, TOK - run)], axis=0).astype(BF16)
    sent[...] = (dot_nt(places[...], rows) + shares[...].astype(F32)).astype(BF16)


def spread_rows(keep_rows, first, got, out, keep, weight):
    turned = got[...].T
    kept = turned[:keep_rows]
    for i in range(out.shape[0]):
        out[i] = kept
    count = keep.shape[0] // 2
    weights = turned[first : first + 16].astype(F32)
    seen = jnp.zeros((1, weights.shape[1]), F32)
    picked = [jnp.zeros((1, weights.shape[1]), F32) for _ in range(2)]
    for expert in range(count):
        row = weights[expert : expert + 1]
        chosen = jnp.where(row > 0.0, 1.0, 0.0)
        for pick in range(2):
            flag = jnp.where(seen == pick, chosen, 0.0)
            keep[2 * expert + pick : 2 * expert + pick + 1, :] = flag
            picked[pick] = picked[pick] + flag * row
        seen = seen + chosen
    weight[...] = jnp.concatenate(picked, axis=0)


def pack(gate, up, down, mine, swapped, far_x, far_z, far_xz, held):
    count = held.shape[0]
    part = gate.shape[2] // count
    for pair in range(held.shape[1]):
        for near in range(count):
            span = slice(near * part, (near + 1) * part)
            pieces = []
            for expert in (2 * pair, 2 * pair + 1):
                pieces += [gate[expert, :, span], up[expert, :, span]]
            pieces += [down[2 * pair, :, span], down[2 * pair + 1, :, span]]
            held[near, pair] = jnp.concatenate(pieces, axis=1)
    near = lax.axis_index(NEAR)
    mine[...] = held[near]
    swapped[...] = held[near ^ 1]
    for out, flip in ((far_x, 2), (far_z, 4), (far_xz, 6)):
        out[0] = held[near ^ flip]
        out[1] = held[near ^ flip ^ 1]


def gather_swap(swapped, far_x, far_z, low, high):
    low[0] = swapped[...]
    low[1] = far_x[1]
    high[...] = far_z[1]


def second_half(got, out):
    out[...] = got[1]


def unpack(part, mine, far_x, far_z, far_xz, low, high, last, into, back):
    pairs = mine.shape[0]
    for pair in range(pairs):
        rows = []
        for i, own in enumerate((mine, far_x, far_z, far_xz)):
            rows.append(own[pair] if i == 0 else own[0, pair])
            rows.append(low[i, pair] if i < 2 else (high, last)[i - 2][pair])
        wide = jnp.concatenate([row[:, : 4 * part] for row in rows], axis=0)
        into[pair * 4 * part : (pair + 1) * 4 * part, :] = wide.T
        for flip, row in enumerate(rows):
            back[flip, :, pair * 2 * part : (pair + 1) * 2 * part] = row[:, 4 * part :]


def project_up(run, sub, inputs, weights, keep, out, held, arrived):
    count, _, slots = inputs.shape
    pair_rows = weights.shape[0] // arrived.shape[0]
    copies = []
    for i in range(arrived.shape[0]):
        rows = pl.ds(i * pair_rows, pair_rows)
        copies.append(pltpu.make_async_copy(weights.at[rows], held.at[rows], arrived.at[i]))
        copies[-1].start()
    features = jnp.concatenate(
        [inputs[lax.axis_index(NEAR) ^ flip, :run, :] for flip in range(count)], axis=0
    )
    ends = jnp.sum(inputs[...].astype(F32)[:, run:], axis=0)
    square = ends[0:1] + ends[1:2]
    unit = 2 * sub * out.shape[0]
    sums = [jnp.zeros((unit, slots), F32) for _ in range(2)]
    for expert in range(weights.shape[0] // unit):
        if expert % 2 == 0:
            copies[expert // 2].wait()
        part = dot(held[expert * unit : (expert + 1) * unit, :], features)
        for pick in range(2):
            sums[pick] = sums[pick] + keep[2 * expert + pick : 2 * expert + pick + 1, :] * part
    tail = tail_rows(square, 8)
    for dest in range(out.shape[0]):
        pieces = []
        for pick in range(2):
            for kind in range(2):
                start = kind * unit // 2 + dest * sub
                pieces.append(sums[pick][start : start + sub])
        out[dest] = jnp.concatenate(pieces + [tail], axis=0).astype(BF16)


def activate(sub, got, weight, out):
    total = jnp.sum(got[...].astype(F32), axis=0)
    square = total[4 * sub : 4 * sub + 1] + total[4 * sub + 1 : 4 * sub + 2]
    scale = lax.rsqrt(square / D + EPSILON)
    pieces = []
    for pick in range(2):
        gate = total[2 * pick * sub : (2 * pick + 1) * sub] * scale
        up = total[(2 * pick + 1) * sub : (2 * pick + 2) * sub] * scale
        act = gate / (1.0 + jnp.exp(-gate)) * up
        pieces.append(act * weight[pick : pick + 1, :])
    rounded = jnp.concatenate(pieces, axis=0).astype(BF16)
    for i in range(out.shape[0]):
        out[i] = rounded


def project_down(sub, acts, keep, weights, out):
    count, _, slots = acts.shape
    wide = acts[...].astype(F32)
    first = wide[:, :sub].reshape(count * sub, slots)
    second = wide[:, sub:].reshape(count * sub, slots)
    picked = []
    for expert in range(keep.shape[0] // 2):
        picked.append(
            (
                keep[2 * expert : 2 * expert + 1, :] * first
                + keep[2 * expert + 1 : 2 * expert + 2, :] * second
            ).astype(BF16)
        )
    stacked = jnp.concatenate(picked, axis=0)
    for flip in range(weights.shape[0]):
        out[lax.axis_index(NEAR) ^ flip] = dot(weights[flip], stacked).astype(BF16)


def finish_rows(got, out):
    total = jnp.sum(got[...].astype(F32), axis=0).astype(BF16)
    run, slots = total.shape
    padded = jnp.concatenate([total, jnp.zeros((TOK - run, slots), BF16)], axis=0)
    out[...] = padded.T


def combine(got, places, hidden, out):
    run, rows = out.shape
    turned = got[...].T[:run]
    added = dot(turned, places[...])
    out[...] = (hidden[...].astype(F32) + added)[:, :rows].astype(BF16)


def exchange(x, axes):
    return lax.all_to_all(x, axes, split_axis=0, concat_axis=0, tiled=True)


def on_device(
    queries,
    latents,
    block_mask,
    value_up,
    out_proj,
    residual,
    norm_gain,
    group_ids,
    expert_ids,
    route_weights,
    w_gate,
    w_up,
    w_down,
):
    ctx_count = lax.axis_size(CTX)
    near_count = lax.axis_size(NEAR)
    far_count = lax.axis_size(FAR)
    block_rows, key_width = latents.shape
    heads = queries.shape[1]
    value_width = value_up.shape[2]
    run = residual.shape[1]
    local_experts, _, hidden_units = w_gate.shape
    pad_rows = TOK - block_rows
    slots = ctx_count * SLOT
    part = hidden_units // near_count
    sub = part // far_count

    quarter = key_width // lax.axis_size(PAIR)
    turned_keys = latents.T
    spread = call(spread_keys, shape((ctx_count, quarter, TOK)), [VMEM])(turned_keys)
    pieces = exchange(spread, CTX)
    apart = jnp.arange(ctx_count)[:, None] != jnp.arange(ctx_count)[None, :]
    named = jnp.sum(jnp.where((block_mask == 1) & apart, 1, 0), axis=1)
    few = jnp.max(named) <= FEW

    first_share = run + 16
    places, slot_shares = call(
        functools.partial(route, first_share), [shape((slots, TOK))] * 2, [VMEM] * 3
    )(group_ids.T, expert_ids.transpose(1, 2, 0), route_weights.transpose(1, 2, 0))

    pairs = local_experts // 2
    block = (pairs, run, 6 * part)
    mine, swapped, far_x, far_z, far_xz = call(
        pack,
        [shape(block)] * 2 + [shape((2,) + block)] * 3,
        [VMEM] * 3,
        [pltpu.VMEM((near_count,) + block, BF16)],
    )(w_gate, w_up, w_down.transpose(0, 2, 1))
    out_proj, far_x, far_z, far_xz = lax.optimization_barrier((out_proj, far_x, far_z, far_xz))

    def flipped(x, flip):
        return lax.ppermute(x, NEAR, [(a, a ^ flip) for a in range(near_count)])

    far_z = flipped(far_z, 4)
    far_x = flipped(far_x, 2)

    runs = D // run
    depth = heads * value_width
    wide_q, out_mine, *out_theirs = call(
        prepare,
        [shape((heads * TOK, key_width)), shape((runs // 2, run, depth))]
        + [shape((runs // 4, run, depth))] * 2,
        [VMEM] * 2,
        [pltpu.VMEM((D, depth), BF16)],
    )(queries.transpose(1, 2, 0), out_proj)
    out_theirs = [lax.ppermute(x, "core", [(0, 1), (1, 0)]) for x in out_theirs]
    resid = jnp.pad(residual.T, ((0, 0), (0, pad_rows)))
    gain = norm_gain.astype(F32)[:, None]
    pieces, few, wide_q, out_mine, out_theirs, places, slot_shares, resid, gain = (
        lax.optimization_barrier(
            (pieces, few, wide_q, out_mine, out_theirs, places, slot_shares, resid, gain)
        )
    )

    def attention(held_slots, mask, pieces, wide_q, turned_keys, value_up):
        picked = call(pick_keys, shape((held_slots, quarter, TOK)), [SMEM, VMEM])(mask, pieces)
        across = lax.ppermute(picked, "zb", [(0, 1), (1, 0)])
        beside = lax.ppermute(picked, "core", [(0, 1), (1, 0)])
        corner = lax.ppermute(across, "core", [(0, 1), (1, 0)])
        return call(
            attend,
            shape((depth, TOK)),
            [SMEM] + [VMEM] * 7,
            [pltpu.VMEM((key_width, TOK * (held_slots + 1)), BF16)],
        )(mask, wide_q, turned_keys, value_up, picked, beside, across, corner)

    values = lax.cond(
        few,
        functools.partial(attention, FEW),
        functools.partial(attention, ctx_count - 1),
        block_mask,
        pieces,
        wide_q,
        turned_keys,
        value_up,
    )
    values, far_z = lax.optimization_barrier((values, far_z))
    other_values = lax.ppermute(values, "core", [(0, 1), (1, 0)])
    summed = call(project_out, shape((runs // 2, run, TOK)), [VMEM] * 5)(
        values, other_values, out_mine, *out_theirs
    )
    summed, swapped, far_xz = lax.optimization_barrier((summed, swapped, far_xz))
    parts = exchange(summed, ZX)
    far_xz = flipped(far_xz, 6)
    low, high = call(gather_swap, [shape((2,) + block), shape(block)], [VMEM] * 3)(
        swapped, far_x, far_z
    )
    low, high = flipped(low, 1), flipped(high, 1)

    hidden, sent = call(make_rows, [shape((run, TOK)), shape((slots, TOK))], [VMEM] * 5)(
        parts,
        resid,
        gain,
        places,
        slot_shares,
    )
    got = exchange(sent.reshape(ctx_count, SLOT, TOK), CTX).reshape(slots, TOK)
    spread, keep, pick_weight = call(
        functools.partial(spread_rows, run + 8, first_share),
        [
            shape((near_count, run + 8, slots)),
            shape((2 * local_experts, slots), F32),
            shape((2, slots), F32),
        ],
        [VMEM],
    )(got)
    spread, low, high, far_xz = lax.optimization_barrier((spread, low, high, far_xz))
    inputs = exchange(spread, NEAR)
    last = flipped(call(second_half, shape(block), [VMEM])(far_xz), 1)
    weights_in, weights_back = call(
        functools.partial(unpack, part),
        [
            shape((pairs * 4 * part, near_count * run)),
            shape((near_count, run, local_experts * part)),
        ],
        [VMEM] * 7,
    )(mine, far_x, far_z, far_xz, low, high, last)
    partial_sums = call(
        functools.partial(project_up, run, sub),
        shape((far_count, 4 * sub + 8, slots)),
        [VMEM, pl.BlockSpec(memory_space=pl.ANY), VMEM],
        [
            pltpu.VMEM((pairs * 4 * part, near_count * run), BF16),
            pltpu.SemaphoreType.DMA((pairs,)),
        ],
        limit=59,
    )(inputs, weights_in, keep)
    acts = call(functools.partial(activate, sub), shape((far_count, 2 * sub, slots)), [VMEM] * 2)(
        exchange(partial_sums, FAR), pick_weight
    )
    outputs = call(
        functools.partial(project_down, sub),
        shape((near_count, run, slots)),
        [VMEM] * 3,
    )(exchange(acts, FAR), keep, weights_back)
    returned = call(finish_rows, shape((slots, TOK)), [VMEM])(exchange(outputs, NEAR))
    returned = exchange(returned.reshape(ctx_count, SLOT, TOK), CTX).reshape(slots, TOK)
    out = call(combine, shape((run, block_rows)), [VMEM] * 3)(returned, places, hidden)
    return out.T


def solution(mesh):
    names = ("y", "xh", "za", "zb", "xl", "core")
    fine = Mesh(mesh.devices.reshape(8, 2, 4, 2, 2, 2), names)
    return jax.shard_map(
        on_device,
        mesh=fine,
        in_specs=(
            P(CTX, EXP, None),
            P(CTX, None),
            P(),
            P(EXP, None, None),
            P(EXP, None),
            P(CTX, EXP),
            P(EXP),
            P(CTX, None),
            P(CTX, None, None),
            P(CTX, None, None),
            P(CTX, EXP, None),
            P(CTX, EXP, None),
            P(CTX, None, EXP),
        ),
        out_specs=P(CTX, EXP),
        check_vma=False,
    )
```
